512 devices in a mesh: dp: 128 (over y, z, x_lo), tensor: 4 (over x_hi, core).
Axes of the slice: x: 4 (x_hi: 2, x_lo: 2; x = x_hi * 2 + x_lo), y: 4, z: 16, core: 2. Of those that a mesh axis runs over, the one named last changes fastest.
Arguments:
- img_feat: bfloat16 [16384, 1280], P('dp'), may hold values from -8 to 8
- txt_feat: bfloat16 [16384, 1024], P('dp'), may hold values from -8 to 8
- img_proj: bfloat16 [1280, 512], P(None, 'tensor'), may hold values from -0.5 to 0.5
- txt_proj: bfloat16 [1024, 512], P(None, 'tensor'), may hold values from -0.5 to 0.5
- logit_scale: float32 [1], replicated, may hold values from 10 to 40
Outputs:
- grad_img_proj: float32 [1280, 512], P('dp', 'tensor')
- grad_txt_proj: float32 [1024, 512], P('dp', 'tensor')
- grad_img_feat: float32 [16384, 1280], P('dp', 'tensor')
- grad_txt_feat: float32 [16384, 1024], P('dp', 'tensor')
The draws below stay inside these ranges and needn't reach their ends.
All inputs are finite; a program needn't handle non-finite values.
Results may differ from the reference program's by a relative error of at most 0.013.
Values may be sent and summed in bfloat16 or wider, within the bound.
A program may use at most 64 MiB of HBM per device.

```python
import math
import jax
import jax.numpy as jnp
from jax import lax

DI = 1280
DT = 1024
EMB = 512
ROWS = 128
BATCH = 16384
N_DP = 128


def common_rows(key):
    count = max(BATCH // 8, 2)
    labels = jax.random.randint(jax.random.fold_in(key, 101), (BATCH,), 0, count)
    protos = jax.random.normal(jax.random.fold_in(key, 102), (count, DT), jnp.float32)
    return jnp.take(protos, labels, axis=0)


def common_weight(key):
    return jax.random.normal(jax.random.fold_in(key, 103), (DT, EMB), jnp.float32) * DT ** (-0.5)


def draw_img_feat(key, part):
    base = common_rows(key)
    key = jax.random.fold_in(key, 1)
    noise = 0.7 * jax.random.normal(key, (BATCH, DI), jnp.float32)
    feat = jnp.pad(base, ((0, 0), (0, DI - DT))) + noise
    return jnp.clip(feat, -8.0, 8.0).astype(jnp.bfloat16)


def draw_txt_feat(key, part):
    base = common_rows(key)
    key = jax.random.fold_in(key, 2)
    noise = 0.7 * jax.random.normal(key, (BATCH, DT), jnp.float32)
    feat = base + noise
    return jnp.clip(feat, -8.0, 8.0).astype(jnp.bfloat16)


def draw_img_proj(key, part):
    base = common_weight(key)
    key = jax.random.fold_in(key, 3)
    noise = 0.5 * jax.random.normal(key, (DI, EMB), jnp.float32) * DI ** (-0.5)
    weight = jnp.pad(base, ((0, DI - DT), (0, 0))) + noise
    return jnp.clip(weight, -0.5, 0.5).astype(jnp.bfloat16)


def draw_txt_proj(key, part):
    base = common_weight(key)
    key = jax.random.fold_in(key, 4)
    noise = 0.3 * jax.random.normal(key, (DT, EMB), jnp.float32) * DT ** (-0.5)
    return jnp.clip(base + noise, -0.5, 0.5).astype(jnp.bfloat16)


def setup_inputs(seed: int = 0) -> dict:
    key_of = jax.random.split(jax.random.key(seed), 6)
    img_feat = draw_img_feat(jax.random.fold_in(key_of[5], 71), 0)
    txt_feat = draw_txt_feat(jax.random.fold_in(key_of[5], 71), 0)
    img_proj = draw_img_proj(jax.random.fold_in(key_of[5], 71), 0)
    txt_proj = draw_txt_proj(jax.random.fold_in(key_of[5], 71), 0)
    logit_scale = jnp.clip(jnp.exp(jax.random.uniform(key_of[4], (1,), jnp.float32, math.log(10.0), math.log(40.0))), 10.0, 40.0)
    return dict(img_feat=img_feat, txt_feat=txt_feat, img_proj=img_proj, txt_proj=txt_proj, logit_scale=logit_scale)


eps = 1e-06
loss_factor = 256.0

def normalize(feat, proj):
    raw = jnp.dot(feat, proj, preferred_element_type=jnp.float32)
    inv = lax.rsqrt(lax.optimization_barrier(jnp.sum(raw * raw, axis=1, keepdims=True)) + eps)
    return ((raw * inv).astype(jnp.bfloat16), inv)

def grad_block(own, keys, start, scale, coef):
    cosine = lax.dot_general(own, keys, (((1,), (1,)), ((), ())), preferred_element_type=jnp.float32)
    expo = jnp.exp(scale * (cosine - 1.0))
    prob = expo / lax.optimization_barrier(jnp.sum(expo, axis=1, keepdims=True))
    columns = jnp.arange(keys.shape[0], dtype=jnp.int32)
    targets = start + jnp.arange(own.shape[0], dtype=jnp.int32)
    onehot = (columns[None, :] == targets[:, None]).astype(jnp.float32)
    diff = (prob - onehot).astype(jnp.bfloat16)
    grad_emb = coef * jnp.dot(diff, keys, preferred_element_type=jnp.float32)
    own_f = own.astype(jnp.float32)
    align = lax.optimization_barrier(jnp.sum(own_f * grad_emb, axis=1, keepdims=True))
    return grad_emb - own_f * align

def reference(img_feat, txt_feat, img_proj, txt_proj, logit_scale):
    scale = logit_scale[0]
    batch = img_feat.shape[0]
    coef = scale * loss_factor / (2.0 * batch)
    emb_img, inv_img = normalize(img_feat, img_proj)
    emb_txt, inv_txt = normalize(txt_feat, txt_proj)
    blocks_img = emb_img.reshape(N_DP, ROWS, EMB)
    blocks_txt = emb_txt.reshape(N_DP, ROWS, EMB)
    starts = jnp.arange(N_DP, dtype=jnp.int32) * ROWS

    def one_block(items):
        block_img, block_txt, start = items
        return (grad_block(block_img, emb_txt, start, scale, coef), grad_block(block_txt, emb_img, start, scale, coef))
    pre_img, pre_txt = lax.map(one_block, (blocks_img, blocks_txt, starts))
    grad_raw_img = (pre_img.reshape(batch, EMB) * inv_img).astype(jnp.bfloat16)
    grad_raw_txt = (pre_txt.reshape(batch, EMB) * inv_txt).astype(jnp.bfloat16)
    grad_img_proj = lax.dot_general(img_feat, grad_raw_img, (((0,), (0,)), ((), ())), preferred_element_type=jnp.float32)
    grad_txt_proj = lax.dot_general(txt_feat, grad_raw_txt, (((0,), (0,)), ((), ())), preferred_element_type=jnp.float32)
    grad_img_feat = lax.dot_general(grad_raw_img, img_proj, (((1,), (1,)), ((), ())), preferred_element_type=jnp.float32)
    grad_txt_feat = lax.dot_general(grad_raw_txt, txt_proj, (((1,), (1,)), ((), ())), preferred_element_type=jnp.float32)
    return (grad_img_proj, grad_txt_proj, grad_img_feat, grad_txt_feat)
```

```python
import functools

import jax
import jax.numpy as jnp
from jax import lax
from jax.experimental import pallas as pl
from jax.experimental.pallas import tpu as pltpu
from jax.sharding import PartitionSpec as P

Z = 16
XL = 2
T = 4
ROWS = 128
Q = 128
SUMS = 16
PIECE = ROWS + SUMS
eps = 1e-06
loss_factor = 256.0
f32 = jnp.float32
bf16 = jnp.bfloat16


def nt(left, right):
    return lax.dot_general(left, right, (((1,), (1,)), ((), ())), preferred_element_type=f32)


def tn(left, right):
    return lax.dot_general(left, right, (((0,), (0,)), ((), ())), preferred_element_type=f32)


def row_sums(values):
    return jnp.sum(jnp.transpose(values), axis=0, keepdims=True)


def as_columns(row):
    return jnp.transpose(jnp.broadcast_to(row, (ROWS, ROWS)))


def pack_sums(off, diag):
    index = lax.broadcasted_iota(jnp.int32, (SUMS, ROWS), 0)
    off_hi = off.astype(bf16).astype(f32)
    diag_hi = diag.astype(bf16).astype(f32)
    parts = jnp.where(
        index == 0,
        off_hi,
        jnp.where(
            index == 1,
            off - off_hi,
            jnp.where(index == 2, diag_hi, jnp.where(index == 3, diag - diag_hi, 0.0)),
        ),
    )
    return parts.astype(bf16)


def unpack_sums(parts):
    return parts[0:1] + parts[1:2], parts[2:3] + parts[3:4]


def window_of(per):
    return max(-(-(((k * per) % 8) + per) // 8) * 8 for k in range(8))


def kernel(
    ny, di, dt,
    scale_ref, imgf, txtf, imgp, txtp,
    gip, gtp, gif, gtf,
    sqb, invc, own, img_all, zbuf, txt_all,
    psi, pst, gt_acc, col_acc,
    rs_send, rs_recv, gx_send, gz, f_send, f_recv, b_send, b_recv,
    alb, gr_own, gr_all, y_send, y_recv, x_send, x_recv, zsum, z_send, z_recv,
    sq_ss, sq_rs, pp_ss, pp_rs, ig_ss, ig_rs, zf_ss, zf_rs, zb_ss, zb_rs,
    tx_ss, tx_rs, ri_ss, ri_rs, gx_ss, gx_rs, f_ss, f_rs, b_ss, b_rs,
    al_ss, al_rs, gr_ss, gr_rs, y_ss, y_rs, x_ss, x_rs, z_ss, z_rs,
):
    n_blocks = ny * XL
    n_plane = n_blocks * T
    half = Z // 2
    batch = ny * Z * XL * ROWS
    dp = lax.axis_index("dp")
    t = lax.axis_index("tensor")
    xl = dp % XL
    z = (dp // XL) % Z
    y = dp // (XL * Z)
    b = y * XL + xl
    p = b * T + t

    def plane_dev(q):
        block = q // T
        return (((block // XL) * Z + z) * XL + block % XL, q % T)

    def z_dev(other):
        return ((y * Z + other) * XL + xl, t)

    def y_dev(other):
        return ((other * Z + z) * XL + xl, t)

    def t_dev(other):
        return (dp, other)

    def remote(src, dst, send, recv, dev):
        return pltpu.make_async_remote_copy(
            src_ref=src, dst_ref=dst, send_sem=send, recv_sem=recv,
            device_id=dev, device_id_type=pl.DeviceIdType.MESH,
        )

    barrier = pltpu.get_barrier_semaphore()

    @pl.loop(1, n_plane)
    def _(i):
        pl.semaphore_signal(
            barrier, inc=1, device_id=plane_dev((p + i) % n_plane),
            device_id_type=pl.DeviceIdType.MESH,
        )

    @pl.loop(1, Z)
    def _(i):
        pl.semaphore_signal(
            barrier, inc=1, device_id=z_dev((z + i) % Z), device_id_type=pl.DeviceIdType.MESH
        )

    scale = scale_ref[0]
    coef = scale * (loss_factor / (2.0 * batch))

    raw_img = jnp.dot(imgf[...], imgp[...], preferred_element_type=f32)
    raw_txt = jnp.dot(txtf[...], txtp[...], preferred_element_type=f32)
    index8 = lax.broadcasted_iota(jnp.int32, (8, ROWS), 0)
    sqb[t] = jnp.where(
        index8 == 0, row_sums(raw_img * raw_img), row_sums(raw_txt * raw_txt)
    )
    pl.semaphore_wait(barrier, n_plane - 1 + Z - 1)

    def sq_copy(i):
        return remote(sqb.at[t], sqb.at[t], sq_ss.at[i - 1], sq_rs.at[t], t_dev((t + i) % T))

    def sq_wait(i):
        src = (t + i) % T
        return remote(sqb.at[src], sqb.at[src], sq_ss.at[i - 1], sq_rs.at[src], t_dev(src))

    for i in range(1, T):
        sq_copy(i).start()
    for i in range(1, T):
        sq_wait(i).wait_recv()
    square = (sqb[0] + sqb[1]) + (sqb[2] + sqb[3])
    inv = lax.rsqrt(square + eps)
    inv_img = as_columns(inv[0:1])
    inv_txt = as_columns(inv[1:2])
    invc[0] = inv_img
    invc[1] = inv_txt
    emb_img = (raw_img * inv_img).astype(bf16)
    emb_txt = (raw_txt * inv_txt).astype(bf16)
    own[0] = emb_img
    own[1] = emb_txt
    zbuf[z] = emb_txt

    def img_slot(q):
        return img_all.at[
            pl.ds(pl.multiple_of((q // T) * ROWS, ROWS), ROWS),
            pl.ds(pl.multiple_of((q % T) * Q, Q), Q),
        ]

    def txt_slot(k, quarter):
        return txt_all.at[
            pl.ds(pl.multiple_of(k * ROWS, ROWS), ROWS),
            pl.ds(pl.multiple_of(quarter * Q, Q), Q),
        ]

    def zf_copy(s):
        piece = (z - s + Z) % Z
        return remote(zbuf.at[piece], zbuf.at[piece], zf_ss.at[s], zf_rs.at[s], z_dev((z + 1) % Z))

    def zf_land(s):
        piece = (z - 1 - s + 2 * Z) % Z
        return remote(zbuf.at[piece], zbuf.at[piece], zf_ss.at[s], zf_rs.at[s], z_dev((z + 1) % Z))

    def zb_copy(s):
        piece = (z + s) % Z
        return remote(zbuf.at[piece], zbuf.at[piece], zb_ss.at[s], zb_rs.at[s], z_dev((z - 1 + Z) % Z))

    def zb_land(s):
        piece = (z + 1 + s) % Z
        return remote(zbuf.at[piece], zbuf.at[piece], zb_ss.at[s], zb_rs.at[s], z_dev((z - 1 + Z) % Z))

    def tx_remote(piece):
        return remote(
            zbuf.at[piece], txt_slot(piece // T, t), tx_ss.at[piece],
            tx_rs.at[(piece // T) * T + t], t_dev(piece % T),
        )

    def tx_local(piece):
        return pltpu.make_async_copy(zbuf.at[piece], txt_slot(piece // T, t), tx_ss.at[piece])

    def pass_on(piece):
        @pl.when(piece % T != t)
        def _():
            tx_remote(piece).start()

        @pl.when(piece % T == t)
        def _():
            tx_local(piece).start()

    zf_copy(0).start()
    zb_copy(0).start()
    pass_on(z)

    own_img_copy = pltpu.make_async_copy(own.at[0], img_slot(p), ig_ss.at[0])
    own_img_copy.start()

    def ig_copy(i):
        return remote(own.at[0], img_slot(p), ig_ss.at[i], ig_rs.at[p], plane_dev((p + i) % n_plane))

    @pl.loop(1, n_plane)
    def _(i):
        ig_copy(i).start()

    di4, dt4 = di // T, dt // T

    def pp_copies(i):
        dst = (t + i) % T
        return (
            remote(
                imgp.at[pl.ds(pl.multiple_of(dst * di4, di4), di4), :],
                psi.at[:, pl.ds(pl.multiple_of(t * Q, Q), Q)],
                pp_ss.at[2 * i], pp_rs.at[2 * t], t_dev(dst),
            ),
            remote(
                txtp.at[pl.ds(pl.multiple_of(dst * dt4, dt4), dt4), :],
                pst.at[:, pl.ds(pl.multiple_of(t * Q, Q), Q)],
                pp_ss.at[2 * i + 1], pp_rs.at[2 * t + 1], t_dev(dst),
            ),
        )

    def pp_lands(i):
        src = (t + i) % T
        return (
            remote(
                imgp.at[pl.ds(0, di4), :], psi.at[:, pl.ds(pl.multiple_of(src * Q, Q), Q)],
                pp_ss.at[2 * i], pp_rs.at[2 * src], t_dev(src),
            ),
            remote(
                txtp.at[pl.ds(0, dt4), :], pst.at[:, pl.ds(pl.multiple_of(src * Q, Q), Q)],
                pp_ss.at[2 * i + 1], pp_rs.at[2 * src + 1], t_dev(src),
            ),
        )

    own_psi = pltpu.make_async_copy(
        imgp.at[pl.ds(pl.multiple_of(t * di4, di4), di4), :],
        psi.at[:, pl.ds(pl.multiple_of(t * Q, Q), Q)], pp_ss.at[0],
    )
    own_pst = pltpu.make_async_copy(
        txtp.at[pl.ds(pl.multiple_of(t * dt4, dt4), dt4), :],
        pst.at[:, pl.ds(pl.multiple_of(t * Q, Q), Q)], pp_ss.at[1],
    )
    own_psi.start()
    own_pst.start()

    @pl.loop(1, half)
    def _(s):
        zf_land(s - 1).wait_recv()
        zf_copy(s).start()
        pass_on((z - s + Z) % Z)
        zb_land(s - 1).wait_recv()

        @pl.when(s < half - 1)
        def _():
            zb_copy(s).start()

        pass_on((z + s) % Z)

    zf_land(half - 1).wait_recv()
    pass_on((z - half + Z) % Z)

    @pl.loop(1, T)
    def _(i):
        for copy in pp_copies(i):
            copy.start()

    own_img_copy.wait()

    @pl.loop(1, n_plane)
    def _(i):
        src = (p + i) % n_plane
        remote(own.at[0], img_slot(src), ig_ss.at[i], ig_rs.at[src], plane_dev(src)).wait_recv()

    @pl.loop(0, Z)
    def _(piece):
        @pl.when(piece % T == t)
        def _():
            tx_local(piece).wait()

    @pl.loop(0, Z // T)
    def _(k):
        for i in range(1, T):
            src = (t + i) % T
            remote(
                zbuf.at[0], txt_slot(k, src), tx_ss.at[0], tx_rs.at[k * T + src], t_dev(src)
            ).wait_recv()

    keys = Z // T * ROWS
    gt_acc[...] = jnp.zeros_like(gt_acc)
    col_acc[...] = jnp.zeros_like(col_acc)

    def rs_copy(block, quarter):
        q = block * T + quarter
        return remote(rs_send.at[q], rs_recv.at[p], ri_ss.at[q], ri_rs.at[p], plane_dev(q))

    def masked_diag(cond):
        i = lax.broadcasted_iota(jnp.int32, (ROWS, keys), 0)
        j = lax.broadcasted_iota(jnp.int32, (ROWS, keys), 1)
        shift = jnp.where(cond, (z // T) * ROWS, -2 * ROWS)
        return (j - i) == shift

    @pl.loop(0, n_blocks)
    def _(n):
        block = (b + 1 + n) % n_blocks
        rows = img_all[pl.ds(pl.multiple_of(block * ROWS, ROWS), ROWS), :]
        cos = nt(rows, txt_all[...])
        expo = jnp.exp(scale * (cos - 1.0))
        mask = masked_diag((block == b) & (t == z % T))
        off = jnp.where(mask, 0.0, expo)
        on = jnp.where(mask, expo, 0.0)
        diag = jnp.sum(on, axis=0, keepdims=True)
        diag = sum(diag[:, k * ROWS:(k + 1) * ROWS] for k in range(keys // ROWS))
        folded = sum(off[:, k * ROWS:(k + 1) * ROWS] for k in range(keys // ROWS))
        sums = pack_sums(row_sums(folded), diag)
        col_acc[0:1, :] += jnp.sum(off, axis=0, keepdims=True)
        col_acc[1:2, :] += jnp.sum(on, axis=0, keepdims=True)
        weights = off.astype(bf16)
        part = jnp.dot(weights, txt_all[...], preferred_element_type=f32)
        for quarter in range(T):
            q = block * T + quarter
            rs_send[q, 0:ROWS, :] = part[:, quarter * Q:(quarter + 1) * Q].astype(bf16)
            rs_send[q, ROWS:PIECE, :] = sums

        for quarter in range(T):
            @pl.when(block * T + quarter != p)
            def _(quarter=quarter):
                rs_copy(block, quarter).start()

        gt_acc[...] += tn(weights, rows)

    def gx_copy(k, i):
        dst = (t + i) % T
        return remote(
            gx_send.at[k * T + dst], gz.at[k * T + t], gx_ss.at[k * T + dst],
            gx_rs.at[k * T + t], t_dev(dst),
        )

    for k in range(Z // T):
        sums = pack_sums(
            col_acc[0:1, k * ROWS:(k + 1) * ROWS], col_acc[1:2, k * ROWS:(k + 1) * ROWS]
        )
        for quarter in range(T):
            gx_send[k * T + quarter, 0:ROWS, :] = gt_acc[
                k * ROWS:(k + 1) * ROWS, quarter * Q:(quarter + 1) * Q
            ].astype(bf16)
            gx_send[k * T + quarter, ROWS:PIECE, :] = sums
        for i in range(1, T):
            gx_copy(k, i).start()
        gz[k * T + t] = gx_send[k * T + t]

    @pl.loop(0, Z // T)
    def _(k):
        for i in range(1, T):
            src = (t + i) % T
            remote(
                gx_send.at[0], gz.at[k * T + src], gx_ss.at[0], gx_rs.at[k * T + src], t_dev(src)
            ).wait_recv()

    def f_copy(s):
        return remote(f_send.at[s], f_recv.at[s], f_ss.at[s], f_rs.at[s], z_dev((z + 1) % Z))

    def b_copy(s):
        return remote(b_send.at[s], b_recv.at[s], b_ss.at[s], b_rs.at[s], z_dev((z - 1 + Z) % Z))

    def added(left, right):
        total = left[0:ROWS].astype(f32) + right[0:ROWS].astype(f32)
        off, diag = unpack_sums(left[ROWS:PIECE].astype(f32) + right[ROWS:PIECE].astype(f32))
        return total.astype(bf16), pack_sums(off, diag)

    f_send[0] = gz[(z + half) % Z]
    f_copy(0).start()
    b_send[0] = gz[(z + half + 1) % Z]
    b_copy(0).start()

    @pl.loop(1, half)
    def _(s):
        f_copy(s - 1).wait_recv()
        main, sums = added(f_recv[s - 1], gz[(z + half - s) % Z])
        f_send[s, 0:ROWS, :] = main
        f_send[s, ROWS:PIECE, :] = sums
        f_copy(s).start()

        @pl.when(s < half - 1)
        def _():
            b_copy(s - 1).wait_recv()
            main, sums = added(b_recv[s - 1], gz[(z + half + 1 + s) % Z])
            b_send[s, 0:ROWS, :] = main
            b_send[s, ROWS:PIECE, :] = sums
            b_copy(s).start()

    def rs_sum(i, carry):
        total, sums = carry
        src = (p + i) % n_plane
        remote(rs_send.at[0], rs_recv.at[src], ri_ss.at[0], ri_rs.at[src], plane_dev(src)).wait_recv()
        return (
            total + rs_recv[src, 0:ROWS, :].astype(f32),
            sums + rs_recv[src, ROWS:PIECE, :].astype(f32),
        )

    total_img, sums_img = lax.fori_loop(
        1, n_plane, rs_sum,
        (rs_send[p, 0:ROWS, :].astype(f32), rs_send[p, ROWS:PIECE, :].astype(f32)),
    )
    f_copy(half - 1).wait_recv()
    b_copy(half - 2).wait_recv()
    total_txt = (
        gz[z, 0:ROWS, :].astype(f32)
        + f_recv[half - 1, 0:ROWS, :].astype(f32)
        + b_recv[half - 2, 0:ROWS, :].astype(f32)
    )
    sums_txt = (
        gz[z, ROWS:PIECE, :].astype(f32)
        + f_recv[half - 1, ROWS:PIECE, :].astype(f32)
        + b_recv[half - 2, ROWS:PIECE, :].astype(f32)
    )

    def embedding_grad(total, sums, target):
        off, diag = unpack_sums(sums)
        factor = as_columns(coef / (off + diag))
        return factor * (total - as_columns(off) * target)

    own_img = own[0].astype(f32)
    own_txt = own[1].astype(f32)
    g_img = embedding_grad(total_img, sums_img, own_txt)
    g_txt = embedding_grad(total_txt, sums_txt, own_img)

    def al_copy(i):
        return remote(alb.at[t], alb.at[t], al_ss.at[i - 1], al_rs.at[t], t_dev((t + i) % T))

    alb[t] = jnp.where(index8 == 0, row_sums(own_img * g_img), row_sums(own_txt * g_txt))
    for i in range(1, T):
        al_copy(i).start()
    for i in range(1, T):
        src = (t + i) % T
        remote(alb.at[src], alb.at[src], al_ss.at[i - 1], al_rs.at[src], t_dev(src)).wait_recv()
    align = (alb[0] + alb[1]) + (alb[2] + alb[3])
    gr_img = ((g_img - own_img * as_columns(align[0:1])) * invc[0]).astype(bf16)
    gr_txt = ((g_txt - own_txt * as_columns(align[1:2])) * invc[1]).astype(bf16)
    gr_own[0] = gr_img
    gr_own[1] = gr_txt

    def gr_copy(m, i):
        return remote(
            gr_own.at[m], gr_all.at[m, :, pl.ds(pl.multiple_of(t * Q, Q), Q)],
            gr_ss.at[m * T + i], gr_rs.at[m * T + t], t_dev((t + i) % T),
        )

    own_gr = []
    for m in range(2):
        for i in range(1, T):
            gr_copy(m, i).start()
        own_gr.append(
            pltpu.make_async_copy(
                gr_own.at[m], gr_all.at[m, :, pl.ds(pl.multiple_of(t * Q, Q), Q)], gr_ss.at[m * T]
            )
        )
        own_gr[m].start()

    diy, dty = di // ny, dt // ny
    for k in range(ny):
        for c in range(0, diy, 64):
            y_send[k, c:c + 64, :] = tn(
                imgf[:, k * diy + c:k * diy + c + 64], gr_img
            ).astype(bf16)
        for c in range(0, dty, 64):
            y_send[k, diy + c:diy + c + 64, :] = tn(
                txtf[:, k * dty + c:k * dty + c + 64], gr_txt
            ).astype(bf16)

    def y_copy(i):
        dst = (y + i) % ny
        return remote(y_send.at[dst], y_recv.at[y], y_ss.at[i], y_rs.at[y], y_dev(dst))

    for i in range(1, ny):
        y_copy(i).start()

    for m in range(2):
        own_gr[m].wait()
        for i in range(1, T):
            src = (t + i) % T
            remote(
                gr_own.at[m], gr_all.at[m, :, pl.ds(pl.multiple_of(src * Q, Q), Q)],
                gr_ss.at[m * T + i], gr_rs.at[m * T + src], t_dev(src),
            ).wait_recv()
    own_psi.wait()
    own_pst.wait()

    @pl.loop(1, T)
    def _(i):
        for copy in pp_lands(i):
            copy.wait_recv()

    gif[...] = nt(gr_all[0], psi[...])
    gtf[...] = nt(gr_all[1], pst[...])

    zsum[...] = y_send[y].astype(f32)
    for i in range(1, ny):
        src = (y + i) % ny
        remote(y_send.at[0], y_recv.at[src], y_ss.at[i], y_rs.at[src], y_dev(src)).wait_recv()
        zsum[...] += y_recv[src].astype(f32)
    x_send[...] = zsum[...].astype(bf16)
    x_dev = (dp - xl + (XL - 1 - xl), t)
    x_copy = remote(x_send, x_recv, x_ss.at[0], x_rs.at[0], x_dev)
    if XL == 2:
        x_copy.start()
        x_copy.wait_recv()
        zsum[...] = x_send[...].astype(f32) + x_recv[...].astype(f32)

    per_i, per_t = diy // (Z * XL), dty // (Z * XL)
    win = window_of(per_i)

    def z_copy(i):
        dst = (z + i) % Z
        return remote(z_send.at[dst], z_recv.at[z], z_ss.at[i], z_rs.at[z], z_dev(dst))

    @pl.loop(0, Z)
    def _(i):
        dst = (z + i) % Z
        first = ((dst * XL + xl) * per_i) // 8 * 8
        z_send[dst, 0:win, :] = zsum[pl.ds(pl.multiple_of(first, 8), win), :]
        z_send[dst, win:win + per_t, :] = zsum[
            pl.ds(pl.multiple_of(diy + (dst * XL + xl) * per_t, 8), per_t), :
        ]

        @pl.when(i > 0)
        def _():
            z_copy(i).start()

    def z_add(i, total):
        src = (z + i) % Z
        remote(z_send.at[0], z_recv.at[src], z_ss.at[i], z_rs.at[src], z_dev(src)).wait_recv()
        return total + z_recv[src]

    total = lax.fori_loop(1, Z, z_add, z_send[z])
    shift = ((z * XL + xl) * per_i) % 8
    result = total[0:per_i]
    for k in sorted({(k * per_i) % 8 for k in range(8)} - {0}):
        result = jnp.where(shift == k, total[k:k + per_i], result)
    gip[...] = result
    gtp[...] = total[win:win + per_t]

    for i in range(1, T):
        sq_copy(i).wait_send()
        al_copy(i).wait_send()
        for copy in pp_copies(i):
            copy.wait_send()
        for m in range(2):
            gr_copy(m, i).wait_send()
        for k in range(Z // T):
            gx_copy(k, i).wait_send()

    @pl.loop(1, n_plane)
    def _(i):
        ig_copy(i).wait_send()
        q = (p + i) % n_plane
        rs_copy(q // T, q % T).wait_send()

    @pl.loop(0, half)
    def _(s):
        zf_copy(s).wait_send()
        f_copy(s).wait_send()

    @pl.loop(0, half - 1)
    def _(s):
        zb_copy(s).wait_send()
        b_copy(s).wait_send()

    @pl.loop(0, Z)
    def _(piece):
        @pl.when(piece % T != t)
        def _():
            tx_remote(piece).wait_send()

    for i in range(1, ny):
        y_copy(i).wait_send()
    if XL == 2:
        x_copy.wait_send()

    @pl.loop(1, Z)
    def _(i):
        z_copy(i).wait_send()


def shards(ny, img_feat, txt_feat, img_proj, txt_proj, logit_scale):
    di, dt = img_feat.shape[1], txt_feat.shape[1]
    n_blocks = ny * XL
    n_plane = n_blocks * T
    keys = Z // T * ROWS
    emb = T * Q
    half = Z // 2
    ndp = ny * Z * XL
    diy, dty = di // ny, dt // ny
    win = window_of(diy // (Z * XL))
    per_t = dty // (Z * XL)
    dma = pltpu.SemaphoreType.DMA
    vmem = pltpu.VMEM
    scratch = [
        vmem((T, 8, ROWS), f32),
        vmem((2, ROWS, Q), f32),
        vmem((2, ROWS, Q), bf16),
        vmem((n_blocks * ROWS, emb), bf16),
        vmem((Z, ROWS, Q), bf16),
        vmem((keys, emb), bf16),
        vmem((di // T, emb), bf16),
        vmem((dt // T, emb), bf16),
        vmem((keys, emb), f32),
        vmem((8, keys), f32),
        vmem((n_plane, PIECE, Q), bf16),
        vmem((n_plane, PIECE, Q), bf16),
        vmem((Z, PIECE, Q), bf16),
        vmem((Z, PIECE, Q), bf16),
        vmem((half, PIECE, Q), bf16),
        vmem((half, PIECE, Q), bf16),
        vmem((half, PIECE, Q), bf16),
        vmem((half, PIECE, Q), bf16),
        vmem((T, 8, ROWS), f32),
        vmem((2, ROWS, Q), bf16),
        vmem((2, ROWS, emb), bf16),
        vmem((ny, diy + dty, Q), bf16),
        vmem((ny, diy + dty, Q), bf16),
        vmem((diy + dty, Q), bf16),
        vmem((diy + dty, Q), bf16),
        vmem((diy + dty, Q), f32),
        vmem((Z, win + per_t, Q), f32),
        vmem((Z, win + per_t, Q), f32),
    ]
    sems = [
        T, T, 2 * T, 2 * T, n_plane, n_plane, half, half, half, half,
        Z, Z, n_plane, n_plane, Z, Z, half, half, half, half,
        T, T, 2 * T, 2 * T, max(ny, 2), max(ny, 2), 1, 1, Z, Z,
    ]
    scratch += [dma((n,)) for n in sems]
    whole = pl.BlockSpec(memory_space=pltpu.VMEM)
    return pl.pallas_call(
        functools.partial(kernel, ny, di, dt),
        out_shape=(
            jax.ShapeDtypeStruct((di // ndp, Q), f32),
            jax.ShapeDtypeStruct((dt // ndp, Q), f32),
            jax.ShapeDtypeStruct((ROWS, di // T), f32),
            jax.ShapeDtypeStruct((ROWS, dt // T), f32),
        ),
        in_specs=[pl.BlockSpec(memory_space=pltpu.SMEM)] + [whole] * 4,
        out_specs=(whole,) * 4,
        scratch_shapes=scratch,
        compiler_params=pltpu.CompilerParams(
            collective_id=0, has_side_effects=True, vmem_limit_bytes=48 * 1024 * 1024
        ),
    )(logit_scale, img_feat, txt_feat, img_proj, txt_proj)


def solution(mesh):
    ny = mesh.shape["dp"] // (Z * XL)
    return jax.shard_map(
        functools.partial(shards, ny),
        mesh=mesh,
        in_specs=(P("dp", None), P("dp", None), P(None, "tensor"), P(None, "tensor"), P()),
        out_specs=(P("dp", "tensor"), P("dp", "tensor"), P("dp", "tensor"), P("dp", "tensor")),
        check_vma=False,
    )
```

```python
import functools

import jax
import jax.numpy as jnp
from jax import lax
from jax.experimental import pallas as pl
from jax.experimental.pallas import tpu as pltpu
from jax.sharding import PartitionSpec as P

Z = 16
XL = 2
T = 4
ROWS = 128
Q = 128
SUMS = 16
PIECE = ROWS + SUMS
eps = 1e-06
loss_factor = 256.0
f32 = jnp.float32
bf16 = jnp.bfloat16


def nt(left, right):
    return lax.dot_general(left, right, (((1,), (1,)), ((), ())), preferred_element_type=f32)


def tn(left, right):
    return lax.dot_general(left, right, (((0,), (0,)), ((), ())), preferred_element_type=f32)


def row_sums(values):
    return jnp.sum(jnp.transpose(values), axis=0, keepdims=True)


def as_columns(row):
    return jnp.transpose(jnp.broadcast_to(row, (ROWS, ROWS)))


def rows_of(*rows):
    index = lax.broadcasted_iota(jnp.int32, (8, rows[0].shape[1]), 0)
    out = jnp.zeros((8, rows[0].shape[1]), f32)
    for k, row in enumerate(rows):
        out = jnp.where(index == k, row, out)
    return out


def pack(values):
    high = values.astype(bf16)
    return jnp.concatenate([high, (values - high.astype(f32)).astype(bf16)], axis=0)


def unpack(parts):
    parts = parts.astype(f32)
    return parts[0:8] + parts[8:16]


def window_of(per):
    return max(-(-(((k * per) % 8) + per) // 8) * 8 for k in range(8))


def kernel(
    ny, di, dt,
    scale_ref, imgf_hbm, txtf_hbm, imgp_hbm, txtp_hbm,
    gip, gtp, gif, gtf,
    imgf, txtf, imgp, txtp,
    sqb, invr, own, img_all, zbuf, txt_all,
    psi, pst, gt_acc, col_acc,
    cs_send, cs_recv, rs_mid, rs_recv, gx_send, gx_recv, ga_send, ga_recv,
    gr_own, gr_all, yi_send, yi_recv, yt_send, yt_recv,
    xi_send, xi_recv, xt_send, xt_recv, zi_sum, zt_sum, zi_send, zi_recv, zt_send, zt_recv,
    in_ss, sq_ss, sq_rs, pp_ss, pp_rs, ig_ss, fw_ss, ig_rs, za_ss, za_rs,
    tx_ss, tx_rs, cs_ss, cs_rs, ri_ss, ri_rs, gx_ss, gx_rs, ga_ss, ga_rs,
    gr_ss, gr_rs, yi_ss, yi_rs, yt_ss, yt_rs, x_ss, x_rs, zi_ss, zi_rs, zt_ss, zt_rs,
):
    n_blocks = ny * XL
    n_plane = n_blocks * T
    n_half = n_plane // 2
    na = Z // T
    batch = ny * Z * XL * ROWS
    dp = lax.axis_index("dp")
    t = lax.axis_index("tensor")
    core = t % 2
    xl = dp % XL
    z = (dp // XL) % Z
    y = dp // (XL * Z)
    b = y * XL + xl
    p = b * T + t
    h = p // 2
    a = z // T
    c = z % T

    def plane_dev(q):
        block = q // T
        return (((block // XL) * Z + z) * XL + block % XL, q % T)

    def zt_dev(other, tensor):
        return ((y * Z + other) * XL + xl, tensor)

    def z_dev(other):
        return zt_dev(other, t)

    def y_dev(other):
        return ((other * Z + z) * XL + xl, t)

    def t_dev(other):
        return (dp, other)

    sibling = (dp, t + 1 - 2 * core)

    def remote(src, dst, send, recv, dev):
        return pltpu.make_async_remote_copy(
            src_ref=src, dst_ref=dst, send_sem=send, recv_sem=recv,
            device_id=dev, device_id_type=pl.DeviceIdType.MESH,
        )

    barrier = pltpu.get_barrier_semaphore()

    def greet(dev):
        pl.semaphore_signal(barrier, inc=1, device_id=dev, device_id_type=pl.DeviceIdType.MESH)

    @pl.loop(1, Z)
    def _(i):
        greet(z_dev((z + i) % Z))

    loads = [
        pltpu.make_async_copy(src, dst, in_ss.at[k])
        for k, (src, dst) in enumerate(
            [(imgf_hbm, imgf), (imgp_hbm, imgp), (txtf_hbm, txtf), (txtp_hbm, txtp)]
        )
    ]
    for copy in loads:
        copy.start()

    for e in (1, 2, Z - 1, Z - 2):
        for i in range(1, T):
            greet(zt_dev((z + e) % Z, (t + i) % T))

    @pl.loop(1, n_plane)
    def _(i):
        greet(plane_dev((p + i) % n_plane))

    scale = scale_ref[0]
    coef = scale * (loss_factor / (2.0 * batch))

    loads[0].wait()
    loads[1].wait()
    raw_img = jnp.dot(imgf[...], imgp[...], preferred_element_type=f32)
    loads[2].wait()
    loads[3].wait()
    raw_txt = jnp.dot(txtf[...], txtp[...], preferred_element_type=f32)
    sqb[t] = rows_of(row_sums(raw_img * raw_img), row_sums(raw_txt * raw_txt))
    pl.semaphore_wait(barrier, n_plane - 1 + Z - 1 + 4 * (T - 1))

    def sq_copy(i):
        return remote(sqb.at[t], sqb.at[t], sq_ss.at[i - 1], sq_rs.at[t], t_dev((t + i) % T))

    for i in range(1, T):
        sq_copy(i).start()
    for i in range(1, T):
        src = (t + i) % T
        remote(sqb.at[src], sqb.at[src], sq_ss.at[i - 1], sq_rs.at[src], t_dev(src)).wait_recv()
    square = (sqb[0] + sqb[1]) + (sqb[2] + sqb[3])
    inv = lax.rsqrt(square + eps)
    invr[...] = inv
    emb_txt = (raw_txt * as_columns(inv[1:2])).astype(bf16)
    own[1] = emb_txt
    zbuf[a] = emb_txt

    def img_slot(q):
        return img_all.at[
            pl.ds(pl.multiple_of((q // T) * ROWS, ROWS), ROWS),
            pl.ds(pl.multiple_of((q % T) * Q, Q), Q),
        ]

    def txt_slot(k, quarter):
        return txt_all.at[
            pl.ds(pl.multiple_of(k * ROWS, ROWS), ROWS),
            pl.ds(pl.multiple_of(quarter * Q, Q), Q),
        ]

    def za_copy(o):
        return remote(zbuf.at[a], zbuf.at[a], za_ss.at[o], za_rs.at[a], z_dev((z + T * o) % Z))

    def za_land(o):
        src = (a + o) % na
        return remote(zbuf.at[src], zbuf.at[src], za_ss.at[o], za_rs.at[src], z_dev((z + T * o) % Z))

    two = 2 - 4 * core

    def tx_copy(k, m):
        delta = (0, 1, two, -1)[m]
        return remote(
            zbuf.at[k], txt_slot(k, t), tx_ss.at[k * T + m], tx_rs.at[k * T + t],
            zt_dev((z - delta + Z) % Z, c),
        )

    def tx_local(k):
        return pltpu.make_async_copy(zbuf.at[k], txt_slot(k, t), tx_ss.at[k * T])

    def pass_on(k):
        for m in range(1, T):
            tx_copy(k, m).start()

        @pl.when(c != t)
        def _():
            tx_copy(k, 0).start()

        @pl.when(c == t)
        def _():
            tx_local(k).start()

    far_first = sorted(range(1, na), key=lambda o: -min(o, na - o))
    for o in far_first:
        za_copy(o).start()
    pass_on(a)

    emb_img = (raw_img * as_columns(inv[0:1])).astype(bf16)
    own[0] = emb_img
    own_img_copy = pltpu.make_async_copy(own.at[0], img_slot(p), in_ss.at[0])
    own_img_copy.start()

    def same_core(i):
        return ((h + i) % n_half) * 2 + core

    def ig_copy(i):
        return remote(own.at[0], img_slot(p), ig_ss.at[i], ig_rs.at[p], plane_dev(same_core(i)))

    def ig_land(i):
        q = same_core(i)
        return remote(own.at[0], img_slot(q), ig_ss.at[i], ig_rs.at[q], plane_dev(q))

    def fw_copy(i):
        q = same_core(i)
        return remote(img_slot(q), img_slot(q), fw_ss.at[i], ig_rs.at[q], sibling)

    def fw_land(i):
        q = ((h + i) % n_half) * 2 + 1 - core
        return remote(img_slot(q), img_slot(q), fw_ss.at[i], ig_rs.at[q], sibling)

    fw_own = remote(own.at[0], img_slot(p), fw_ss.at[0], ig_rs.at[p], sibling)

    @pl.loop(1, n_half)
    def _(i):
        ig_copy(i).start()

    fw_own.start()

    near_first = far_first[::-1]
    for o in [o for o in near_first if min(o, na - o) == 1]:
        za_land(o).wait_recv()
        pass_on((a + o) % na)

    @pl.loop(1, n_half)
    def _(i):
        ig_land(i).wait_recv()
        fw_copy(i).start()

    for o in [o for o in near_first if min(o, na - o) > 1]:
        za_land(o).wait_recv()
        pass_on((a + o) % na)

    own_img_copy.wait()

    @pl.loop(0, n_half)
    def _(i):
        fw_land(i).wait_recv()

    @pl.when(c == t)
    def _():
        for k in range(na):
            tx_local(k).wait()

    mine = (t - c + T) % T

    @pl.loop(0, na)
    def _(k):
        for quarter in range(T):
            @pl.when((mine != 0) | (t != quarter))
            def _(quarter=quarter):
                remote(
                    zbuf.at[0], txt_slot(k, quarter), tx_ss.at[0],
                    tx_rs.at[k * T + quarter], sibling,
                ).wait_recv()

    keys = na * ROWS
    gt_acc[...] = jnp.zeros_like(gt_acc)
    col_acc[...] = jnp.zeros_like(col_acc)

    def fold(values):
        return sum(values[:, k * ROWS:(k + 1) * ROWS] for k in range(keys // ROWS))

    def cs_copy(block):
        return remote(
            cs_send.at[pl.ds((1 - core) * n_half + block * 2, 2)],
            cs_recv.at[pl.ds(block * 2, 2)], cs_ss.at[block], cs_rs.at[block], sibling,
        )

    def rs_copy(k):
        return remote(
            rs_mid.at[k], rs_recv.at[h], ri_ss.at[k], ri_rs.at[h], plane_dev(k * 2 + core)
        )

    def both_cores(block):
        cs_copy(block).wait_recv()
        for part in range(2):
            k = block * 2 + part
            one = cs_send.at[core * n_half + k]
            other = cs_recv.at[k]
            rs_mid[k, 0:ROWS, :] = (
                one[0:ROWS, :].astype(f32) + other[0:ROWS, :].astype(f32)
            ).astype(bf16)
            rs_mid[k, ROWS:PIECE, :] = pack(unpack(one[ROWS:PIECE, :]) + unpack(other[ROWS:PIECE, :]))

            @pl.when(k != h)
            def _(k=k):
                rs_copy(k).start()

    @pl.loop(0, n_blocks)
    def _(n):
        block = (b + 1 + n) % n_blocks
        rows = img_all[pl.ds(pl.multiple_of(block * ROWS, ROWS), ROWS), :]
        cos = nt(rows, txt_all[...])
        expo = jnp.exp(scale * (cos - 1.0))
        i = lax.broadcasted_iota(jnp.int32, (ROWS, keys), 0)
        j = lax.broadcasted_iota(jnp.int32, (ROWS, keys), 1)
        mask = (j - i) == jnp.where((block == b) & (t == c), a * ROWS, -2 * ROWS)
        weights = jnp.where(mask, 0.0, expo).astype(bf16)
        off = weights.astype(f32)
        inner = off * cos
        diag = jnp.sum(jnp.where(mask, expo, 0.0), axis=0, keepdims=True)
        match = jnp.sum(jnp.where(mask, cos, 0.0), axis=0, keepdims=True)
        sums = pack(
            rows_of(row_sums(fold(off)), fold(diag), row_sums(fold(inner)), fold(match))
        )
        col_acc[...] += rows_of(
            jnp.sum(off, axis=0, keepdims=True), diag,
            jnp.sum(inner, axis=0, keepdims=True), match,
        )
        part = jnp.dot(weights, txt_all[...], preferred_element_type=f32)
        for quarter in range(T):
            k = (quarter % 2) * n_half + block * 2 + quarter // 2
            cs_send[k, 0:ROWS, :] = part[:, quarter * Q:(quarter + 1) * Q].astype(bf16)
            cs_send[k, ROWS:PIECE, :] = sums
        cs_copy(block).start()
        gt_acc[...] += tn(weights, rows)

    def gx_copy(k, quarter):
        delta = jnp.where(
            mine == 0, 0, jnp.where(mine == 1, 1, jnp.where(mine == 3, -1, 2 - 4 * (quarter % 2)))
        )
        return remote(
            gx_send.at[k * T + quarter], gx_recv.at[k * T + mine], gx_ss.at[k * T + quarter],
            gx_rs.at[k * T + mine], zt_dev((z + delta + Z) % Z, quarter),
        )

    for k in range(na):
        sums = pack(col_acc[:, k * ROWS:(k + 1) * ROWS])
        for quarter in range(T):
            slot = k * T + quarter
            gx_send[slot, 0:ROWS, :] = gt_acc[
                k * ROWS:(k + 1) * ROWS, quarter * Q:(quarter + 1) * Q
            ].astype(bf16)
            gx_send[slot, ROWS:PIECE, :] = sums

    @pl.loop(0, na)
    def _(n):
        k = (a + na // 2 + n) % na
        for quarter in range(T):
            @pl.when((mine != 0) | (t != quarter))
            def _(quarter=quarter):
                gx_copy(k, quarter).start()

    @pl.loop(0, n_blocks)
    def _(n):
        both_cores((b + 1 + n) % n_blocks)

    def ga_copy(o):
        return remote(
            ga_send.at[o], ga_recv.at[a], ga_ss.at[o], ga_rs.at[a], z_dev((z + T * o) % Z)
        )

    def near_sum(o):
        k = (a + o) % na

        @pl.when(c == t)
        def _():
            gx_recv[k * T] = gx_send[k * T + t]

        for m in range(T):
            wait = remote(
                gx_send.at[0], gx_recv.at[k * T + m], gx_ss.at[0], gx_rs.at[k * T + m], sibling
            ).wait_recv
            if m == 0:
                pl.when(c != t)(wait)
            else:
                wait()
        total = sum(gx_recv[k * T + m, 0:ROWS, :].astype(f32) for m in range(T))
        ga_send[o, 0:ROWS, :] = total.astype(bf16)
        ga_send[o, ROWS:PIECE, :] = pack(
            sum(unpack(gx_recv[k * T + m, ROWS:PIECE, :]) for m in range(T))
        )

    for o in far_first:
        near_sum(o)
        ga_copy(o).start()
    near_sum(0)

    def raw_grad(total, sums, emb, target, inv_row):
        off, diag, inner, match = (sums[k:k + 1] for k in range(4))
        factor = coef / (off + diag) * inv_row
        align = inner - off * match
        return (
            as_columns(factor) * (total - as_columns(off) * target - as_columns(align) * emb)
        ).astype(bf16)

    def gr_copy(m, i):
        return remote(
            gr_own.at[m], gr_all.at[m, :, pl.ds(pl.multiple_of(t * Q, Q), Q)],
            gr_ss.at[m * T + i], gr_rs.at[m * T + t], t_dev((t + i) % T),
        )

    own_gr = [
        pltpu.make_async_copy(
            gr_own.at[m], gr_all.at[m, :, pl.ds(pl.multiple_of(t * Q, Q), Q)], gr_ss.at[m * T]
        )
        for m in range(2)
    ]

    diy, dty = di // ny, dt // ny
    per_i, per_t = diy // (Z * XL), dty // (Z * XL)
    win = window_of(per_i)

    class Proj:
        def __init__(self, feat, per_y, send, recv, ss, rs, x_send, x_recv, x_sem, zsum, m):
            self.__dict__.update(locals())

        def y_copy(self, i):
            dst = (y + i) % ny
            return remote(
                self.send.at[pl.ds(pl.multiple_of(dst * self.per_y, 16), self.per_y)],
                self.recv.at[y], self.ss.at[i], self.rs.at[y], y_dev(dst),
            )

        def x_copy(self):
            return remote(
                self.x_send, self.x_recv, x_ss.at[self.x_sem], x_rs.at[self.x_sem],
                (dp - xl + (XL - 1 - xl), t),
            )

        def begin(self, grad):
            gr_own[self.m] = grad
            for k in range(0, self.feat.shape[1], 128):
                self.send[k:k + 128, :] = tn(self.feat[:, k:k + 128], grad).astype(bf16)
            for i in range(1, ny):
                self.y_copy(i).start()

        def middle(self):
            self.zsum[...] = self.send[
                pl.ds(pl.multiple_of(y * self.per_y, 16), self.per_y), :
            ].astype(f32)
            for i in range(1, ny):
                src = (y + i) % ny
                remote(
                    self.send.at[pl.ds(0, self.per_y)], self.recv.at[src], self.ss.at[i],
                    self.rs.at[src], y_dev(src),
                ).wait_recv()
            total = self.zsum[...]
            for i in range(1, ny):
                total += self.recv[(y + i) % ny].astype(f32)
            self.zsum[...] = total
            if XL == 2:
                self.x_send[...] = total.astype(bf16)
                self.x_copy().start()

        def last(self):
            if XL == 2:
                self.x_copy().wait_recv()
                self.zsum[...] += self.x_recv[...].astype(f32)

        def finish(self):
            for i in range(1, ny):
                self.y_copy(i).wait_send()
            if XL == 2:
                self.x_copy().wait_send()

    img = Proj(imgf, diy, yi_send, yi_recv, yi_ss, yi_rs, xi_send, xi_recv, 0, zi_sum, 0)
    txt = Proj(txtf, dty, yt_send, yt_recv, yt_ss, yt_rs, xt_send, xt_recv, 1, zt_sum, 1)

    def rs_sum(i, carry):
        total, sums = carry
        src = (h + i) % n_half
        remote(
            rs_mid.at[0], rs_recv.at[src], ri_ss.at[0], ri_rs.at[src], sibling
        ).wait_recv()
        return (
            total + rs_recv[src, 0:ROWS, :].astype(f32),
            sums + unpack(rs_recv[src, ROWS:PIECE, :]),
        )

    total_img, sums_img = lax.fori_loop(
        1, n_half, rs_sum, (rs_mid[h, 0:ROWS, :].astype(f32), unpack(rs_mid[h, ROWS:PIECE, :]))
    )
    own_img = own[0].astype(f32)
    own_txt = own[1].astype(f32)
    img.begin(raw_grad(total_img, sums_img, own_img, own_txt, invr[0:1, :]))

    total_txt = ga_send[0, 0:ROWS, :].astype(f32)
    sums_txt = unpack(ga_send[0, ROWS:PIECE, :])
    for o in near_first:
        src = (a + o) % na
        remote(ga_send.at[0], ga_recv.at[src], ga_ss.at[o], ga_rs.at[src], sibling).wait_recv()
        total_txt += ga_recv[src, 0:ROWS, :].astype(f32)
        sums_txt += unpack(ga_recv[src, ROWS:PIECE, :])
    txt.begin(raw_grad(total_txt, sums_txt, own_txt, own_img, invr[1:2, :]))

    img.middle()
    txt.middle()

    for m in range(2):
        own_gr[m].start()
        for i in range(1, T):
            gr_copy(m, i).start()
    di4, dt4 = di // T, dt // T

    def pp_pair(i, src, first):
        other = (t + i) % T
        quarter = pl.ds(pl.multiple_of(src * Q, Q), Q)
        return (
            remote(
                imgp.at[pl.ds(pl.multiple_of(first * di4, 16), di4), :], psi.at[:, quarter],
                pp_ss.at[2 * i], pp_rs.at[2 * src], t_dev(other),
            ),
            remote(
                txtp.at[pl.ds(pl.multiple_of(first * dt4, 16), dt4), :], pst.at[:, quarter],
                pp_ss.at[2 * i + 1], pp_rs.at[2 * src + 1], t_dev(other),
            ),
        )

    def pp_copies(i):
        return pp_pair(i, t, (t + i) % T)

    for i in range(1, T):
        for copy in pp_copies(i):
            copy.start()
    own_pp = [
        pltpu.make_async_copy(
            ref.at[pl.ds(pl.multiple_of(t * size, 16), size), :],
            dst.at[:, pl.ds(pl.multiple_of(t * Q, Q), Q)], pp_ss.at[k],
        )
        for k, (ref, dst, size) in enumerate([(imgp, psi, di4), (txtp, pst, dt4)])
    ]
    for copy in own_pp:
        copy.start()

    def zi_copy(i):
        dst = (z + i) % Z
        return remote(zi_send.at[dst], zi_recv.at[z], zi_ss.at[i], zi_rs.at[z], z_dev(dst))

    def zt_copy(i):
        dst = (z + i) % Z
        return remote(zt_send.at[dst], zt_recv.at[z], zt_ss.at[i], zt_rs.at[z], z_dev(dst))

    img.last()

    @pl.loop(0, Z)
    def _(n):
        i = (Z // 2 + n) % Z
        dst = (z + i) % Z
        first = ((dst * XL + xl) * per_i) // 8 * 8
        zi_send[dst] = zi_sum[pl.ds(pl.multiple_of(first, 8), win), :].astype(bf16)

        @pl.when(i > 0)
        def _():
            zi_copy(i).start()

    txt.last()

    @pl.loop(0, Z)
    def _(n):
        i = (Z // 2 + n) % Z
        dst = (z + i) % Z
        first = (dst * XL + xl) * per_t
        block = zt_sum[pl.ds(pl.multiple_of(first, 8), per_t), :]
        if per_t % 16:
            block = jnp.concatenate([block, block], axis=0)
        zt_send[dst] = block.astype(bf16)

        @pl.when(i > 0)
        def _():
            zt_copy(i).start()

    for m in range(2):
        own_gr[m].wait()
        own_pp[m].wait()
        for i in range(1, T):
            src = (t + i) % T
            remote(
                gr_own.at[m], gr_all.at[m, :, pl.ds(pl.multiple_of(src * Q, Q), Q)],
                gr_ss.at[m * T + i], gr_rs.at[m * T + src], t_dev(src),
            ).wait_recv()
    for i in range(1, T):
        for copy in pp_pair(i, (t + i) % T, 0):
            copy.wait_recv()
    gif[...] = nt(gr_all[0], psi[...])
    gtf[...] = nt(gr_all[1], pst[...])

    def zi_add(i, total):
        src = (z + i) % Z
        remote(zi_send.at[0], zi_recv.at[src], zi_ss.at[i], zi_rs.at[src], sibling).wait_recv()
        return total + zi_recv[src].astype(f32)

    total = lax.fori_loop(1, Z, zi_add, zi_send[z].astype(f32))
    shift = ((z * XL + xl) * per_i) % 8
    result = total[0:per_i]
    for k in sorted({(k * per_i) % 8 for k in range(8)} - {0}):
        result = jnp.where(shift == k, total[k:k + per_i], result)
    gip[...] = result

    def zt_add(i, total):
        src = (z + i) % Z
        remote(zt_send.at[0], zt_recv.at[src], zt_ss.at[i], zt_rs.at[src], sibling).wait_recv()
        return total + zt_recv[src, 0:per_t, :].astype(f32)

    gtp[...] = lax.fori_loop(1, Z, zt_add, zt_send[z, 0:per_t, :].astype(f32))

    for i in range(1, T):
        sq_copy(i).wait_send()
        for copy in pp_copies(i):
            copy.wait_send()
        for m in range(2):
            gr_copy(m, i).wait_send()
    for o in far_first:
        za_copy(o).wait_send()
        ga_copy(o).wait_send()
    fw_own.wait_send()

    @pl.loop(1, n_half)
    def _(i):
        ig_copy(i).wait_send()
        fw_copy(i).wait_send()
        rs_copy((h + i) % n_half).wait_send()

    @pl.loop(0, n_blocks)
    def _(block):
        cs_copy(block).wait_send()

    @pl.loop(0, na)
    def _(k):
        for m in range(1, T):
            tx_copy(k, m).wait_send()

        @pl.when(c != t)
        def _():
            tx_copy(k, 0).wait_send()

        for quarter in range(T):
            @pl.when((mine != 0) | (t != quarter))
            def _(quarter=quarter):
                gx_copy(k, quarter).wait_send()

    img.finish()
    txt.finish()

    @pl.loop(1, Z)
    def _(i):
        zi_copy(i).wait_send()
        zt_copy(i).wait_send()


def shards(ny, img_feat, txt_feat, img_proj, txt_proj, logit_scale):
    di, dt = img_feat.shape[1], txt_feat.shape[1]
    n_blocks = ny * XL
    n_plane = n_blocks * T
    n_half = n_plane // 2
    na = Z // T
    keys = na * ROWS
    emb = T * Q
    ndp = ny * Z * XL
    diy, dty = di // ny, dt // ny
    win = window_of(diy // (Z * XL))
    tall = max(dty // (Z * XL), 16)
    dma = pltpu.SemaphoreType.DMA
    vmem = pltpu.VMEM
    piece = (PIECE, Q)
    scratch = [
        vmem((ROWS, di), bf16),
        vmem((ROWS, dt), bf16),
        vmem((di, Q), bf16),
        vmem((dt, Q), bf16),
        vmem((T, 8, ROWS), f32),
        vmem((8, ROWS), f32),
        vmem((2, ROWS, Q), bf16),
        vmem((n_blocks * ROWS, emb), bf16),
        vmem((na, ROWS, Q), bf16),
        vmem((keys, emb), bf16),
        vmem((di // T, emb), bf16),
        vmem((dt // T, emb), bf16),
        vmem((keys, emb), f32),
        vmem((8, keys), f32),
        vmem((n_plane, *piece), bf16),
        vmem((n_half, *piece), bf16),
        vmem((n_half, *piece), bf16),
        vmem((n_half, *piece), bf16),
        vmem((na * T, *piece), bf16),
        vmem((na * T, *piece), bf16),
        vmem((na, *piece), bf16),
        vmem((na, *piece), bf16),
        vmem((2, ROWS, Q), bf16),
        vmem((2, ROWS, emb), bf16),
        vmem((di, Q), bf16),
        vmem((ny, diy, Q), bf16),
        vmem((dt, Q), bf16),
        vmem((ny, dty, Q), bf16),
        vmem((diy, Q), bf16),
        vmem((diy, Q), bf16),
        vmem((dty, Q), bf16),
        vmem((dty, Q), bf16),
        vmem((diy, Q), f32),
        vmem((dty, Q), f32),
        vmem((Z, win, Q), bf16),
        vmem((Z, win, Q), bf16),
        vmem((Z, tall, Q), bf16),
        vmem((Z, tall, Q), bf16),
    ]
    wide = max(ny, 2)
    sems = [
        4, T, T, 2 * T, 2 * T, n_half, n_half, n_plane, na, na,
        na * T, na * T, n_blocks, n_blocks, n_half, n_half, na * T, na * T, na, na,
        2 * T, 2 * T, wide, wide, wide, wide, 2, 2, Z, Z, Z, Z,
    ]
    scratch += [dma((n,)) for n in sems]
    whole = pl.BlockSpec(memory_space=pltpu.VMEM)
    return pl.pallas_call(
        functools.partial(kernel, ny, di, dt),
        out_shape=(
            jax.ShapeDtypeStruct((di // ndp, Q), f32),
            jax.ShapeDtypeStruct((dt // ndp, Q), f32),
            jax.ShapeDtypeStruct((ROWS, di // T), f32),
            jax.ShapeDtypeStruct((ROWS, dt // T), f32),
        ),
        in_specs=[pl.BlockSpec(memory_space=pltpu.SMEM)]
        + [pl.BlockSpec(memory_space=pl.ANY)] * 4,
        out_specs=(whole,) * 4,
        scratch_shapes=scratch,
        compiler_params=pltpu.CompilerParams(
            collective_id=0, has_side_effects=True, vmem_limit_bytes=56 * 1024 * 1024
        ),
    )(logit_scale, img_feat, txt_feat, img_proj, txt_proj)


def solution(mesh):
    ny = mesh.shape["dp"] // (Z * XL)
    return jax.shard_map(
        functools.partial(shards, ny),
        mesh=mesh,
        in_specs=(P("dp", None), P("dp", None), P(None, "tensor"), P(None, "tensor"), P()),
        out_specs=(P("dp", "tensor"), P("dp", "tensor"), P("dp", "tensor"), P("dp", "tensor")),
        check_vma=False,
    )
```

```python
import functools

import jax
import jax.numpy as jnp
from jax import lax
from jax.experimental import pallas as pl
from jax.experimental.pallas import tpu as pltpu
from jax.sharding import PartitionSpec as P

Z = 16
XL = 2
T = 4
ROWS = 128
Q = 128
SUMS = 16
PIECE = ROWS + SUMS
eps = 1e-06
loss_factor = 256.0
f32 = jnp.float32
bf16 = jnp.bfloat16


def nt(left, right):
    return lax.dot_general(left, right, (((1,), (1,)), ((), ())), preferred_element_type=f32)


def tn(left, right):
    return lax.dot_general(left, right, (((0,), (0,)), ((), ())), preferred_element_type=f32)


def row_sums(values):
    return jnp.sum(jnp.transpose(values), axis=0, keepdims=True)


def as_columns(row):
    return jnp.transpose(jnp.broadcast_to(row, (ROWS, ROWS)))


def rows_of(*rows):
    index = lax.broadcasted_iota(jnp.int32, (8, rows[0].shape[1]), 0)
    out = jnp.zeros((8, rows[0].shape[1]), f32)
    for k, row in enumerate(rows):
        out = jnp.where(index == k, row, out)
    return out


def pack(values):
    high = values.astype(bf16)
    return jnp.concatenate([high, (values - high.astype(f32)).astype(bf16)], axis=0)


def unpack(parts):
    parts = parts.astype(f32)
    return parts[0:8] + parts[8:16]


def window_of(per):
    return max(-(-(((k * per) % 8) + per) // 8) * 8 for k in range(8))


def kernel(
    ny, di, dt,
    scale_ref, imgf_hbm, txtf_hbm, imgp_hbm, txtp_hbm,
    gip, gtp, gif, gtf,
    imgf, txtf, imgp, txtp,
    sqb, invr, own, img_all, zbuf, txt_all,
    psi, pst, gt_acc, col_acc, weight,
    cs_send, cs_recv, rs_mid, rs_recv, gx_send, gx_recv, ga_send, ga_recv,
    gr_own, gr_all, yi_send, yi_recv, yt_send, yt_recv,
    xi_send, xi_recv, xt_send, xt_recv, zi_sum, zt_sum, zi_send, zi_recv, zt_send, zt_recv,
    in_ss, sq_ss, sq_rs, pp_ss, pp_rs, ig_ss, fw_ss, ig_rs, za_ss, za_rs,
    tx_ss, tx_rs, cs_ss, cs_rs, ri_ss, ri_rs, gx_ss, gx_rs, ga_ss, ga_rs,
    gr_ss, gr_rs, yi_ss, yi_rs, yt_ss, yt_rs, x_ss, x_rs, zi_ss, zi_rs, zt_ss, zt_rs,
):
    n_blocks = ny * XL
    n_plane = n_blocks * T
    n_half = n_plane // 2
    na = Z // T
    batch = ny * Z * XL * ROWS
    dp = lax.axis_index("dp")
    t = lax.axis_index("tensor")
    core = t % 2
    xl = dp % XL
    z = (dp // XL) % Z
    y = dp // (XL * Z)
    b = y * XL + xl
    p = b * T + t
    h = p // 2
    xh = t // 2
    a = z // T
    c = z % T

    def plane_dev(q):
        block = q // T
        return (((block // XL) * Z + z) * XL + block % XL, q % T)

    def zt_dev(other, tensor):
        return ((y * Z + other) * XL + xl, tensor)

    def z_dev(other):
        return zt_dev(other, t)

    def y_dev(other):
        return ((other * Z + z) * XL + xl, t)

    def t_dev(other):
        return (dp, other)

    sibling = (dp, t + 1 - 2 * core)

    def remote(src, dst, send, recv, dev):
        return pltpu.make_async_remote_copy(
            src_ref=src, dst_ref=dst, send_sem=send, recv_sem=recv,
            device_id=dev, device_id_type=pl.DeviceIdType.MESH,
        )

    barrier = pltpu.get_barrier_semaphore()

    def greet(dev):
        pl.semaphore_signal(barrier, inc=1, device_id=dev, device_id_type=pl.DeviceIdType.MESH)

    @pl.loop(1, Z)
    def _(i):
        greet(z_dev((z + i) % Z))

    loads = [
        pltpu.make_async_copy(src, dst, in_ss.at[k])
        for k, (src, dst) in enumerate(
            [(imgf_hbm, imgf), (imgp_hbm, imgp), (txtf_hbm, txtf), (txtp_hbm, txtp)]
        )
    ]
    for copy in loads:
        copy.start()

    for e in (1, 2, Z - 1, Z - 2):
        for i in range(1, T):
            greet(zt_dev((z + e) % Z, (t + i) % T))

    @pl.loop(1, n_plane)
    def _(i):
        greet(plane_dev((p + i) % n_plane))

    scale = scale_ref[0]
    coef = scale * (loss_factor / (2.0 * batch))

    loads[0].wait()
    loads[1].wait()
    raw_img = jnp.dot(imgf[...], imgp[...], preferred_element_type=f32)
    loads[2].wait()
    loads[3].wait()
    raw_txt = jnp.dot(txtf[...], txtp[...], preferred_element_type=f32)
    sqb[t] = rows_of(row_sums(raw_img * raw_img), row_sums(raw_txt * raw_txt))
    pl.semaphore_wait(barrier, n_plane - 1 + Z - 1 + 4 * (T - 1))

    def sq_copy(i):
        return remote(sqb.at[t], sqb.at[t], sq_ss.at[i - 1], sq_rs.at[t], t_dev((t + i) % T))

    for i in range(1, T):
        sq_copy(i).start()
    for i in range(1, T):
        src = (t + i) % T
        remote(sqb.at[src], sqb.at[src], sq_ss.at[i - 1], sq_rs.at[src], t_dev(src)).wait_recv()
    square = (sqb[0] + sqb[1]) + (sqb[2] + sqb[3])
    inv = lax.rsqrt(square + eps)
    invr[...] = inv
    emb_txt = (raw_txt * as_columns(inv[1:2])).astype(bf16)
    own[1] = emb_txt
    zbuf[a] = emb_txt

    def img_slot(q):
        return img_all.at[
            pl.ds(pl.multiple_of((q // T) * ROWS, ROWS), ROWS),
            pl.ds(pl.multiple_of((q % T) * Q, Q), Q),
        ]

    def txt_slot(k, quarter):
        return txt_all.at[
            pl.ds(pl.multiple_of(k * ROWS, ROWS), ROWS),
            pl.ds(pl.multiple_of(quarter * Q, Q), Q),
        ]

    def za_copy(o):
        return remote(zbuf.at[a], zbuf.at[a], za_ss.at[o], za_rs.at[a], z_dev((z + T * o) % Z))

    def za_land(o):
        src = (a + o) % na
        return remote(zbuf.at[src], zbuf.at[src], za_ss.at[o], za_rs.at[src], z_dev((z + T * o) % Z))

    two = 2 - 4 * core

    def tx_copy(k, m):
        delta = (0, 1, two, -1)[m]
        return remote(
            zbuf.at[k], txt_slot(k, t), tx_ss.at[k * T + m], tx_rs.at[k * T + t],
            zt_dev((z - delta + Z) % Z, c),
        )

    def tx_local(k):
        return pltpu.make_async_copy(zbuf.at[k], txt_slot(k, t), tx_ss.at[k * T])

    def pass_on(k):
        for m in range(1, T):
            tx_copy(k, m).start()

        @pl.when(c != t)
        def _():
            tx_copy(k, 0).start()

        @pl.when(c == t)
        def _():
            tx_local(k).start()

    far_first = sorted(range(1, na), key=lambda o: -min(o, na - o))
    for o in far_first:
        za_copy(o).start()
    pass_on(a)

    emb_img = (raw_img * as_columns(inv[0:1])).astype(bf16)
    own[0] = emb_img
    own_img_copy = pltpu.make_async_copy(own.at[0], img_slot(p), in_ss.at[0])
    own_img_copy.start()

    def peer(n, flip):
        return ((b + n + n_blocks) % n_blocks) * 2 + xh + flip - 2 * xh * flip

    def ig_copy(i):
        dst = peer(-(i // 2), i % 2) * 2 + core
        return remote(own.at[0], img_slot(p), ig_ss.at[i], ig_rs.at[p], plane_dev(dst))

    def ig_land(i):
        q = peer(i // 2, i % 2) * 2 + core
        return remote(own.at[0], img_slot(q), ig_ss.at[i], ig_rs.at[q], plane_dev(q))

    def fw_copy(i):
        q = peer(i // 2, i % 2) * 2 + core
        return remote(img_slot(q), img_slot(q), fw_ss.at[i], ig_rs.at[q], sibling)

    def fw_land(i):
        q = peer(i // 2, i % 2) * 2 + 1 - core
        return remote(img_slot(q), img_slot(q), fw_ss.at[i], ig_rs.at[q], sibling)

    fw_own = remote(own.at[0], img_slot(p), fw_ss.at[0], ig_rs.at[p], sibling)

    @pl.loop(1, n_half)
    def _(i):
        ig_copy(i).start()

    fw_own.start()
    near_first = far_first[::-1]
    near_groups = [o for o in near_first if min(o, na - o) == 1]
    far_groups = [o for o in near_first if min(o, na - o) > 1]

    mine = (t - c + T) % T

    def delta_of(quarter):
        return jnp.where(
            mine == 0, 0, jnp.where(mine == 1, 1, jnp.where(mine == 3, -1, 2 - 4 * (quarter % 2)))
        )

    base = jnp.where(mine == 2, a, ((z + delta_of(0) + Z) % Z) // T)
    turn = jnp.where((mine == 2) & (c < T // 2), -1, 1)
    if na == 4:
        order = [base, (base + turn + na) % na, (base - turn + na) % na, (base + 2) % na]
    else:
        order = [(base + n) % na for n in range(na)]

    def keys_ready(k):
        for quarter in range(T):
            @pl.when((mine != 0) | (t != quarter))
            def _(quarter=quarter):
                remote(
                    zbuf.at[0], txt_slot(k, quarter), tx_ss.at[0],
                    tx_rs.at[k * T + quarter], sibling,
                ).wait_recv()

        @pl.when(c == t)
        def _():
            tx_local(k).wait()

    keys = na * ROWS
    col_acc[...] = jnp.zeros_like(col_acc)

    def fold(values):
        return sum(values[:, k * ROWS:(k + 1) * ROWS] for k in range(values.shape[1] // ROWS))

    def score(first, count, k):
        rows = img_all[pl.ds(pl.multiple_of(first, ROWS), count), :]
        cos = nt(rows, txt_all[pl.ds(pl.multiple_of(k * ROWS, ROWS), ROWS), :])
        expo = jnp.exp(scale * (cos - 1.0))
        i = lax.broadcasted_iota(jnp.int32, (count, ROWS), 0)
        j = lax.broadcasted_iota(jnp.int32, (count, ROWS), 1)
        mask = (j - i) == jnp.where((k == a) & (t == c), first - b * ROWS, ROWS)
        part = jnp.where(mask, 0.0, expo).astype(bf16)
        weight[
            pl.ds(pl.multiple_of(first, ROWS), count), pl.ds(pl.multiple_of(k * ROWS, ROWS), ROWS)
        ] = part
        none = jnp.zeros((1, ROWS), f32)
        col_acc[k] += rows_of(
            jnp.sum(part.astype(f32), axis=0, keepdims=True),
            jnp.sum(jnp.where(mask, expo, 0.0), axis=0, keepdims=True),
            none,
            jnp.sum(jnp.where(mask, cos, 0.0), axis=0, keepdims=True),
        )
        gt_acc[...] += tn(part, rows)

    def gx_copy(k, quarter):
        return remote(
            gx_send.at[k * T + quarter], gx_recv.at[k * T + mine], gx_ss.at[k * T + quarter],
            gx_rs.at[k * T + mine], zt_dev((z + delta_of(quarter) + Z) % Z, quarter),
        )

    def texts_out(k):
        total = gt_acc[...]
        rows = txt_all[pl.ds(pl.multiple_of(k * ROWS, ROWS), ROWS), :].astype(f32)
        none = jnp.zeros((1, ROWS), f32)
        sums = pack(col_acc[k] + rows_of(none, none, row_sums(fold(total * rows))))
        for quarter in range(T):
            gx_send[k * T + quarter, 0:ROWS, :] = total[:, quarter * Q:(quarter + 1) * Q].astype(bf16)
            gx_send[k * T + quarter, ROWS:PIECE, :] = sums

            @pl.when((mine != 0) | (t != quarter))
            def _(quarter=quarter):
                gx_copy(k, quarter).start()

    for o in near_groups:
        za_land(o).wait_recv()
        pass_on((a + o) % na)

    @pl.loop(1, n_half)
    def _(i):
        ig_land(i).wait_recv()
        fw_copy(i).start()

    for o in far_groups:
        za_land(o).wait_recv()
        pass_on((a + o) % na)
    own_img_copy.wait()

    @pl.loop(0, n_half)
    def _(i):
        fw_land(i).wait_recv()

    tall_rows = min(4, n_blocks) * ROWS
    for k in order:
        keys_ready(k)
        gt_acc[...] = jnp.zeros_like(gt_acc)

        @pl.loop(0, n_blocks * ROWS // tall_rows)
        def _(n, k=k):
            score(n * tall_rows, tall_rows, k)

        texts_out(k)

    def cs_copy(block):
        return remote(
            cs_send.at[pl.ds((1 - core) * n_half + block * 2, 2)],
            cs_recv.at[pl.ds(block * 2, 2)], cs_ss.at[block], cs_rs.at[block], sibling,
        )

    def rs_copy(k):
        return remote(
            rs_mid.at[k], rs_recv.at[h], ri_ss.at[k], ri_rs.at[h], plane_dev(k * 2 + core)
        )

    def both_cores(block):
        cs_copy(block).wait_recv()
        for part in range(2):
            k = block * 2 + part
            one = cs_send.at[core * n_half + k]
            other = cs_recv.at[k]
            rs_mid[k, 0:ROWS, :] = (
                one[0:ROWS, :].astype(f32) + other[0:ROWS, :].astype(f32)
            ).astype(bf16)
            rs_mid[k, ROWS:PIECE, :] = pack(unpack(one[ROWS:PIECE, :]) + unpack(other[ROWS:PIECE, :]))

            @pl.when(k != h)
            def _(k=k):
                rs_copy(k).start()

    @pl.loop(0, n_blocks)
    def _(n):
        block = (b + 1 + n) % n_blocks
        first = pl.ds(pl.multiple_of(block * ROWS, ROWS), ROWS)
        part = jnp.dot(weight[first, :], txt_all[...], preferred_element_type=f32)
        diag = jnp.where(block == b, col_acc[a], 0.0)
        sums = pack(
            rows_of(
                row_sums(fold(weight[first, :].astype(f32))), diag[1:2],
                row_sums(fold(part * img_all[first, :].astype(f32))), diag[3:4],
            )
        )
        for quarter in range(T):
            k = (quarter % 2) * n_half + block * 2 + quarter // 2
            cs_send[k, 0:ROWS, :] = part[:, quarter * Q:(quarter + 1) * Q].astype(bf16)
            cs_send[k, ROWS:PIECE, :] = sums
        cs_copy(block).start()

    def ga_copy(o):
        return remote(
            ga_send.at[o], ga_recv.at[a], ga_ss.at[o], ga_rs.at[a], z_dev((z + T * o) % Z)
        )

    def near_sum(o):
        k = (a + o) % na

        @pl.when(c == t)
        def _():
            gx_recv[k * T] = gx_send[k * T + t]

        for m in range(T):
            wait = remote(
                gx_send.at[0], gx_recv.at[k * T + m], gx_ss.at[0], gx_rs.at[k * T + m], sibling
            ).wait_recv
            if m == 0:
                pl.when(c != t)(wait)
            else:
                wait()
        total = sum(gx_recv[k * T + m, 0:ROWS, :].astype(f32) for m in range(T))
        ga_send[o, 0:ROWS, :] = total.astype(bf16)
        ga_send[o, ROWS:PIECE, :] = pack(
            sum(unpack(gx_recv[k * T + m, ROWS:PIECE, :]) for m in range(T))
        )

    for o in near_groups:
        near_sum(o)
        ga_copy(o).start()

    @pl.loop(0, n_blocks)
    def _(n):
        both_cores((b + 1 + n) % n_blocks)

    for o in far_groups:
        near_sum(o)
        ga_copy(o).start()
    near_sum(0)

    def raw_grad(total, sums, emb, target, inv_row):
        off, diag, inner, match = (sums[k:k + 1] for k in range(4))
        factor = coef / (off + diag) * inv_row
        align = inner - off * match
        return (
            as_columns(factor) * (total - as_columns(off) * target - as_columns(align) * emb)
        ).astype(bf16)

    def gr_copy(m, i):
        return remote(
            gr_own.at[m], gr_all.at[m, :, pl.ds(pl.multiple_of(t * Q, Q), Q)],
            gr_ss.at[m * T + i], gr_rs.at[m * T + t], t_dev((t + i) % T),
        )

    own_gr = [
        pltpu.make_async_copy(
            gr_own.at[m], gr_all.at[m, :, pl.ds(pl.multiple_of(t * Q, Q), Q)], gr_ss.at[m * T]
        )
        for m in range(2)
    ]

    diy, dty = di // ny, dt // ny
    per_i, per_t = diy // (Z * XL), dty // (Z * XL)
    win = window_of(per_i)

    class Proj:
        def __init__(self, feat, per_y, send, recv, ss, rs, x_send, x_recv, x_sem, zsum, m):
            self.__dict__.update(locals())

        def y_copy(self, i):
            dst = (y + i) % ny
            return remote(
                self.send.at[pl.ds(pl.multiple_of(dst * self.per_y, 16), self.per_y)],
                self.recv.at[y], self.ss.at[i], self.rs.at[y], y_dev(dst),
            )

        def x_copy(self):
            return remote(
                self.x_send, self.x_recv, x_ss.at[self.x_sem], x_rs.at[self.x_sem],
                (dp - xl + (XL - 1 - xl), t),
            )

        def begin(self, grad):
            gr_own[self.m] = grad
            for k in range(0, self.feat.shape[1], 128):
                self.send[k:k + 128, :] = tn(self.feat[:, k:k + 128], grad).astype(bf16)
            for i in range(1, ny):
                self.y_copy(i).start()

        def middle(self):
            self.zsum[...] = self.send[
                pl.ds(pl.multiple_of(y * self.per_y, 16), self.per_y), :
            ].astype(f32)
            for i in range(1, ny):
                src = (y + i) % ny
                remote(
                    self.send.at[pl.ds(0, self.per_y)], self.recv.at[src], self.ss.at[i],
                    self.rs.at[src], y_dev(src),
                ).wait_recv()
            total = self.zsum[...]
            for i in range(1, ny):
                total += self.recv[(y + i) % ny].astype(f32)
            self.zsum[...] = total
            if XL == 2:
                self.x_send[...] = total.astype(bf16)
                self.x_copy().start()

        def last(self):
            if XL == 2:
                self.x_copy().wait_recv()
                self.zsum[...] += self.x_recv[...].astype(f32)

        def finish(self):
            for i in range(1, ny):
                self.y_copy(i).wait_send()
            if XL == 2:
                self.x_copy().wait_send()

    img = Proj(imgf, diy, yi_send, yi_recv, yi_ss, yi_rs, xi_send, xi_recv, 0, zi_sum, 0)
    txt = Proj(txtf, dty, yt_send, yt_recv, yt_ss, yt_rs, xt_send, xt_recv, 1, zt_sum, 1)

    def rs_sum(i, carry):
        total, sums = carry
        src = (h + i) % n_half
        remote(
            rs_mid.at[0], rs_recv.at[src], ri_ss.at[0], ri_rs.at[src], sibling
        ).wait_recv()
        return (
            total + rs_recv[src, 0:ROWS, :].astype(f32),
            sums + unpack(rs_recv[src, ROWS:PIECE, :]),
        )

    total_img, sums_img = lax.fori_loop(
        1, n_half, rs_sum, (rs_mid[h, 0:ROWS, :].astype(f32), unpack(rs_mid[h, ROWS:PIECE, :]))
    )
    own_img = own[0].astype(f32)
    own_txt = own[1].astype(f32)
    img.begin(raw_grad(total_img, sums_img, own_img, own_txt, invr[0:1, :]))

    total_txt = ga_send[0, 0:ROWS, :].astype(f32)
    sums_txt = unpack(ga_send[0, ROWS:PIECE, :])
    for o in near_first:
        src = (a + o) % na
        remote(ga_send.at[0], ga_recv.at[src], ga_ss.at[o], ga_rs.at[src], sibling).wait_recv()
        total_txt += ga_recv[src, 0:ROWS, :].astype(f32)
        sums_txt += unpack(ga_recv[src, ROWS:PIECE, :])
    txt.begin(raw_grad(total_txt, sums_txt, own_txt, own_img, invr[1:2, :]))

    img.middle()
    txt.middle()

    for m in range(2):
        own_gr[m].start()
        for i in range(1, T):
            gr_copy(m, i).start()
    di4, dt4 = di // T, dt // T

    def pp_pair(i, src, first):
        other = (t + i) % T
        quarter = pl.ds(pl.multiple_of(src * Q, Q), Q)
        return (
            remote(
                imgp.at[pl.ds(pl.multiple_of(first * di4, 16), di4), :], psi.at[:, quarter],
                pp_ss.at[2 * i], pp_rs.at[2 * src], t_dev(other),
            ),
            remote(
                txtp.at[pl.ds(pl.multiple_of(first * dt4, 16), dt4), :], pst.at[:, quarter],
                pp_ss.at[2 * i + 1], pp_rs.at[2 * src + 1], t_dev(other),
            ),
        )

    def pp_copies(i):
        return pp_pair(i, t, (t + i) % T)

    for i in range(1, T):
        for copy in pp_copies(i):
            copy.start()
    own_pp = [
        pltpu.make_async_copy(
            ref.at[pl.ds(pl.multiple_of(t * size, 16), size), :],
            dst.at[:, pl.ds(pl.multiple_of(t * Q, Q), Q)], pp_ss.at[k],
        )
        for k, (ref, dst, size) in enumerate([(imgp, psi, di4), (txtp, pst, dt4)])
    ]
    for copy in own_pp:
        copy.start()

    def zi_copy(i):
        dst = (z + i) % Z
        return remote(zi_send.at[dst], zi_recv.at[z], zi_ss.at[i], zi_rs.at[z], z_dev(dst))

    def zt_copy(i):
        dst = (z + i) % Z
        return remote(zt_send.at[dst], zt_recv.at[z], zt_ss.at[i], zt_rs.at[z], z_dev(dst))

    img.last()

    @pl.loop(0, Z)
    def _(n):
        i = (Z // 2 + n) % Z
        dst = (z + i) % Z
        first = ((dst * XL + xl) * per_i) // 8 * 8
        zi_send[dst] = zi_sum[pl.ds(pl.multiple_of(first, 8), win), :].astype(bf16)

        @pl.when(i > 0)
        def _():
            zi_copy(i).start()

    txt.last()

    @pl.loop(0, Z)
    def _(n):
        i = (Z // 2 + n) % Z
        dst = (z + i) % Z
        first = (dst * XL + xl) * per_t
        block = zt_sum[pl.ds(pl.multiple_of(first, 8), per_t), :]
        if per_t % 16:
            block = jnp.concatenate([block, block], axis=0)
        zt_send[dst] = block.astype(bf16)

        @pl.when(i > 0)
        def _():
            zt_copy(i).start()

    for m in range(2):
        own_gr[m].wait()
        own_pp[m].wait()
        for i in range(1, T):
            src = (t + i) % T
            remote(
                gr_own.at[m], gr_all.at[m, :, pl.ds(pl.multiple_of(src * Q, Q), Q)],
                gr_ss.at[m * T + i], gr_rs.at[m * T + src], t_dev(src),
            ).wait_recv()
    for i in range(1, T):
        for copy in pp_pair(i, (t + i) % T, 0):
            copy.wait_recv()
    gif[...] = nt(gr_all[0], psi[...])
    gtf[...] = nt(gr_all[1], pst[...])

    def zi_add(i, total):
        src = (z + i) % Z
        remote(zi_send.at[0], zi_recv.at[src], zi_ss.at[i], zi_rs.at[src], sibling).wait_recv()
        return total + zi_recv[src].astype(f32)

    total = lax.fori_loop(1, Z, zi_add, zi_send[z].astype(f32))
    shift = ((z * XL + xl) * per_i) % 8
    result = total[0:per_i]
    for k in sorted({(k * per_i) % 8 for k in range(8)} - {0}):
        result = jnp.where(shift == k, total[k:k + per_i], result)
    gip[...] = result

    def zt_add(i, total):
        src = (z + i) % Z
        remote(zt_send.at[0], zt_recv.at[src], zt_ss.at[i], zt_rs.at[src], sibling).wait_recv()
        return total + zt_recv[src, 0:per_t, :].astype(f32)

    gtp[...] = lax.fori_loop(1, Z, zt_add, zt_send[z, 0:per_t, :].astype(f32))

    for i in range(1, T):
        sq_copy(i).wait_send()
        for copy in pp_copies(i):
            copy.wait_send()
        for m in range(2):
            gr_copy(m, i).wait_send()
    for o in far_first:
        za_copy(o).wait_send()
        ga_copy(o).wait_send()
    fw_own.wait_send()

    @pl.loop(1, n_half)
    def _(i):
        ig_copy(i).wait_send()
        fw_copy(i).wait_send()
        rs_copy((h + i) % n_half).wait_send()

    @pl.loop(0, n_blocks)
    def _(block):
        cs_copy(block).wait_send()

    @pl.loop(0, na)
    def _(k):
        for m in range(1, T):
            tx_copy(k, m).wait_send()

        @pl.when(c != t)
        def _():
            tx_copy(k, 0).wait_send()

        for quarter in range(T):
            @pl.when((mine != 0) | (t != quarter))
            def _(quarter=quarter):
                gx_copy(k, quarter).wait_send()

    img.finish()
    txt.finish()

    @pl.loop(1, Z)
    def _(i):
        zi_copy(i).wait_send()
        zt_copy(i).wait_send()


def shards(ny, img_feat, txt_feat, img_proj, txt_proj, logit_scale):
    di, dt = img_feat.shape[1], txt_feat.shape[1]
    n_blocks = ny * XL
    n_plane = n_blocks * T
    n_half = n_plane // 2
    na = Z // T
    keys = na * ROWS
    emb = T * Q
    ndp = ny * Z * XL
    diy, dty = di // ny, dt // ny
    win = window_of(diy // (Z * XL))
    tall = max(dty // (Z * XL), 16)
    dma = pltpu.SemaphoreType.DMA
    vmem = pltpu.VMEM
    piece = (PIECE, Q)
    scratch = [
        vmem((ROWS, di), bf16),
        vmem((ROWS, dt), bf16),
        vmem((di, Q), bf16),
        vmem((dt, Q), bf16),
        vmem((T, 8, ROWS), f32),
        vmem((8, ROWS), f32),
        vmem((2, ROWS, Q), bf16),
        vmem((n_blocks * ROWS, emb), bf16),
        vmem((na, ROWS, Q), bf16),
        vmem((keys, emb), bf16),
        vmem((di // T, emb), bf16),
        vmem((dt // T, emb), bf16),
        vmem((ROWS, emb), f32),
        vmem((na, 8, ROWS), f32),
        vmem((n_blocks * ROWS, keys), bf16),
        vmem((n_plane, *piece), bf16),
        vmem((n_half, *piece), bf16),
        vmem((n_half, *piece), bf16),
        vmem((n_half, *piece), bf16),
        vmem((na * T, *piece), bf16),
        vmem((na * T, *piece), bf16),
        vmem((na, *piece), bf16),
        vmem((na, *piece), bf16),
        vmem((2, ROWS, Q), bf16),
        vmem((2, ROWS, emb), bf16),
        vmem((di, Q), bf16),
        vmem((ny, diy, Q), bf16),
        vmem((dt, Q), bf16),
        vmem((ny, dty, Q), bf16),
        vmem((diy, Q), bf16),
        vmem((diy, Q), bf16),
        vmem((dty, Q), bf16),
        vmem((dty, Q), bf16),
        vmem((diy, Q), f32),
        vmem((dty, Q), f32),
        vmem((Z, win, Q), bf16),
        vmem((Z, win, Q), bf16),
        vmem((Z, tall, Q), bf16),
        vmem((Z, tall, Q), bf16),
    ]
    wide = max(ny, 2)
    sems = [
        4, T, T, 2 * T, 2 * T, n_half, n_half, n_plane, na, na,
        na * T, na * T, n_blocks, n_blocks, n_half, n_half, na * T, na * T, na, na,
        2 * T, 2 * T, wide, wide, wide, wide, 2, 2, Z, Z, Z, Z,
    ]
    scratch += [dma((n,)) for n in sems]
    whole = pl.BlockSpec(memory_space=pltpu.VMEM)
    return pl.pallas_call(
        functools.partial(kernel, ny, di, dt),
        out_shape=(
            jax.ShapeDtypeStruct((di // ndp, Q), f32),
            jax.ShapeDtypeStruct((dt // ndp, Q), f32),
            jax.ShapeDtypeStruct((ROWS, di // T), f32),
            jax.ShapeDtypeStruct((ROWS, dt // T), f32),
        ),
        in_specs=[pl.BlockSpec(memory_space=pltpu.SMEM)]
        + [pl.BlockSpec(memory_space=pl.ANY)] * 4,
        out_specs=(whole,) * 4,
        scratch_shapes=scratch,
        compiler_params=pltpu.CompilerParams(
            collective_id=0, has_side_effects=True, vmem_limit_bytes=56 * 1024 * 1024
        ),
    )(logit_scale, img_feat, txt_feat, img_proj, txt_proj)


def solution(mesh):
    ny = mesh.shape["dp"] // (Z * XL)
    return jax.shard_map(
        functools.partial(shards, ny),
        mesh=mesh,
        in_specs=(P("dp", None), P("dp", None), P(None, "tensor"), P(None, "tensor"), P()),
        out_specs=(P("dp", "tensor"), P("dp", "tensor"), P("dp", "tensor"), P("dp", "tensor")),
        check_vma=False,
    )
```

```python
import functools

import jax
import jax.numpy as jnp
from jax import lax
from jax.experimental import pallas as pl
from jax.experimental.pallas import tpu as pltpu
from jax.sharding import PartitionSpec as P

Z = 16
XL = 2
T = 4
ROWS = 128
Q = 128
SUMS = 16
PIECE = ROWS + SUMS
eps = 1e-06
loss_factor = 256.0
f32 = jnp.float32
bf16 = jnp.bfloat16


def nt(left, right):
    return lax.dot_general(left, right, (((1,), (1,)), ((), ())), preferred_element_type=f32)


def tn(left, right):
    return lax.dot_general(left, right, (((0,), (0,)), ((), ())), preferred_element_type=f32)


def row_sums(values):
    return jnp.sum(jnp.transpose(values), axis=0, keepdims=True)


def as_columns(row):
    return jnp.transpose(jnp.broadcast_to(row, (ROWS, ROWS)))


def rows_of(*rows):
    index = lax.broadcasted_iota(jnp.int32, (8, rows[0].shape[1]), 0)
    out = jnp.zeros((8, rows[0].shape[1]), f32)
    for k, row in enumerate(rows):
        out = jnp.where(index == k, row, out)
    return out


def pack(values):
    high = values.astype(bf16)
    return jnp.concatenate([high, (values - high.astype(f32)).astype(bf16)], axis=0)


def unpack(parts):
    parts = parts.astype(f32)
    return parts[0:8] + parts[8:16]


def window_of(per):
    return max(-(-(((k * per) % 8) + per) // 8) * 8 for k in range(8))


def kernel(
    ny, di, dt,
    scale_ref, imgf_hbm, txtf_hbm, imgp_hbm, txtp_hbm,
    gip, gtp, gif, gtf,
    imgf, txtf, imgp, txtp,
    sqb, invr, own, img_all, zbuf, txt_all,
    psi, pst, gt_acc, col_acc, weight,
    cs_send, cs_recv, rs_mid, rs_recv, gx_send, gx_recv, ga_send, ga_recv,
    gr_own, gr_all, yi_send, yi_recv, yt_send, yt_recv,
    term_i, term_t, zi_send, zi_recv, zt_send, zt_recv,
    in_ss, sq_ss, sq_rs, pp_ss, pp_rs, ig_ss, fw_ss, ig_rs, za_ss, za_rs,
    tx_ss, tx_rs, cs_ss, cs_rs, ri_ss, ri_rs, gx_ss, gx_rs, ga_ss, ga_rs,
    gr_ss, gr_rs, yi_ss, yi_rs, yt_ss, yt_rs, zi_ss, zi_rs, zt_ss, zt_rs,
):
    n_blocks = ny * XL
    n_plane = n_blocks * T
    n_half = n_plane // 2
    na = Z // T
    batch = ny * Z * XL * ROWS
    dp = lax.axis_index("dp")
    t = lax.axis_index("tensor")
    core = t % 2
    xl = dp % XL
    z = (dp // XL) % Z
    y = dp // (XL * Z)
    b = y * XL + xl
    p = b * T + t
    h = p // 2
    xh = t // 2
    a = z // T
    c = z % T

    def plane_dev(q):
        block = q // T
        return (((block // XL) * Z + z) * XL + block % XL, q % T)

    def zt_dev(other, tensor):
        return ((y * Z + other) * XL + xl, tensor)

    def z_dev(other):
        return zt_dev(other, t)

    def t_dev(other):
        return (dp, other)

    sibling = (dp, t + 1 - 2 * core)

    def remote(src, dst, send, recv, dev):
        return pltpu.make_async_remote_copy(
            src_ref=src, dst_ref=dst, send_sem=send, recv_sem=recv,
            device_id=dev, device_id_type=pl.DeviceIdType.MESH,
        )

    barrier = pltpu.get_barrier_semaphore()

    def greet(dev):
        pl.semaphore_signal(barrier, inc=1, device_id=dev, device_id_type=pl.DeviceIdType.MESH)

    @pl.loop(1, Z)
    def _(i):
        greet(z_dev((z + i) % Z))

    loads = [
        pltpu.make_async_copy(src, dst, in_ss.at[k])
        for k, (src, dst) in enumerate(
            [(imgf_hbm, imgf), (imgp_hbm, imgp), (txtf_hbm, txtf), (txtp_hbm, txtp)]
        )
    ]
    for copy in loads:
        copy.start()

    for e in (1, 2, Z - 1, Z - 2):
        for i in range(1, T):
            greet(zt_dev((z + e) % Z, (t + i) % T))

    @pl.loop(1, n_plane)
    def _(i):
        greet(plane_dev((p + i) % n_plane))

    scale = scale_ref[0]
    coef = scale * (loss_factor / (2.0 * batch))

    loads[0].wait()
    loads[1].wait()
    raw_img = jnp.dot(imgf[...], imgp[...], preferred_element_type=f32)
    loads[2].wait()
    loads[3].wait()
    raw_txt = jnp.dot(txtf[...], txtp[...], preferred_element_type=f32)
    sqb[t] = rows_of(row_sums(raw_img * raw_img), row_sums(raw_txt * raw_txt))
    pl.semaphore_wait(barrier, n_plane - 1 + Z - 1 + 4 * (T - 1))

    def sq_copy(i):
        return remote(sqb.at[t], sqb.at[t], sq_ss.at[i - 1], sq_rs.at[t], t_dev((t + i) % T))

    for i in range(1, T):
        sq_copy(i).start()

    di4, dt4 = di // T, dt // T

    def pp_pair(i, src, first):
        other = (t + i) % T
        quarter = pl.ds(pl.multiple_of(src * Q, Q), Q)
        return (
            remote(
                imgp.at[pl.ds(pl.multiple_of(first * di4, 16), di4), :], psi.at[:, quarter],
                pp_ss.at[2 * i], pp_rs.at[2 * src], t_dev(other),
            ),
            remote(
                txtp.at[pl.ds(pl.multiple_of(first * dt4, 16), dt4), :], pst.at[:, quarter],
                pp_ss.at[2 * i + 1], pp_rs.at[2 * src + 1], t_dev(other),
            ),
        )

    def pp_copies(i):
        return pp_pair(i, t, (t + i) % T)

    for i in range(1, T):
        for copy in pp_copies(i):
            copy.start()
    own_pp = [
        pltpu.make_async_copy(
            ref.at[pl.ds(pl.multiple_of(t * size, 16), size), :],
            dst.at[:, pl.ds(pl.multiple_of(t * Q, Q), Q)], pp_ss.at[k],
        )
        for k, (ref, dst, size) in enumerate([(imgp, psi, di4), (txtp, pst, dt4)])
    ]
    for copy in own_pp:
        copy.start()

    for i in range(1, T):
        src = (t + i) % T
        remote(sqb.at[src], sqb.at[src], sq_ss.at[i - 1], sq_rs.at[src], t_dev(src)).wait_recv()
    square = (sqb[0] + sqb[1]) + (sqb[2] + sqb[3])
    inv = lax.rsqrt(square + eps)
    invr[...] = inv
    emb_txt = (raw_txt * as_columns(inv[1:2])).astype(bf16)
    own[1] = emb_txt
    zbuf[a] = emb_txt

    def img_slot(q):
        return img_all.at[
            pl.ds(pl.multiple_of((q // T) * ROWS, ROWS), ROWS),
            pl.ds(pl.multiple_of((q % T) * Q, Q), Q),
        ]

    def txt_slot(k, quarter):
        return txt_all.at[
            pl.ds(pl.multiple_of(k * ROWS, ROWS), ROWS),
            pl.ds(pl.multiple_of(quarter * Q, Q), Q),
        ]

    def za_copy(o):
        return remote(zbuf.at[a], zbuf.at[a], za_ss.at[o], za_rs.at[a], z_dev((z + T * o) % Z))

    def za_land(o):
        src = (a + o) % na
        return remote(zbuf.at[src], zbuf.at[src], za_ss.at[o], za_rs.at[src], z_dev((z + T * o) % Z))

    two = 2 - 4 * core

    def tx_copy(k, m):
        delta = (0, 1, two, -1)[m]
        return remote(
            zbuf.at[k], txt_slot(k, t), tx_ss.at[k * T + m], tx_rs.at[k * T + t],
            zt_dev((z - delta + Z) % Z, c),
        )

    def tx_local(k):
        return pltpu.make_async_copy(zbuf.at[k], txt_slot(k, t), tx_ss.at[k * T])

    def pass_on(k):
        for m in range(1, T):
            tx_copy(k, m).start()

        @pl.when(c != t)
        def _():
            tx_copy(k, 0).start()

        @pl.when(c == t)
        def _():
            tx_local(k).start()

    far_first = sorted(range(1, na), key=lambda o: -min(o, na - o))
    near_first = far_first[::-1]
    near_groups = [o for o in near_first if min(o, na - o) == 1]
    far_groups = [o for o in near_first if min(o, na - o) > 1]
    for o in far_groups:
        za_copy(o).start()

    emb_img = (raw_img * as_columns(inv[0:1])).astype(bf16)
    own[0] = emb_img
    own_img_copy = pltpu.make_async_copy(own.at[0], img_slot(p), in_ss.at[0])
    own_img_copy.start()

    def peer(n, flip):
        return ((b + n + n_blocks) % n_blocks) * 2 + xh + flip - 2 * xh * flip

    def ig_copy(i):
        dst = peer(-(i // 2), i % 2) * 2 + core
        return remote(own.at[0], img_slot(p), ig_ss.at[i], ig_rs.at[p], plane_dev(dst))

    def ig_land(i):
        q = peer(i // 2, i % 2) * 2 + core
        return remote(own.at[0], img_slot(q), ig_ss.at[i], ig_rs.at[q], plane_dev(q))

    def fw_copy(i):
        q = peer(i // 2, i % 2) * 2 + core
        return remote(img_slot(q), img_slot(q), fw_ss.at[i], ig_rs.at[q], sibling)

    def fw_land(i):
        q = peer(i // 2, i % 2) * 2 + 1 - core
        return remote(img_slot(q), img_slot(q), fw_ss.at[i], ig_rs.at[q], sibling)

    fw_own = remote(own.at[0], img_slot(p), fw_ss.at[0], ig_rs.at[p], sibling)

    @pl.loop(1, n_half)
    def _(i):
        ig_copy(i).start()

    fw_own.start()
    for o in near_groups:
        za_copy(o).start()
    pass_on(a)

    mine = (t - c + T) % T

    def delta_of(quarter):
        return jnp.where(
            mine == 0, 0, jnp.where(mine == 1, 1, jnp.where(mine == 3, -1, 2 - 4 * (quarter % 2)))
        )

    base = jnp.where(mine == 2, a, ((z + delta_of(0) + Z) % Z) // T)
    turn = jnp.where((mine == 2) & (c < T // 2), -1, 1)
    if na == 4:
        order = [base, (base + turn + na) % na, (base - turn + na) % na, (base + 2) % na]
    else:
        order = [(base + n) % na for n in range(na)]

    def keys_ready(k):
        for quarter in range(T):
            @pl.when((mine != 0) | (t != quarter))
            def _(quarter=quarter):
                remote(
                    zbuf.at[0], txt_slot(k, quarter), tx_ss.at[0],
                    tx_rs.at[k * T + quarter], sibling,
                ).wait_recv()

        @pl.when(c == t)
        def _():
            tx_local(k).wait()

    keys = na * ROWS
    col_acc[...] = jnp.zeros_like(col_acc)

    def fold(values):
        return sum(values[:, k * ROWS:(k + 1) * ROWS] for k in range(values.shape[1] // ROWS))

    def score(first, count, k):
        rows = img_all[pl.ds(pl.multiple_of(first, ROWS), count), :]
        cos = nt(rows, txt_all[pl.ds(pl.multiple_of(k * ROWS, ROWS), ROWS), :])
        expo = jnp.exp(scale * (cos - 1.0))
        i = lax.broadcasted_iota(jnp.int32, (count, ROWS), 0)
        j = lax.broadcasted_iota(jnp.int32, (count, ROWS), 1)
        mask = (j - i) == jnp.where((k == a) & (t == c), first - b * ROWS, ROWS)
        part = jnp.where(mask, 0.0, expo).astype(bf16)
        weight[
            pl.ds(pl.multiple_of(first, ROWS), count), pl.ds(pl.multiple_of(k * ROWS, ROWS), ROWS)
        ] = part
        none = jnp.zeros((1, ROWS), f32)
        col_acc[k] += rows_of(
            jnp.sum(part.astype(f32), axis=0, keepdims=True),
            jnp.sum(jnp.where(mask, expo, 0.0), axis=0, keepdims=True),
            none,
            jnp.sum(jnp.where(mask, cos, 0.0), axis=0, keepdims=True),
        )
        gt_acc[...] += tn(part, rows)

    def gx_copy(k, quarter):
        return remote(
            gx_send.at[k * T + quarter], gx_recv.at[k * T + mine], gx_ss.at[k * T + quarter],
            gx_rs.at[k * T + mine], zt_dev((z + delta_of(quarter) + Z) % Z, quarter),
        )

    def texts_out(k):
        total = gt_acc[...]
        rows = txt_all[pl.ds(pl.multiple_of(k * ROWS, ROWS), ROWS), :].astype(f32)
        none = jnp.zeros((1, ROWS), f32)
        sums = pack(col_acc[k] + rows_of(none, none, row_sums(fold(total * rows))))
        for quarter in range(T):
            gx_send[k * T + quarter, 0:ROWS, :] = total[:, quarter * Q:(quarter + 1) * Q].astype(bf16)
            gx_send[k * T + quarter, ROWS:PIECE, :] = sums

            @pl.when((mine != 0) | (t != quarter))
            def _(quarter=quarter):
                gx_copy(k, quarter).start()

    for o in near_groups:
        za_land(o).wait_recv()
        pass_on((a + o) % na)

    middle = n_half * 5 // 8

    @pl.loop(1, middle)
    def _(i):
        ig_land(i).wait_recv()
        fw_copy(i).start()

    for o in far_groups:
        za_land(o).wait_recv()
        pass_on((a + o) % na)

    @pl.loop(middle, n_half)
    def _(i):
        ig_land(i).wait_recv()
        fw_copy(i).start()

    own_img_copy.wait()

    @pl.loop(0, n_half)
    def _(i):
        fw_land(i).wait_recv()

    tall_rows = min(4, n_blocks) * ROWS
    for k in order:
        keys_ready(k)
        gt_acc[...] = jnp.zeros_like(gt_acc)

        @pl.loop(0, n_blocks * ROWS // tall_rows)
        def _(n, k=k):
            score(n * tall_rows, tall_rows, k)

        texts_out(k)

    def cs_copy(block):
        return remote(
            cs_send.at[pl.ds((1 - core) * n_half + block * 2, 2)],
            cs_recv.at[pl.ds(block * 2, 2)], cs_ss.at[block], cs_rs.at[block], sibling,
        )

    def rs_copy(k):
        return remote(
            rs_mid.at[k], rs_recv.at[h], ri_ss.at[k], ri_rs.at[h], plane_dev(k * 2 + core)
        )

    def both_cores(block):
        cs_copy(block).wait_recv()
        for part in range(2):
            k = block * 2 + part
            one = cs_send.at[core * n_half + k]
            other = cs_recv.at[k]
            rs_mid[k, 0:ROWS, :] = (
                one[0:ROWS, :].astype(f32) + other[0:ROWS, :].astype(f32)
            ).astype(bf16)
            rs_mid[k, ROWS:PIECE, :] = pack(unpack(one[ROWS:PIECE, :]) + unpack(other[ROWS:PIECE, :]))

            @pl.when(k != h)
            def _(k=k):
                rs_copy(k).start()

    @pl.loop(0, n_blocks)
    def _(n):
        block = (b + 1 + n) % n_blocks
        first = pl.ds(pl.multiple_of(block * ROWS, ROWS), ROWS)
        part = jnp.dot(weight[first, :], txt_all[...], preferred_element_type=f32)
        diag = jnp.where(block == b, col_acc[a], 0.0)
        sums = pack(
            rows_of(
                row_sums(fold(weight[first, :].astype(f32))), diag[1:2],
                row_sums(fold(part * img_all[first, :].astype(f32))), diag[3:4],
            )
        )
        for quarter in range(T):
            k = (quarter % 2) * n_half + block * 2 + quarter // 2
            cs_send[k, 0:ROWS, :] = part[:, quarter * Q:(quarter + 1) * Q].astype(bf16)
            cs_send[k, ROWS:PIECE, :] = sums
        cs_copy(block).start()

    def ga_copy(o):
        return remote(
            ga_send.at[o], ga_recv.at[a], ga_ss.at[o], ga_rs.at[a], z_dev((z + T * o) % Z)
        )

    def near_sum(o):
        k = (a + o) % na

        @pl.when(c == t)
        def _():
            gx_recv[k * T] = gx_send[k * T + t]

        for m in range(T):
            wait = remote(
                gx_send.at[0], gx_recv.at[k * T + m], gx_ss.at[0], gx_rs.at[k * T + m], sibling
            ).wait_recv
            if m == 0:
                pl.when(c != t)(wait)
            else:
                wait()
        total = sum(gx_recv[k * T + m, 0:ROWS, :].astype(f32) for m in range(T))
        ga_send[o, 0:ROWS, :] = total.astype(bf16)
        ga_send[o, ROWS:PIECE, :] = pack(
            sum(unpack(gx_recv[k * T + m, ROWS:PIECE, :]) for m in range(T))
        )

    @pl.loop(0, n_blocks)
    def _(n):
        both_cores((b + 1 + n) % n_blocks)

    for o in near_groups:
        near_sum(o)
        ga_copy(o).start()

    for o in far_groups:
        near_sum(o)
        ga_copy(o).start()
    near_sum(0)

    def raw_grad(total, sums, emb, target, inv_row):
        off, diag, inner, match = (sums[k:k + 1] for k in range(4))
        factor = coef / (off + diag) * inv_row
        align = inner - off * match
        return (
            as_columns(factor) * (total - as_columns(off) * target - as_columns(align) * emb)
        ).astype(bf16)

    def gr_copy(m, i):
        return remote(
            gr_own.at[m], gr_all.at[m, :, pl.ds(pl.multiple_of(t * Q, Q), Q)],
            gr_ss.at[m * T + i], gr_rs.at[m * T + t], t_dev((t + i) % T),
        )

    own_gr = [
        pltpu.make_async_copy(
            gr_own.at[m], gr_all.at[m, :, pl.ds(pl.multiple_of(t * Q, Q), Q)], gr_ss.at[m * T]
        )
        for m in range(2)
    ]

    diy, dty = di // ny, dt // ny
    per_i, per_t = diy // (Z * XL), dty // (Z * XL)
    win = window_of(per_i)
    pair = 2 if per_t % 16 else 1

    def img_rows(block, other):
        return (block // XL) * diy + ((other * XL + block % XL) * per_i) // 8 * 8

    def txt_rows(block, other):
        return (block // XL) * dty + (other * XL + block % XL) * per_t

    def yi_copy(i):
        dst = (b + i) % n_blocks
        return remote(
            yi_send.at[dst], yi_recv.at[b], yi_ss.at[i], yi_rs.at[b], plane_dev(dst * T + t)
        )

    def yt_copy(i):
        dst = (b + i) % n_blocks
        return remote(
            yt_send.at[dst], yt_recv.at[b], yt_ss.at[i], yt_rs.at[b], plane_dev(dst * T + t)
        )

    def terms(feat, grad, term):
        for k in range(0, feat.shape[1], 128):
            term[k:k + 128, :] = tn(feat[:, k:k + 128], grad)

    def img_begin(grad):
        gr_own[0] = grad
        terms(imgf, grad, term_i)
        for block in range(n_blocks):
            for other in range(Z):
                first = img_rows(block, other)
                yi_send[block, other] = term_i[first:first + win, :].astype(bf16)
        for i in range(1, n_blocks):
            yi_copy(i).start()

    def txt_begin(grad):
        gr_own[1] = grad
        terms(txtf, grad, term_t)
        for block in range(n_blocks):
            for group in range(Z // pair):
                rows = [
                    term_t[txt_rows(block, group * pair + n):txt_rows(block, group * pair + n) + per_t, :]
                    for n in range(pair)
                ]
                yt_send[block, group] = jnp.concatenate(rows, axis=0).astype(bf16)
        for i in range(1, n_blocks):
            yt_copy(i).start()

    def plane_sum(send, recv, ss, rs):
        total = send[b].astype(f32)
        for i in range(1, n_blocks):
            src = (b + i) % n_blocks
            remote(send.at[0], recv.at[src], ss.at[i], rs.at[src], sibling).wait_recv()
            total += recv[src].astype(f32)
        return total

    def rs_sum(i, carry):
        total, sums = carry
        src = (h + i) % n_half
        remote(
            rs_mid.at[0], rs_recv.at[src], ri_ss.at[0], ri_rs.at[src], sibling
        ).wait_recv()
        return (
            total + rs_recv[src, 0:ROWS, :].astype(f32),
            sums + unpack(rs_recv[src, ROWS:PIECE, :]),
        )

    total_img, sums_img = lax.fori_loop(
        1, n_half, rs_sum, (rs_mid[h, 0:ROWS, :].astype(f32), unpack(rs_mid[h, ROWS:PIECE, :]))
    )
    own_img = own[0].astype(f32)
    own_txt = own[1].astype(f32)
    img_begin(raw_grad(total_img, sums_img, own_img, own_txt, invr[0:1, :]))

    total_txt = ga_send[0, 0:ROWS, :].astype(f32)
    sums_txt = unpack(ga_send[0, ROWS:PIECE, :])
    for o in near_first:
        src = (a + o) % na
        remote(ga_send.at[0], ga_recv.at[src], ga_ss.at[o], ga_rs.at[src], sibling).wait_recv()
        total_txt += ga_recv[src, 0:ROWS, :].astype(f32)
        sums_txt += unpack(ga_recv[src, ROWS:PIECE, :])
    txt_begin(raw_grad(total_txt, sums_txt, own_txt, own_img, invr[1:2, :]))

    def zi_copy(i):
        dst = (z + i) % Z
        return remote(zi_send.at[dst], zi_recv.at[z], zi_ss.at[i], zi_rs.at[z], z_dev(dst))

    def zt_copy(i):
        dst = (z + i) % Z
        return remote(zt_send.at[dst], zt_recv.at[z], zt_ss.at[i], zt_rs.at[z], z_dev(dst))

    zi_send[...] = plane_sum(yi_send, yi_recv, yi_ss, yi_rs).astype(bf16)

    @pl.loop(0, Z)
    def _(n):
        i = (Z // 2 + n) % Z

        @pl.when(i > 0)
        def _():
            zi_copy(i).start()

    total = plane_sum(yt_send, yt_recv, yt_ss, yt_rs)
    for other in range(Z):
        first = other % pair * per_t
        rows = total[other // pair, first:first + per_t, :]
        zt_send[other] = jnp.concatenate([rows] * pair, axis=0).astype(bf16)

    @pl.loop(0, Z)
    def _(n):
        i = (Z // 2 + n) % Z

        @pl.when(i > 0)
        def _():
            zt_copy(i).start()

    for m in range(2):
        own_gr[m].start()
        for i in range(1, T):
            gr_copy(m, i).start()
    for m in range(2):
        own_gr[m].wait()
        own_pp[m].wait()
        for i in range(1, T):
            src = (t + i) % T
            remote(
                gr_own.at[m], gr_all.at[m, :, pl.ds(pl.multiple_of(src * Q, Q), Q)],
                gr_ss.at[m * T + i], gr_rs.at[m * T + src], t_dev(src),
            ).wait_recv()
    for i in range(1, T):
        for copy in pp_pair(i, (t + i) % T, 0):
            copy.wait_recv()
    gif[...] = nt(gr_all[0], psi[...])
    gtf[...] = nt(gr_all[1], pst[...])

    def zi_add(i, total):
        src = (z + i) % Z
        remote(zi_send.at[0], zi_recv.at[src], zi_ss.at[i], zi_rs.at[src], sibling).wait_recv()
        return total + zi_recv[src].astype(f32)

    total = lax.fori_loop(1, Z, zi_add, zi_send[z].astype(f32))
    shift = ((z * XL + xl) * per_i) % 8
    result = total[0:per_i]
    for k in sorted({(k * per_i) % 8 for k in range(8)} - {0}):
        result = jnp.where(shift == k, total[k:k + per_i], result)
    gip[...] = result

    def zt_add(i, total):
        src = (z + i) % Z
        remote(zt_send.at[0], zt_recv.at[src], zt_ss.at[i], zt_rs.at[src], sibling).wait_recv()
        return total + zt_recv[src, 0:per_t, :].astype(f32)

    gtp[...] = lax.fori_loop(1, Z, zt_add, zt_send[z, 0:per_t, :].astype(f32))

    for i in range(1, T):
        sq_copy(i).wait_send()
        for copy in pp_copies(i):
            copy.wait_send()
        for m in range(2):
            gr_copy(m, i).wait_send()
    for o in far_first:
        za_copy(o).wait_send()
        ga_copy(o).wait_send()
    fw_own.wait_send()

    @pl.loop(1, n_half)
    def _(i):
        ig_copy(i).wait_send()
        fw_copy(i).wait_send()
        rs_copy((h + i) % n_half).wait_send()

    @pl.loop(0, n_blocks)
    def _(block):
        cs_copy(block).wait_send()

    @pl.loop(0, na)
    def _(k):
        for m in range(1, T):
            tx_copy(k, m).wait_send()

        @pl.when(c != t)
        def _():
            tx_copy(k, 0).wait_send()

        for quarter in range(T):
            @pl.when((mine != 0) | (t != quarter))
            def _(quarter=quarter):
                gx_copy(k, quarter).wait_send()

    for i in range(1, n_blocks):
        yi_copy(i).wait_send()
        yt_copy(i).wait_send()

    @pl.loop(1, Z)
    def _(i):
        zi_copy(i).wait_send()
        zt_copy(i).wait_send()


def shards(ny, img_feat, txt_feat, img_proj, txt_proj, logit_scale):
    di, dt = img_feat.shape[1], txt_feat.shape[1]
    n_blocks = ny * XL
    n_plane = n_blocks * T
    n_half = n_plane // 2
    na = Z // T
    keys = na * ROWS
    emb = T * Q
    ndp = ny * Z * XL
    diy, dty = di // ny, dt // ny
    win = window_of(diy // (Z * XL))
    per_t = dty // (Z * XL)
    pair = 2 if per_t % 16 else 1
    tall = per_t * pair
    dma = pltpu.SemaphoreType.DMA
    vmem = pltpu.VMEM
    piece = (PIECE, Q)
    scratch = [
        vmem((ROWS, di), bf16),
        vmem((ROWS, dt), bf16),
        vmem((di, Q), bf16),
        vmem((dt, Q), bf16),
        vmem((T, 8, ROWS), f32),
        vmem((8, ROWS), f32),
        vmem((2, ROWS, Q), bf16),
        vmem((n_blocks * ROWS, emb), bf16),
        vmem((na, ROWS, Q), bf16),
        vmem((keys, emb), bf16),
        vmem((di // T, emb), bf16),
        vmem((dt // T, emb), bf16),
        vmem((ROWS, emb), f32),
        vmem((na, 8, ROWS), f32),
        vmem((n_blocks * ROWS, keys), bf16),
        vmem((n_plane, *piece), bf16),
        vmem((n_half, *piece), bf16),
        vmem((n_half, *piece), bf16),
        vmem((n_half, *piece), bf16),
        vmem((na * T, *piece), bf16),
        vmem((na * T, *piece), bf16),
        vmem((na, *piece), bf16),
        vmem((na, *piece), bf16),
        vmem((2, ROWS, Q), bf16),
        vmem((2, ROWS, emb), bf16),
        vmem((n_blocks, Z, win, Q), bf16),
        vmem((n_blocks, Z, win, Q), bf16),
        vmem((n_blocks, Z // pair, pair * per_t, Q), bf16),
        vmem((n_blocks, Z // pair, pair * per_t, Q), bf16),
        vmem((di, Q), f32),
        vmem((dt, Q), f32),
        vmem((Z, win, Q), bf16),
        vmem((Z, win, Q), bf16),
        vmem((Z, tall, Q), bf16),
        vmem((Z, tall, Q), bf16),
    ]
    wide = max(n_blocks, 2)
    sems = [
        4, T, T, 2 * T, 2 * T, n_half, n_half, n_plane, na, na,
        na * T, na * T, n_blocks, n_blocks, n_half, n_half, na * T, na * T, na, na,
        2 * T, 2 * T, wide, wide, wide, wide, Z, Z, Z, Z,
    ]
    scratch += [dma((n,)) for n in sems]
    whole = pl.BlockSpec(memory_space=pltpu.VMEM)
    return pl.pallas_call(
        functools.partial(kernel, ny, di, dt),
        out_shape=(
            jax.ShapeDtypeStruct((di // ndp, Q), f32),
            jax.ShapeDtypeStruct((dt // ndp, Q), f32),
            jax.ShapeDtypeStruct((ROWS, di // T), f32),
            jax.ShapeDtypeStruct((ROWS, dt // T), f32),
        ),
        in_specs=[pl.BlockSpec(memory_space=pltpu.SMEM)]
        + [pl.BlockSpec(memory_space=pl.ANY)] * 4,
        out_specs=(whole,) * 4,
        scratch_shapes=scratch,
        compiler_params=pltpu.CompilerParams(
            collective_id=0, has_side_effects=True, vmem_limit_bytes=56 * 1024 * 1024
        ),
    )(logit_scale, img_feat, txt_feat, img_proj, txt_proj)


def solution(mesh):
    ny = mesh.shape["dp"] // (Z * XL)
    return jax.shard_map(
        functools.partial(shards, ny),
        mesh=mesh,
        in_specs=(P("dp", None), P("dp", None), P(None, "tensor"), P(None, "tensor"), P()),
        out_specs=(P("dp", "tensor"), P("dp", "tensor"), P("dp", "tensor"), P("dp", "tensor")),
        check_vma=False,
    )
```

```python
import functools

import jax
import jax.numpy as jnp
from jax import lax
from jax.experimental import pallas as pl
from jax.experimental.pallas import tpu as pltpu
from jax.sharding import PartitionSpec as P

Z = 16
XL = 2
T = 4
ROWS = 128
Q = 128
SUMS = 16
PIECE = ROWS + SUMS
eps = 1e-06
loss_factor = 256.0
f32 = jnp.float32
bf16 = jnp.bfloat16


def nt(left, right):
    return lax.dot_general(left, right, (((1,), (1,)), ((), ())), preferred_element_type=f32)


def tn(left, right):
    return lax.dot_general(left, right, (((0,), (0,)), ((), ())), preferred_element_type=f32)


def row_sums(values):
    return jnp.sum(jnp.transpose(values), axis=0, keepdims=True)


def as_columns(row):
    return jnp.transpose(jnp.broadcast_to(row, (ROWS, ROWS)))


def rows_of(*rows):
    index = lax.broadcasted_iota(jnp.int32, (8, rows[0].shape[1]), 0)
    out = jnp.zeros((8, rows[0].shape[1]), f32)
    for k, row in enumerate(rows):
        out = jnp.where(index == k, row, out)
    return out


def pack(values):
    high = values.astype(bf16)
    return jnp.concatenate([high, (values - high.astype(f32)).astype(bf16)], axis=0)


def unpack(parts):
    parts = parts.astype(f32)
    return parts[0:8] + parts[8:16]


def window_of(per):
    return max(-(-(((k * per) % 8) + per) // 8) * 8 for k in range(8))


def kernel(
    ny, di, dt,
    scale_ref, imgf_hbm, txtf_hbm, imgp_hbm, txtp_hbm,
    gip, gtp, gif, gtf,
    imgf, txtf, imgp, txtp,
    sqb, invr, own, img_all, zbuf, txt_all,
    psi, pst, gt_acc, col_acc, weight,
    cs_send, cs_recv, rs_mid, rs_recv, gx_send, gx_recv, ga_send, ga_recv,
    gr_own, gr_all, yi_send, yi_recv, yt_send, yt_recv,
    term_i, term_t, back_i, back_t, zi_send, zi_recv, zt_send, zt_recv,
    in_ss, sq_ss, sq_rs, pp_ss, pp_rs, ig_ss, fw_ss, ig_rs, za_ss, za_rs,
    tx_ss, tx_rs, cs_ss, cs_rs, ri_ss, ri_rs, gx_ss, gx_rs, ga_ss, ga_rs,
    gr_ss, gr_rs, yi_ss, yi_rs, yt_ss, yt_rs, zi_ss, zi_rs, zt_ss, zt_rs,
):
    n_blocks = ny * XL
    n_plane = n_blocks * T
    n_half = n_plane // 2
    na = Z // T
    batch = ny * Z * XL * ROWS
    dp = lax.axis_index("dp")
    t = lax.axis_index("tensor")
    core = t % 2
    xl = dp % XL
    z = (dp // XL) % Z
    y = dp // (XL * Z)
    b = y * XL + xl
    p = b * T + t
    h = p // 2
    xh = t // 2
    a = z // T
    c = z % T

    def plane_dev(q):
        block = q // T
        return (((block // XL) * Z + z) * XL + block % XL, q % T)

    def zt_dev(other, tensor):
        return ((y * Z + other) * XL + xl, tensor)

    def z_dev(other):
        return zt_dev(other, t)

    def t_dev(other):
        return (dp, other)

    sibling = (dp, t + 1 - 2 * core)

    def remote(src, dst, send, recv, dev):
        return pltpu.make_async_remote_copy(
            src_ref=src, dst_ref=dst, send_sem=send, recv_sem=recv,
            device_id=dev, device_id_type=pl.DeviceIdType.MESH,
        )

    barrier = pltpu.get_barrier_semaphore()

    def greet(dev):
        pl.semaphore_signal(barrier, inc=1, device_id=dev, device_id_type=pl.DeviceIdType.MESH)

    @pl.loop(1, Z)
    def _(i):
        greet(z_dev((z + i) % Z))

    loads = [
        pltpu.make_async_copy(src, dst, in_ss.at[k])
        for k, (src, dst) in enumerate(
            [(imgf_hbm, imgf), (imgp_hbm, imgp), (txtf_hbm, txtf), (txtp_hbm, txtp)]
        )
    ]
    for copy in loads:
        copy.start()

    for e in (1, 2, Z - 1, Z - 2):
        for i in range(1, T):
            greet(zt_dev((z + e) % Z, (t + i) % T))

    @pl.loop(1, n_plane)
    def _(i):
        greet(plane_dev((p + i) % n_plane))

    scale = scale_ref[0]
    coef = scale * (loss_factor / (2.0 * batch))

    loads[0].wait()
    loads[1].wait()
    raw_img = jnp.dot(imgf[...], imgp[...], preferred_element_type=f32)
    loads[2].wait()
    loads[3].wait()
    raw_txt = jnp.dot(txtf[...], txtp[...], preferred_element_type=f32)
    sqb[t] = rows_of(row_sums(raw_img * raw_img), row_sums(raw_txt * raw_txt))
    pl.semaphore_wait(barrier, n_plane - 1 + Z - 1 + 4 * (T - 1))

    def sq_copy(i):
        return remote(sqb.at[t], sqb.at[t], sq_ss.at[i - 1], sq_rs.at[t], t_dev((t + i) % T))

    for i in range(1, T):
        sq_copy(i).start()

    di4, dt4 = di // T, dt // T

    def pp_pair(i, src, first):
        other = (t + i) % T
        quarter = pl.ds(pl.multiple_of(src * Q, Q), Q)
        return (
            remote(
                imgp.at[pl.ds(pl.multiple_of(first * di4, 16), di4), :], psi.at[:, quarter],
                pp_ss.at[2 * i], pp_rs.at[2 * src], t_dev(other),
            ),
            remote(
                txtp.at[pl.ds(pl.multiple_of(first * dt4, 16), dt4), :], pst.at[:, quarter],
                pp_ss.at[2 * i + 1], pp_rs.at[2 * src + 1], t_dev(other),
            ),
        )

    def pp_copies(i):
        return pp_pair(i, t, (t + i) % T)

    for i in range(1, T):
        for copy in pp_copies(i):
            copy.start()
    own_pp = [
        pltpu.make_async_copy(
            ref.at[pl.ds(pl.multiple_of(t * size, 16), size), :],
            dst.at[:, pl.ds(pl.multiple_of(t * Q, Q), Q)], pp_ss.at[k],
        )
        for k, (ref, dst, size) in enumerate([(imgp, psi, di4), (txtp, pst, dt4)])
    ]
    for copy in own_pp:
        copy.start()

    for i in range(1, T):
        src = (t + i) % T
        remote(sqb.at[src], sqb.at[src], sq_ss.at[i - 1], sq_rs.at[src], t_dev(src)).wait_recv()
    square = (sqb[0] + sqb[1]) + (sqb[2] + sqb[3])
    inv = lax.rsqrt(square + eps)
    invr[...] = inv
    emb_txt = (raw_txt * as_columns(inv[1:2])).astype(bf16)
    own[1] = emb_txt
    zbuf[a] = emb_txt

    def img_slot(q):
        return img_all.at[
            pl.ds(pl.multiple_of((q // T) * ROWS, ROWS), ROWS),
            pl.ds(pl.multiple_of((q % T) * Q, Q), Q),
        ]

    def txt_slot(k, quarter):
        return txt_all.at[
            pl.ds(pl.multiple_of(k * ROWS, ROWS), ROWS),
            pl.ds(pl.multiple_of(quarter * Q, Q), Q),
        ]

    def za_copy(o):
        return remote(zbuf.at[a], zbuf.at[a], za_ss.at[o], za_rs.at[a], z_dev((z + T * o) % Z))

    def za_land(o):
        src = (a + o) % na
        return remote(zbuf.at[src], zbuf.at[src], za_ss.at[o], za_rs.at[src], z_dev((z + T * o) % Z))

    two = 2 - 4 * core

    def tx_copy(k, m):
        delta = (0, 1, two, -1)[m]
        return remote(
            zbuf.at[k], txt_slot(k, t), tx_ss.at[k * T + m], tx_rs.at[k * T + t],
            zt_dev((z - delta + Z) % Z, c),
        )

    def tx_local(k):
        return pltpu.make_async_copy(zbuf.at[k], txt_slot(k, t), tx_ss.at[k * T])

    def pass_on(k):
        for m in range(1, T):
            tx_copy(k, m).start()

        @pl.when(c != t)
        def _():
            tx_copy(k, 0).start()

        @pl.when(c == t)
        def _():
            tx_local(k).start()

    far_first = sorted(range(1, na), key=lambda o: -min(o, na - o))
    near_first = far_first[::-1]
    near_groups = [o for o in near_first if min(o, na - o) == 1]
    far_groups = [o for o in near_first if min(o, na - o) > 1]
    for o in far_groups:
        za_copy(o).start()

    emb_img = (raw_img * as_columns(inv[0:1])).astype(bf16)
    own[0] = emb_img
    own_img_copy = pltpu.make_async_copy(own.at[0], img_slot(p), in_ss.at[0])
    own_img_copy.start()

    def peer(n, flip):
        return ((b + n + n_blocks) % n_blocks) * 2 + xh + flip - 2 * xh * flip

    def ig_copy(i):
        dst = peer(-(i // 2), i % 2) * 2 + core
        return remote(own.at[0], img_slot(p), ig_ss.at[i], ig_rs.at[p], plane_dev(dst))

    def ig_land(i):
        q = peer(i // 2, i % 2) * 2 + core
        return remote(own.at[0], img_slot(q), ig_ss.at[i], ig_rs.at[q], plane_dev(q))

    def fw_copy(i):
        q = peer(i // 2, i % 2) * 2 + core
        return remote(img_slot(q), img_slot(q), fw_ss.at[i], ig_rs.at[q], sibling)

    def fw_land(i):
        q = peer(i // 2, i % 2) * 2 + 1 - core
        return remote(img_slot(q), img_slot(q), fw_ss.at[i], ig_rs.at[q], sibling)

    fw_own = remote(own.at[0], img_slot(p), fw_ss.at[0], ig_rs.at[p], sibling)

    @pl.loop(1, n_half)
    def _(i):
        ig_copy(i).start()

    fw_own.start()
    for o in near_groups:
        za_copy(o).start()
    pass_on(a)

    mine = (t - c + T) % T

    def delta_of(quarter):
        return jnp.where(
            mine == 0, 0, jnp.where(mine == 1, 1, jnp.where(mine == 3, -1, 2 - 4 * (quarter % 2)))
        )

    base = jnp.where(mine == 2, a, ((z + delta_of(0) + Z) % Z) // T)
    turn = jnp.where((mine == 2) & (c < T // 2), -1, 1)
    if na == 4:
        order = [base, (base + turn + na) % na, (base - turn + na) % na, (base + 2) % na]
    else:
        order = [(base + n) % na for n in range(na)]

    def keys_ready(k):
        for quarter in range(T):
            @pl.when((mine != 0) | (t != quarter))
            def _(quarter=quarter):
                remote(
                    zbuf.at[0], txt_slot(k, quarter), tx_ss.at[0],
                    tx_rs.at[k * T + quarter], sibling,
                ).wait_recv()

        @pl.when(c == t)
        def _():
            tx_local(k).wait()

    keys = na * ROWS
    col_acc[...] = jnp.zeros_like(col_acc)

    def fold(values):
        return sum(values[:, k * ROWS:(k + 1) * ROWS] for k in range(values.shape[1] // ROWS))

    def score(first, count, k):
        rows = img_all[pl.ds(pl.multiple_of(first, ROWS), count), :]
        cos = nt(rows, txt_all[pl.ds(pl.multiple_of(k * ROWS, ROWS), ROWS), :])
        expo = jnp.exp(scale * (cos - 1.0))
        i = lax.broadcasted_iota(jnp.int32, (count, ROWS), 0)
        j = lax.broadcasted_iota(jnp.int32, (count, ROWS), 1)
        mask = (j - i) == jnp.where((k == a) & (t == c), first - b * ROWS, ROWS)
        part = jnp.where(mask, 0.0, expo).astype(bf16)
        weight[
            pl.ds(pl.multiple_of(first, ROWS), count), pl.ds(pl.multiple_of(k * ROWS, ROWS), ROWS)
        ] = part
        none = jnp.zeros((1, ROWS), f32)
        col_acc[k] += rows_of(
            jnp.sum(part.astype(f32), axis=0, keepdims=True),
            jnp.sum(jnp.where(mask, expo, 0.0), axis=0, keepdims=True),
            none,
            jnp.sum(jnp.where(mask, cos, 0.0), axis=0, keepdims=True),
        )
        gt_acc[...] += tn(part, rows)

    def gx_copy(k, quarter):
        return remote(
            gx_send.at[k * T + quarter], gx_recv.at[k * T + mine], gx_ss.at[k * T + quarter],
            gx_rs.at[k * T + mine], zt_dev((z + delta_of(quarter) + Z) % Z, quarter),
        )

    def texts_out(k):
        total = gt_acc[...]
        rows = txt_all[pl.ds(pl.multiple_of(k * ROWS, ROWS), ROWS), :].astype(f32)
        none = jnp.zeros((1, ROWS), f32)
        sums = pack(col_acc[k] + rows_of(none, none, row_sums(fold(total * rows))))
        for quarter in range(T):
            gx_send[k * T + quarter, 0:ROWS, :] = total[:, quarter * Q:(quarter + 1) * Q].astype(bf16)
            gx_send[k * T + quarter, ROWS:PIECE, :] = sums

            @pl.when((mine != 0) | (t != quarter))
            def _(quarter=quarter):
                gx_copy(k, quarter).start()

    for o in near_groups:
        za_land(o).wait_recv()
        pass_on((a + o) % na)

    middle = n_half * 5 // 8

    @pl.loop(1, middle)
    def _(i):
        ig_land(i).wait_recv()
        fw_copy(i).start()

    for o in far_groups:
        za_land(o).wait_recv()
        pass_on((a + o) % na)

    @pl.loop(middle, n_half)
    def _(i):
        ig_land(i).wait_recv()
        fw_copy(i).start()

    own_img_copy.wait()

    @pl.loop(0, n_half)
    def _(i):
        fw_land(i).wait_recv()

    tall_rows = min(4, n_blocks) * ROWS
    for k in order:
        keys_ready(k)
        gt_acc[...] = jnp.zeros_like(gt_acc)

        @pl.loop(0, n_blocks * ROWS // tall_rows)
        def _(n, k=k):
            score(n * tall_rows, tall_rows, k)

        texts_out(k)

    def cs_copy(block):
        return remote(
            cs_send.at[pl.ds((1 - core) * n_half + block * 2, 2)],
            cs_recv.at[pl.ds(block * 2, 2)], cs_ss.at[block], cs_rs.at[block], sibling,
        )

    def rs_copy(k):
        return remote(
            rs_mid.at[k], rs_recv.at[h], ri_ss.at[k], ri_rs.at[h], plane_dev(k * 2 + core)
        )

    def both_cores(block):
        cs_copy(block).wait_recv()
        for part in range(2):
            k = block * 2 + part
            one = cs_send.at[core * n_half + k]
            other = cs_recv.at[k]
            rs_mid[k, 0:ROWS, :] = (
                one[0:ROWS, :].astype(f32) + other[0:ROWS, :].astype(f32)
            ).astype(bf16)
            rs_mid[k, ROWS:PIECE, :] = pack(unpack(one[ROWS:PIECE, :]) + unpack(other[ROWS:PIECE, :]))

            @pl.when(k != h)
            def _(k=k):
                rs_copy(k).start()

    @pl.loop(0, n_blocks)
    def _(n):
        block = (b + 1 + n) % n_blocks
        first = pl.ds(pl.multiple_of(block * ROWS, ROWS), ROWS)
        part = jnp.dot(weight[first, :], txt_all[...], preferred_element_type=f32)
        diag = jnp.where(block == b, col_acc[a], 0.0)
        sums = pack(
            rows_of(
                row_sums(fold(weight[first, :].astype(f32))), diag[1:2],
                row_sums(fold(part * img_all[first, :].astype(f32))), diag[3:4],
            )
        )
        for quarter in range(T):
            k = (quarter % 2) * n_half + block * 2 + quarter // 2
            cs_send[k, 0:ROWS, :] = part[:, quarter * Q:(quarter + 1) * Q].astype(bf16)
            cs_send[k, ROWS:PIECE, :] = sums
        cs_copy(block).start()

    def ga_copy(o):
        return remote(
            ga_send.at[o], ga_recv.at[a], ga_ss.at[o], ga_rs.at[a], z_dev((z + T * o) % Z)
        )

    def near_sum(o):
        k = (a + o) % na

        @pl.when(c == t)
        def _():
            gx_recv[k * T] = gx_send[k * T + t]

        for m in range(T):
            wait = remote(
                gx_send.at[0], gx_recv.at[k * T + m], gx_ss.at[0], gx_rs.at[k * T + m], sibling
            ).wait_recv
            if m == 0:
                pl.when(c != t)(wait)
            else:
                wait()
        total = sum(gx_recv[k * T + m, 0:ROWS, :].astype(f32) for m in range(T))
        ga_send[o, 0:ROWS, :] = total.astype(bf16)
        ga_send[o, ROWS:PIECE, :] = pack(
            sum(unpack(gx_recv[k * T + m, ROWS:PIECE, :]) for m in range(T))
        )

    @pl.loop(0, n_blocks)
    def _(n):
        both_cores((b + 1 + n) % n_blocks)

    for o in near_groups:
        near_sum(o)
        ga_copy(o).start()

    for o in far_groups:
        near_sum(o)
        ga_copy(o).start()
    near_sum(0)

    def raw_grad(total, sums, emb, target, inv_row):
        off, diag, inner, match = (sums[k:k + 1] for k in range(4))
        factor = coef / (off + diag) * inv_row
        align = inner - off * match
        return (
            as_columns(factor) * (total - as_columns(off) * target - as_columns(align) * emb)
        ).astype(bf16)

    def gr_copy(m, i):
        return remote(
            gr_own.at[m], gr_all.at[m, :, pl.ds(pl.multiple_of(t * Q, Q), Q)],
            gr_ss.at[m * T + i], gr_rs.at[m * T + t], t_dev((t + i) % T),
        )

    own_gr = [
        pltpu.make_async_copy(
            gr_own.at[m], gr_all.at[m, :, pl.ds(pl.multiple_of(t * Q, Q), Q)], gr_ss.at[m * T]
        )
        for m in range(2)
    ]

    diy, dty = di // ny, dt // ny
    per_i, per_t = diy // (Z * XL), dty // (Z * XL)
    win = window_of(per_i)
    pair = 2 if per_t % 16 else 1

    def img_rows(block, other):
        return (block // XL) * diy + ((other * XL + block % XL) * per_i) // 8 * 8

    def txt_rows(block, other):
        return (block // XL) * dty + (other * XL + block % XL) * per_t

    def yi_copy(i):
        dst = (b + i) % n_blocks
        return remote(
            yi_send.at[dst], yi_recv.at[b], yi_ss.at[i], yi_rs.at[b], plane_dev(dst * T + t)
        )

    def yt_copy(i):
        dst = (b + i) % n_blocks
        return remote(
            yt_send.at[dst], yt_recv.at[b], yt_ss.at[i], yt_rs.at[b], plane_dev(dst * T + t)
        )

    def terms(feat, grad, term):
        for k in range(0, feat.shape[1], 128):
            term[k:k + 128, :] = tn(feat[:, k:k + 128], grad)

    def share_grad(m):
        own_gr[m].start()
        for i in range(1, T):
            gr_copy(m, i).start()

    def img_begin(grad):
        gr_own[0] = grad
        share_grad(0)
        terms(imgf, grad, term_i)
        for block in range(n_blocks):
            for other in range(Z):
                first = img_rows(block, other)
                yi_send[block, other] = term_i[first:first + win, :].astype(bf16)
        for i in range(1, n_blocks):
            yi_copy(i).start()

    def txt_begin(grad):
        gr_own[1] = grad
        share_grad(1)
        terms(txtf, grad, term_t)
        for block in range(n_blocks):
            for group in range(Z // pair):
                rows = [
                    term_t[txt_rows(block, group * pair + n):txt_rows(block, group * pair + n) + per_t, :]
                    for n in range(pair)
                ]
                yt_send[block, group] = jnp.concatenate(rows, axis=0).astype(bf16)
        for i in range(1, n_blocks):
            yt_copy(i).start()

    def plane_sum(send, recv, ss, rs):
        total = send[b].astype(f32)
        for i in range(1, n_blocks):
            src = (b + i) % n_blocks
            remote(send.at[0], recv.at[src], ss.at[i], rs.at[src], sibling).wait_recv()
            total += recv[src].astype(f32)
        return total

    def rs_sum(i, carry):
        total, sums = carry
        src = (h + i) % n_half
        remote(
            rs_mid.at[0], rs_recv.at[src], ri_ss.at[0], ri_rs.at[src], sibling
        ).wait_recv()
        return (
            total + rs_recv[src, 0:ROWS, :].astype(f32),
            sums + unpack(rs_recv[src, ROWS:PIECE, :]),
        )

    total_img, sums_img = lax.fori_loop(
        1, n_half, rs_sum, (rs_mid[h, 0:ROWS, :].astype(f32), unpack(rs_mid[h, ROWS:PIECE, :]))
    )
    own_img = own[0].astype(f32)
    own_txt = own[1].astype(f32)
    img_begin(raw_grad(total_img, sums_img, own_img, own_txt, invr[0:1, :]))

    total_txt = ga_send[0, 0:ROWS, :].astype(f32)
    sums_txt = unpack(ga_send[0, ROWS:PIECE, :])
    for o in near_first:
        src = (a + o) % na
        remote(ga_send.at[0], ga_recv.at[src], ga_ss.at[o], ga_rs.at[src], sibling).wait_recv()
        total_txt += ga_recv[src, 0:ROWS, :].astype(f32)
        sums_txt += unpack(ga_recv[src, ROWS:PIECE, :])
    txt_begin(raw_grad(total_txt, sums_txt, own_txt, own_img, invr[1:2, :]))

    def zi_copy(i):
        dst = (z + i) % Z
        return remote(zi_send.at[dst], zi_recv.at[z], zi_ss.at[i], zi_rs.at[z], z_dev(dst))

    def zt_copy(i):
        dst = (z + i) % Z
        return remote(zt_send.at[dst], zt_recv.at[z], zt_ss.at[i], zt_rs.at[z], z_dev(dst))

    def feature(m, back, rows, out):
        own_gr[m].wait()
        own_pp[m].wait()
        for i in range(1, T):
            src = (t + i) % T
            remote(
                gr_own.at[m], gr_all.at[m, :, pl.ds(pl.multiple_of(src * Q, Q), Q)],
                gr_ss.at[m * T + i], gr_rs.at[m * T + src], t_dev(src),
            ).wait_recv()
            pp_pair(i, src, 0)[m].wait_recv()
        back[...] = nt(gr_all[m], rows[...])
        copy = pltpu.make_async_copy(back, out, in_ss.at[m])
        copy.start()
        return copy

    feature_out = [feature(0, back_i, psi, gif)]
    zi_send[...] = plane_sum(yi_send, yi_recv, yi_ss, yi_rs).astype(bf16)

    @pl.loop(0, Z)
    def _(n):
        i = (Z // 2 + n) % Z

        @pl.when(i > 0)
        def _():
            zi_copy(i).start()

    feature_out.append(feature(1, back_t, pst, gtf))

    for i in range(1, T):
        sq_copy(i).wait_send()
        for copy in pp_copies(i):
            copy.wait_send()
        for m in range(2):
            gr_copy(m, i).wait_send()
    for o in far_first:
        za_copy(o).wait_send()
        ga_copy(o).wait_send()
    fw_own.wait_send()

    @pl.loop(1, n_half)
    def _(i):
        ig_copy(i).wait_send()
        fw_copy(i).wait_send()
        rs_copy((h + i) % n_half).wait_send()

    @pl.loop(0, n_blocks)
    def _(block):
        cs_copy(block).wait_send()

    @pl.loop(0, na)
    def _(k):
        for m in range(1, T):
            tx_copy(k, m).wait_send()

        @pl.when(c != t)
        def _():
            tx_copy(k, 0).wait_send()

        for quarter in range(T):
            @pl.when((mine != 0) | (t != quarter))
            def _(quarter=quarter):
                gx_copy(k, quarter).wait_send()

    total = plane_sum(yt_send, yt_recv, yt_ss, yt_rs)
    for other in range(Z):
        first = other % pair * per_t
        rows = total[other // pair, first:first + per_t, :]
        zt_send[other] = jnp.concatenate([rows] * pair, axis=0).astype(bf16)

    @pl.loop(0, Z)
    def _(n):
        i = (Z // 2 + n) % Z

        @pl.when(i > 0)
        def _():
            zt_copy(i).start()

    for i in range(1, n_blocks):
        yi_copy(i).wait_send()
        yt_copy(i).wait_send()

    def zi_add(i, total):
        src = (z + i) % Z
        remote(zi_send.at[0], zi_recv.at[src], zi_ss.at[i], zi_rs.at[src], sibling).wait_recv()
        return total + zi_recv[src].astype(f32)

    total = lax.fori_loop(1, Z, zi_add, zi_send[z].astype(f32))
    shift = ((z * XL + xl) * per_i) % 8
    result = total[0:per_i]
    for k in sorted({(k * per_i) % 8 for k in range(8)} - {0}):
        result = jnp.where(shift == k, total[k:k + per_i], result)
    gip[...] = result

    def zt_add(i, total):
        src = (z + i) % Z
        remote(zt_send.at[0], zt_recv.at[src], zt_ss.at[i], zt_rs.at[src], sibling).wait_recv()
        return total + zt_recv[src, 0:per_t, :].astype(f32)

    gtp[...] = lax.fori_loop(1, Z, zt_add, zt_send[z, 0:per_t, :].astype(f32))

    @pl.loop(1, Z)
    def _(i):
        zi_copy(i).wait_send()
        zt_copy(i).wait_send()
    for copy in feature_out:
        copy.wait()


def shards(ny, img_feat, txt_feat, img_proj, txt_proj, logit_scale):
    di, dt = img_feat.shape[1], txt_feat.shape[1]
    n_blocks = ny * XL
    n_plane = n_blocks * T
    n_half = n_plane // 2
    na = Z // T
    keys = na * ROWS
    emb = T * Q
    ndp = ny * Z * XL
    diy, dty = di // ny, dt // ny
    win = window_of(diy // (Z * XL))
    per_t = dty // (Z * XL)
    pair = 2 if per_t % 16 else 1
    tall = per_t * pair
    dma = pltpu.SemaphoreType.DMA
    vmem = pltpu.VMEM
    piece = (PIECE, Q)
    scratch = [
        vmem((ROWS, di), bf16),
        vmem((ROWS, dt), bf16),
        vmem((di, Q), bf16),
        vmem((dt, Q), bf16),
        vmem((T, 8, ROWS), f32),
        vmem((8, ROWS), f32),
        vmem((2, ROWS, Q), bf16),
        vmem((n_blocks * ROWS, emb), bf16),
        vmem((na, ROWS, Q), bf16),
        vmem((keys, emb), bf16),
        vmem((di // T, emb), bf16),
        vmem((dt // T, emb), bf16),
        vmem((ROWS, emb), f32),
        vmem((na, 8, ROWS), f32),
        vmem((n_blocks * ROWS, keys), bf16),
        vmem((n_plane, *piece), bf16),
        vmem((n_half, *piece), bf16),
        vmem((n_half, *piece), bf16),
        vmem((n_half, *piece), bf16),
        vmem((na * T, *piece), bf16),
        vmem((na * T, *piece), bf16),
        vmem((na, *piece), bf16),
        vmem((na, *piece), bf16),
        vmem((2, ROWS, Q), bf16),
        vmem((2, ROWS, emb), bf16),
        vmem((n_blocks, Z, win, Q), bf16),
        vmem((n_blocks, Z, win, Q), bf16),
        vmem((n_blocks, Z // pair, pair * per_t, Q), bf16),
        vmem((n_blocks, Z // pair, pair * per_t, Q), bf16),
        vmem((di, Q), f32),
        vmem((dt, Q), f32),
        vmem((ROWS, di // T), f32),
        vmem((ROWS, dt // T), f32),
        vmem((Z, win, Q), bf16),
        vmem((Z, win, Q), bf16),
        vmem((Z, tall, Q), bf16),
        vmem((Z, tall, Q), bf16),
    ]
    wide = max(n_blocks, 2)
    sems = [
        4, T, T, 2 * T, 2 * T, n_half, n_half, n_plane, na, na,
        na * T, na * T, n_blocks, n_blocks, n_half, n_half, na * T, na * T, na, na,
        2 * T, 2 * T, wide, wide, wide, wide, Z, Z, Z, Z,
    ]
    scratch += [dma((n,)) for n in sems]
    whole = pl.BlockSpec(memory_space=pltpu.VMEM)
    return pl.pallas_call(
        functools.partial(kernel, ny, di, dt),
        out_shape=(
            jax.ShapeDtypeStruct((di // ndp, Q), f32),
            jax.ShapeDtypeStruct((dt // ndp, Q), f32),
            jax.ShapeDtypeStruct((ROWS, di // T), f32),
            jax.ShapeDtypeStruct((ROWS, dt // T), f32),
        ),
        in_specs=[pl.BlockSpec(memory_space=pltpu.SMEM)]
        + [pl.BlockSpec(memory_space=pl.ANY)] * 4,
        out_specs=(whole, whole) + (pl.BlockSpec(memory_space=pl.ANY),) * 2,
        scratch_shapes=scratch,
        compiler_params=pltpu.CompilerParams(
            collective_id=0, has_side_effects=True, vmem_limit_bytes=56 * 1024 * 1024
        ),
    )(logit_scale, img_feat, txt_feat, img_proj, txt_proj)


def solution(mesh):
    ny = mesh.shape["dp"] // (Z * XL)
    return jax.shard_map(
        functools.partial(shards, ny),
        mesh=mesh,
        in_specs=(P("dp", None), P("dp", None), P(None, "tensor"), P(None, "tensor"), P()),
        out_specs=(P("dp", "tensor"), P("dp", "tensor"), P("dp", "tensor"), P("dp", "tensor")),
        check_vma=False,
    )
```

```python
import functools

import jax
import jax.numpy as jnp
from jax import lax
from jax.experimental import pallas as pl
from jax.experimental.pallas import tpu as pltpu
from jax.sharding import PartitionSpec as P

Z = 16
XL = 2
T = 4
ROWS = 128
Q = 128
SUMS = 16
PIECE = ROWS + SUMS
eps = 1e-06
loss_factor = 256.0
f32 = jnp.float32
bf16 = jnp.bfloat16


def nt(left, right):
    return lax.dot_general(left, right, (((1,), (1,)), ((), ())), preferred_element_type=f32)


def tn(left, right):
    return lax.dot_general(left, right, (((0,), (0,)), ((), ())), preferred_element_type=f32)


def row_sums(values):
    return jnp.sum(jnp.transpose(values), axis=0, keepdims=True)


def as_columns(row):
    return jnp.transpose(jnp.broadcast_to(row, (ROWS, ROWS)))


def rows_of(*rows):
    index = lax.broadcasted_iota(jnp.int32, (8, rows[0].shape[1]), 0)
    out = jnp.zeros((8, rows[0].shape[1]), f32)
    for k, row in enumerate(rows):
        out = jnp.where(index == k, row, out)
    return out


def pack(values):
    high = values.astype(bf16)
    return jnp.concatenate([high, (values - high.astype(f32)).astype(bf16)], axis=0)


def unpack(parts):
    parts = parts.astype(f32)
    return parts[0:8] + parts[8:16]


def window_of(per):
    return max(-(-(((k * per) % 8) + per) // 8) * 8 for k in range(8))


def kernel(
    ny, di, dt,
    scale_ref, imgf_hbm, txtf_hbm, imgp_hbm, txtp_hbm,
    gip, gtp, gif, gtf,
    imgf, txtf, imgp, txtp,
    sqb, invr, own, img_all, zbuf, txt_all,
    psi, pst, gt_acc, col_acc, weight,
    cs_send, cs_recv, rs_mid, rs_recv, gx_send, gx_recv, ga_send, ga_recv,
    gr_own, gr_all, yi_send, yi_recv, yt_send, yt_recv,
    term_i, term_t, back_i, back_t, zi_send, zi_recv, zt_send, zt_recv,
    in_ss, sq_ss, sq_rs, pp_ss, pp_rs, ig_ss, fw_ss, ig_rs, za_ss, za_rs,
    tx_ss, tx_rs, cs_ss, cs_rs, ri_ss, ri_rs, gx_ss, gx_rs, ga_ss, ga_rs,
    gr_ss, gr_rs, yi_ss, yi_rs, yt_ss, yt_rs, zi_ss, zi_rs, zt_ss, zt_rs,
):
    n_blocks = ny * XL
    n_plane = n_blocks * T
    n_half = n_plane // 2
    na = Z // T
    batch = ny * Z * XL * ROWS
    dp = lax.axis_index("dp")
    t = lax.axis_index("tensor")
    core = t % 2
    xl = dp % XL
    z = (dp // XL) % Z
    y = dp // (XL * Z)
    b = y * XL + xl
    p = b * T + t
    h = p // 2
    xh = t // 2
    a = z // T
    c = z % T

    def plane_dev(q):
        block = q // T
        return (((block // XL) * Z + z) * XL + block % XL, q % T)

    def zt_dev(other, tensor):
        return ((y * Z + other) * XL + xl, tensor)

    def z_dev(other):
        return zt_dev(other, t)

    def t_dev(other):
        return (dp, other)

    sibling = (dp, t + 1 - 2 * core)

    def remote(src, dst, send, recv, dev):
        return pltpu.make_async_remote_copy(
            src_ref=src, dst_ref=dst, send_sem=send, recv_sem=recv,
            device_id=dev, device_id_type=pl.DeviceIdType.MESH,
        )

    barrier = pltpu.get_barrier_semaphore()

    def greet(dev):
        pl.semaphore_signal(barrier, inc=1, device_id=dev, device_id_type=pl.DeviceIdType.MESH)

    @pl.loop(1, Z)
    def _(i):
        greet(z_dev((z + i) % Z))

    loads = [
        pltpu.make_async_copy(src, dst, in_ss.at[k])
        for k, (src, dst) in enumerate(
            [(imgf_hbm, imgf), (imgp_hbm, imgp), (txtf_hbm, txtf), (txtp_hbm, txtp)]
        )
    ]
    for copy in loads:
        copy.start()

    for e in (1, 2, Z - 1, Z - 2):
        for i in range(1, T):
            greet(zt_dev((z + e) % Z, (t + i) % T))

    @pl.loop(1, n_plane)
    def _(i):
        greet(plane_dev((p + i) % n_plane))

    scale = scale_ref[0]
    coef = scale * (loss_factor / (2.0 * batch))

    loads[0].wait()
    loads[1].wait()
    raw_img = jnp.dot(imgf[...], imgp[...], preferred_element_type=f32)
    loads[2].wait()
    loads[3].wait()
    raw_txt = jnp.dot(txtf[...], txtp[...], preferred_element_type=f32)
    sqb[t] = rows_of(row_sums(raw_img * raw_img), row_sums(raw_txt * raw_txt))
    pl.semaphore_wait(barrier, n_plane - 1 + Z - 1 + 4 * (T - 1))

    def sq_copy(i):
        return remote(sqb.at[t], sqb.at[t], sq_ss.at[i - 1], sq_rs.at[t], t_dev((t + i) % T))

    for i in range(1, T):
        sq_copy(i).start()

    di4, dt4 = di // T, dt // T

    def pp_pair(i, src, first):
        other = (t + i) % T
        quarter = pl.ds(pl.multiple_of(src * Q, Q), Q)
        return (
            remote(
                imgp.at[pl.ds(pl.multiple_of(first * di4, 16), di4), :], psi.at[:, quarter],
                pp_ss.at[2 * i], pp_rs.at[2 * src], t_dev(other),
            ),
            remote(
                txtp.at[pl.ds(pl.multiple_of(first * dt4, 16), dt4), :], pst.at[:, quarter],
                pp_ss.at[2 * i + 1], pp_rs.at[2 * src + 1], t_dev(other),
            ),
        )

    def pp_copies(i):
        return pp_pair(i, t, (t + i) % T)

    for i in range(1, T):
        for copy in pp_copies(i):
            copy.start()
    own_pp = [
        pltpu.make_async_copy(
            ref.at[pl.ds(pl.multiple_of(t * size, 16), size), :],
            dst.at[:, pl.ds(pl.multiple_of(t * Q, Q), Q)], pp_ss.at[k],
        )
        for k, (ref, dst, size) in enumerate([(imgp, psi, di4), (txtp, pst, dt4)])
    ]
    for copy in own_pp:
        copy.start()

    for i in range(1, T):
        src = (t + i) % T
        remote(sqb.at[src], sqb.at[src], sq_ss.at[i - 1], sq_rs.at[src], t_dev(src)).wait_recv()
    square = (sqb[0] + sqb[1]) + (sqb[2] + sqb[3])
    inv = lax.rsqrt(square + eps)
    invr[...] = inv
    emb_txt = (raw_txt * as_columns(inv[1:2])).astype(bf16)
    own[1] = emb_txt
    zbuf[a] = emb_txt

    def img_slot(q):
        return img_all.at[
            pl.ds(pl.multiple_of((q // T) * ROWS, ROWS), ROWS),
            pl.ds(pl.multiple_of((q % T) * Q, Q), Q),
        ]

    def txt_slot(k, quarter):
        return txt_all.at[
            pl.ds(pl.multiple_of(k * ROWS, ROWS), ROWS),
            pl.ds(pl.multiple_of(quarter * Q, Q), Q),
        ]

    def za_copy(o):
        return remote(zbuf.at[a], zbuf.at[a], za_ss.at[o], za_rs.at[a], z_dev((z + T * o) % Z))

    def za_land(o):
        src = (a + o) % na
        return remote(zbuf.at[src], zbuf.at[src], za_ss.at[o], za_rs.at[src], z_dev((z + T * o) % Z))

    two = 2 - 4 * core

    def tx_copy(k, m):
        delta = (0, 1, two, -1)[m]
        return remote(
            zbuf.at[k], txt_slot(k, t), tx_ss.at[k * T + m], tx_rs.at[k * T + t],
            zt_dev((z - delta + Z) % Z, c),
        )

    def tx_local(k):
        return pltpu.make_async_copy(zbuf.at[k], txt_slot(k, t), tx_ss.at[k * T])

    def pass_on(k):
        for m in range(1, T):
            tx_copy(k, m).start()

        @pl.when(c != t)
        def _():
            tx_copy(k, 0).start()

        @pl.when(c == t)
        def _():
            tx_local(k).start()

    far_first = sorted(range(1, na), key=lambda o: -min(o, na - o))
    near_first = far_first[::-1]
    near_groups = [o for o in near_first if min(o, na - o) == 1]
    far_groups = [o for o in near_first if min(o, na - o) > 1]
    for o in far_groups:
        za_copy(o).start()

    emb_img = (raw_img * as_columns(inv[0:1])).astype(bf16)
    own[0] = emb_img
    own_img_copy = pltpu.make_async_copy(own.at[0], img_slot(p), in_ss.at[0])
    own_img_copy.start()

    def peer(n, flip):
        return ((b + n + n_blocks) % n_blocks) * 2 + xh + flip - 2 * xh * flip

    def ig_copy(i):
        dst = peer(-(i // 2), i % 2) * 2 + core
        return remote(own.at[0], img_slot(p), ig_ss.at[i], ig_rs.at[p], plane_dev(dst))

    def ig_land(i):
        q = peer(i // 2, i % 2) * 2 + core
        return remote(own.at[0], img_slot(q), ig_ss.at[i], ig_rs.at[q], plane_dev(q))

    def fw_copy(i):
        q = peer(i // 2, i % 2) * 2 + core
        return remote(img_slot(q), img_slot(q), fw_ss.at[i], ig_rs.at[q], sibling)

    def fw_land(i):
        q = peer(i // 2, i % 2) * 2 + 1 - core
        return remote(img_slot(q), img_slot(q), fw_ss.at[i], ig_rs.at[q], sibling)

    fw_own = remote(own.at[0], img_slot(p), fw_ss.at[0], ig_rs.at[p], sibling)

    @pl.loop(1, n_half)
    def _(i):
        ig_copy(i).start()

    fw_own.start()
    for o in near_groups:
        za_copy(o).start()
    pass_on(a)

    mine = (t - c + T) % T

    def delta_of(quarter):
        return jnp.where(
            mine == 0, 0, jnp.where(mine == 1, 1, jnp.where(mine == 3, -1, 2 - 4 * (quarter % 2)))
        )

    base = jnp.where(mine == 2, a, ((z + delta_of(0) + Z) % Z) // T)
    turn = jnp.where((mine == 2) & (c < T // 2), -1, 1)
    if na == 4:
        order = [base, (base + turn + na) % na, (base - turn + na) % na, (base + 2) % na]
    else:
        order = [(base + n) % na for n in range(na)]

    def keys_ready(k):
        for quarter in range(T):
            @pl.when((mine != 0) | (t != quarter))
            def _(quarter=quarter):
                remote(
                    zbuf.at[0], txt_slot(k, quarter), tx_ss.at[0],
                    tx_rs.at[k * T + quarter], sibling,
                ).wait_recv()

        @pl.when(c == t)
        def _():
            tx_local(k).wait()

    keys = na * ROWS
    col_acc[...] = jnp.zeros_like(col_acc)

    def fold(values):
        return sum(values[:, k * ROWS:(k + 1) * ROWS] for k in range(values.shape[1] // ROWS))

    def score(first, count, k):
        rows = img_all[pl.ds(pl.multiple_of(first, ROWS), count), :]
        cos = nt(rows, txt_all[pl.ds(pl.multiple_of(k * ROWS, ROWS), ROWS), :])
        expo = jnp.exp(scale * (cos - 1.0))
        i = lax.broadcasted_iota(jnp.int32, (count, ROWS), 0)
        j = lax.broadcasted_iota(jnp.int32, (count, ROWS), 1)
        mask = (j - i) == jnp.where((k == a) & (t == c), first - b * ROWS, ROWS)
        part = jnp.where(mask, 0.0, expo).astype(bf16)
        weight[
            pl.ds(pl.multiple_of(first, ROWS), count), pl.ds(pl.multiple_of(k * ROWS, ROWS), ROWS)
        ] = part
        none = jnp.zeros((1, ROWS), f32)
        col_acc[k] += rows_of(
            jnp.sum(part.astype(f32), axis=0, keepdims=True),
            jnp.sum(jnp.where(mask, expo, 0.0), axis=0, keepdims=True),
            none,
            jnp.sum(jnp.where(mask, cos, 0.0), axis=0, keepdims=True),
        )
        gt_acc[...] += tn(part, rows)

    def gx_copy(k, quarter):
        return remote(
            gx_send.at[k * T + quarter], gx_recv.at[k * T + mine], gx_ss.at[k * T + quarter],
            gx_rs.at[k * T + mine], zt_dev((z + delta_of(quarter) + Z) % Z, quarter),
        )

    def texts_out(k):
        total = gt_acc[...]
        rows = txt_all[pl.ds(pl.multiple_of(k * ROWS, ROWS), ROWS), :].astype(f32)
        none = jnp.zeros((1, ROWS), f32)
        sums = pack(col_acc[k] + rows_of(none, none, row_sums(fold(total * rows))))
        for quarter in range(T):
            gx_send[k * T + quarter, 0:ROWS, :] = total[:, quarter * Q:(quarter + 1) * Q].astype(bf16)
            gx_send[k * T + quarter, ROWS:PIECE, :] = sums

            @pl.when((mine != 0) | (t != quarter))
            def _(quarter=quarter):
                gx_copy(k, quarter).start()

    for o in near_groups:
        za_land(o).wait_recv()
        pass_on((a + o) % na)

    middle = n_half * 5 // 8

    @pl.loop(1, middle)
    def _(i):
        ig_land(i).wait_recv()
        fw_copy(i).start()

    for o in far_groups:
        za_land(o).wait_recv()
        pass_on((a + o) % na)

    @pl.loop(middle, n_half)
    def _(i):
        ig_land(i).wait_recv()
        fw_copy(i).start()

    own_img_copy.wait()

    @pl.loop(0, n_half)
    def _(i):
        fw_land(i).wait_recv()

    tall_rows = min(4, n_blocks) * ROWS
    for k in order:
        keys_ready(k)
        gt_acc[...] = jnp.zeros_like(gt_acc)

        @pl.loop(0, n_blocks * ROWS // tall_rows)
        def _(n, k=k):
            score(n * tall_rows, tall_rows, k)

        texts_out(k)

    def cs_copy(block):
        return remote(
            cs_send.at[pl.ds((1 - core) * n_half + block * 2, 2)],
            cs_recv.at[pl.ds(block * 2, 2)], cs_ss.at[block], cs_rs.at[block], sibling,
        )

    def rs_copy(k):
        return remote(
            rs_mid.at[k], rs_recv.at[h], ri_ss.at[k], ri_rs.at[h], plane_dev(k * 2 + core)
        )

    def both_cores(block):
        cs_copy(block).wait_recv()
        for part in range(2):
            k = block * 2 + part
            one = cs_send.at[core * n_half + k]
            other = cs_recv.at[k]
            rs_mid[k, 0:ROWS, :] = (
                one[0:ROWS, :].astype(f32) + other[0:ROWS, :].astype(f32)
            ).astype(bf16)
            rs_mid[k, ROWS:PIECE, :] = pack(unpack(one[ROWS:PIECE, :]) + unpack(other[ROWS:PIECE, :]))

            @pl.when(k != h)
            def _(k=k):
                rs_copy(k).start()

    @pl.loop(0, n_blocks)
    def _(n):
        block = (b + 1 + n) % n_blocks
        first = pl.ds(pl.multiple_of(block * ROWS, ROWS), ROWS)
        part = jnp.dot(weight[first, :], txt_all[...], preferred_element_type=f32)
        diag = jnp.where(block == b, col_acc[a], 0.0)
        sums = pack(
            rows_of(
                row_sums(fold(weight[first, :].astype(f32))), diag[1:2],
                row_sums(fold(part * img_all[first, :].astype(f32))), diag[3:4],
            )
        )
        for quarter in range(T):
            k = (quarter % 2) * n_half + block * 2 + quarter // 2
            cs_send[k, 0:ROWS, :] = part[:, quarter * Q:(quarter + 1) * Q].astype(bf16)
            cs_send[k, ROWS:PIECE, :] = sums
        cs_copy(block).start()

    def ga_copy(o):
        return remote(
            ga_send.at[o], ga_recv.at[a], ga_ss.at[o], ga_rs.at[a], z_dev((z + T * o) % Z)
        )

    def near_sum(o):
        k = (a + o) % na

        @pl.when(c == t)
        def _():
            gx_recv[k * T] = gx_send[k * T + t]

        for m in range(T):
            wait = remote(
                gx_send.at[0], gx_recv.at[k * T + m], gx_ss.at[0], gx_rs.at[k * T + m], sibling
            ).wait_recv
            if m == 0:
                pl.when(c != t)(wait)
            else:
                wait()
        total = sum(gx_recv[k * T + m, 0:ROWS, :].astype(f32) for m in range(T))
        ga_send[o, 0:ROWS, :] = total.astype(bf16)
        ga_send[o, ROWS:PIECE, :] = pack(
            sum(unpack(gx_recv[k * T + m, ROWS:PIECE, :]) for m in range(T))
        )

    @pl.loop(0, n_blocks)
    def _(n):
        both_cores((b + 1 + n) % n_blocks)

    for o in near_groups:
        near_sum(o)
        ga_copy(o).start()

    for o in far_groups:
        near_sum(o)
        ga_copy(o).start()
    near_sum(0)

    def raw_grad(total, sums, emb, target, inv_row):
        off, diag, inner, match = (sums[k:k + 1] for k in range(4))
        factor = coef / (off + diag) * inv_row
        align = inner - off * match
        return (
            as_columns(factor) * (total - as_columns(off) * target - as_columns(align) * emb)
        ).astype(bf16)

    def gr_copy(m, i):
        return remote(
            gr_own.at[m], gr_all.at[m, :, pl.ds(pl.multiple_of(t * Q, Q), Q)],
            gr_ss.at[m * T + i], gr_rs.at[m * T + t], t_dev((t + i) % T),
        )

    own_gr = [
        pltpu.make_async_copy(
            gr_own.at[m], gr_all.at[m, :, pl.ds(pl.multiple_of(t * Q, Q), Q)], gr_ss.at[m * T]
        )
        for m in range(2)
    ]

    diy, dty = di // ny, dt // ny
    per_i, per_t = diy // (Z * XL), dty // (Z * XL)
    win = window_of(per_i)
    pair = 2 if per_t % 16 else 1

    def img_rows(block, other):
        return (block // XL) * diy + ((other * XL + block % XL) * per_i) // 8 * 8

    def txt_rows(block, other):
        return (block // XL) * dty + (other * XL + block % XL) * per_t

    def yi_copy(i):
        dst = (b + i) % n_blocks
        return remote(
            yi_send.at[dst], yi_recv.at[b], yi_ss.at[i], yi_rs.at[b], plane_dev(dst * T + t)
        )

    def yt_copy(i):
        dst = (b + i) % n_blocks
        return remote(
            yt_send.at[dst], yt_recv.at[b], yt_ss.at[i], yt_rs.at[b], plane_dev(dst * T + t)
        )

    def terms(feat, grad, term):
        for k in range(0, feat.shape[1], 128):
            term[k:k + 128, :] = tn(feat[:, k:k + 128], grad)

    def share_grad(m):
        own_gr[m].start()
        for i in range(1, T):
            gr_copy(m, i).start()

    def img_begin(grad):
        gr_own[0] = grad
        share_grad(0)
        terms(imgf, grad, term_i)
        for block in range(n_blocks):
            for other in range(Z):
                first = img_rows(block, other)
                yi_send[block, other] = term_i[first:first + win, :].astype(bf16)
        for i in range(1, n_blocks):
            yi_copy(i).start()

    def txt_begin(grad):
        gr_own[1] = grad
        terms(txtf, grad, term_t)
        for block in range(n_blocks):
            for group in range(Z // pair):
                rows = [
                    term_t[txt_rows(block, group * pair + n):txt_rows(block, group * pair + n) + per_t, :]
                    for n in range(pair)
                ]
                yt_send[block, group] = jnp.concatenate(rows, axis=0).astype(bf16)
        for i in range(1, n_blocks):
            yt_copy(i).start()
        share_grad(1)

    def plane_sum(send, recv, ss, rs):
        total = send[b].astype(f32)
        for i in range(1, n_blocks):
            src = (b + i) % n_blocks
            remote(send.at[0], recv.at[src], ss.at[i], rs.at[src], sibling).wait_recv()
            total += recv[src].astype(f32)
        return total

    def rs_sum(i, carry):
        total, sums = carry
        src = (h + i) % n_half
        remote(
            rs_mid.at[0], rs_recv.at[src], ri_ss.at[0], ri_rs.at[src], sibling
        ).wait_recv()
        return (
            total + rs_recv[src, 0:ROWS, :].astype(f32),
            sums + unpack(rs_recv[src, ROWS:PIECE, :]),
        )

    total_img, sums_img = lax.fori_loop(
        1, n_half, rs_sum, (rs_mid[h, 0:ROWS, :].astype(f32), unpack(rs_mid[h, ROWS:PIECE, :]))
    )
    own_img = own[0].astype(f32)
    own_txt = own[1].astype(f32)
    img_begin(raw_grad(total_img, sums_img, own_img, own_txt, invr[0:1, :]))

    total_txt = ga_send[0, 0:ROWS, :].astype(f32)
    sums_txt = unpack(ga_send[0, ROWS:PIECE, :])
    for o in near_first:
        src = (a + o) % na
        remote(ga_send.at[0], ga_recv.at[src], ga_ss.at[o], ga_rs.at[src], sibling).wait_recv()
        total_txt += ga_recv[src, 0:ROWS, :].astype(f32)
        sums_txt += unpack(ga_recv[src, ROWS:PIECE, :])
    txt_begin(raw_grad(total_txt, sums_txt, own_txt, own_img, invr[1:2, :]))

    def zi_copy(i):
        dst = (z + i) % Z
        return remote(zi_send.at[dst], zi_recv.at[z], zi_ss.at[i], zi_rs.at[z], z_dev(dst))

    def zt_copy(i):
        dst = (z + i) % Z
        return remote(zt_send.at[dst], zt_recv.at[z], zt_ss.at[i], zt_rs.at[z], z_dev(dst))

    def feature(m, back, rows, out):
        own_gr[m].wait()
        own_pp[m].wait()
        for i in range(1, T):
            src = (t + i) % T
            remote(
                gr_own.at[m], gr_all.at[m, :, pl.ds(pl.multiple_of(src * Q, Q), Q)],
                gr_ss.at[m * T + i], gr_rs.at[m * T + src], t_dev(src),
            ).wait_recv()
            pp_pair(i, src, 0)[m].wait_recv()
        back[...] = nt(gr_all[m], rows[...])
        copy = pltpu.make_async_copy(back, out, in_ss.at[m])
        copy.start()
        return copy

    zi_send[...] = plane_sum(yi_send, yi_recv, yi_ss, yi_rs).astype(bf16)

    @pl.loop(0, Z)
    def _(n):
        i = (Z // 2 + n) % Z

        @pl.when(i > 0)
        def _():
            zi_copy(i).start()

    feature_out = [feature(0, back_i, psi, gif)]
    total = plane_sum(yt_send, yt_recv, yt_ss, yt_rs)
    for other in range(Z):
        first = other % pair * per_t
        rows = total[other // pair, first:first + per_t, :]
        zt_send[other] = jnp.concatenate([rows] * pair, axis=0).astype(bf16)

    @pl.loop(0, Z)
    def _(n):
        i = (Z // 2 + n) % Z

        @pl.when(i > 0)
        def _():
            zt_copy(i).start()

    feature_out.append(feature(1, back_t, pst, gtf))

    for i in range(1, T):
        sq_copy(i).wait_send()
        for copy in pp_copies(i):
            copy.wait_send()
        for m in range(2):
            gr_copy(m, i).wait_send()
    for o in far_first:
        za_copy(o).wait_send()
        ga_copy(o).wait_send()
    fw_own.wait_send()

    @pl.loop(1, n_half)
    def _(i):
        ig_copy(i).wait_send()
        fw_copy(i).wait_send()
        rs_copy((h + i) % n_half).wait_send()

    @pl.loop(0, n_blocks)
    def _(block):
        cs_copy(block).wait_send()

    @pl.loop(0, na)
    def _(k):
        for m in range(1, T):
            tx_copy(k, m).wait_send()

        @pl.when(c != t)
        def _():
            tx_copy(k, 0).wait_send()

        for quarter in range(T):
            @pl.when((mine != 0) | (t != quarter))
            def _(quarter=quarter):
                gx_copy(k, quarter).wait_send()

    for i in range(1, n_blocks):
        yi_copy(i).wait_send()
        yt_copy(i).wait_send()

    def zi_add(i, total):
        src = (z + i) % Z
        remote(zi_send.at[0], zi_recv.at[src], zi_ss.at[i], zi_rs.at[src], sibling).wait_recv()
        return total + zi_recv[src].astype(f32)

    total = lax.fori_loop(1, Z, zi_add, zi_send[z].astype(f32))
    shift = ((z * XL + xl) * per_i) % 8
    result = total[0:per_i]
    for k in sorted({(k * per_i) % 8 for k in range(8)} - {0}):
        result = jnp.where(shift == k, total[k:k + per_i], result)
    gip[...] = result

    def zt_add(i, total):
        src = (z + i) % Z
        remote(zt_send.at[0], zt_recv.at[src], zt_ss.at[i], zt_rs.at[src], sibling).wait_recv()
        return total + zt_recv[src, 0:per_t, :].astype(f32)

    gtp[...] = lax.fori_loop(1, Z, zt_add, zt_send[z, 0:per_t, :].astype(f32))

    @pl.loop(1, Z)
    def _(i):
        zi_copy(i).wait_send()
        zt_copy(i).wait_send()
    for copy in feature_out:
        copy.wait()


def shards(ny, img_feat, txt_feat, img_proj, txt_proj, logit_scale):
    di, dt = img_feat.shape[1], txt_feat.shape[1]
    n_blocks = ny * XL
    n_plane = n_blocks * T
    n_half = n_plane // 2
    na = Z // T
    keys = na * ROWS
    emb = T * Q
    ndp = ny * Z * XL
    diy, dty = di // ny, dt // ny
    win = window_of(diy // (Z * XL))
    per_t = dty // (Z * XL)
    pair = 2 if per_t % 16 else 1
    tall = per_t * pair
    dma = pltpu.SemaphoreType.DMA
    vmem = pltpu.VMEM
    piece = (PIECE, Q)
    scratch = [
        vmem((ROWS, di), bf16),
        vmem((ROWS, dt), bf16),
        vmem((di, Q), bf16),
        vmem((dt, Q), bf16),
        vmem((T, 8, ROWS), f32),
        vmem((8, ROWS), f32),
        vmem((2, ROWS, Q), bf16),
        vmem((n_blocks * ROWS, emb), bf16),
        vmem((na, ROWS, Q), bf16),
        vmem((keys, emb), bf16),
        vmem((di // T, emb), bf16),
        vmem((dt // T, emb), bf16),
        vmem((ROWS, emb), f32),
        vmem((na, 8, ROWS), f32),
        vmem((n_blocks * ROWS, keys), bf16),
        vmem((n_plane, *piece), bf16),
        vmem((n_half, *piece), bf16),
        vmem((n_half, *piece), bf16),
        vmem((n_half, *piece), bf16),
        vmem((na * T, *piece), bf16),
        vmem((na * T, *piece), bf16),
        vmem((na, *piece), bf16),
        vmem((na, *piece), bf16),
        vmem((2, ROWS, Q), bf16),
        vmem((2, ROWS, emb), bf16),
        vmem((n_blocks, Z, win, Q), bf16),
        vmem((n_blocks, Z, win, Q), bf16),
        vmem((n_blocks, Z // pair, pair * per_t, Q), bf16),
        vmem((n_blocks, Z // pair, pair * per_t, Q), bf16),
        vmem((di, Q), f32),
        vmem((dt, Q), f32),
        vmem((ROWS, di // T), f32),
        vmem((ROWS, dt // T), f32),
        vmem((Z, win, Q), bf16),
        vmem((Z, win, Q), bf16),
        vmem((Z, tall, Q), bf16),
        vmem((Z, tall, Q), bf16),
    ]
    wide = max(n_blocks, 2)
    sems = [
        4, T, T, 2 * T, 2 * T, n_half, n_half, n_plane, na, na,
        na * T, na * T, n_blocks, n_blocks, n_half, n_half, na * T, na * T, na, na,
        2 * T, 2 * T, wide, wide, wide, wide, Z, Z, Z, Z,
    ]
    scratch += [dma((n,)) for n in sems]
    whole = pl.BlockSpec(memory_space=pltpu.VMEM)
    return pl.pallas_call(
        functools.partial(kernel, ny, di, dt),
        out_shape=(
            jax.ShapeDtypeStruct((di // ndp, Q), f32),
            jax.ShapeDtypeStruct((dt // ndp, Q), f32),
            jax.ShapeDtypeStruct((ROWS, di // T), f32),
            jax.ShapeDtypeStruct((ROWS, dt // T), f32),
        ),
        in_specs=[pl.BlockSpec(memory_space=pltpu.SMEM)]
        + [pl.BlockSpec(memory_space=pl.ANY)] * 4,
        out_specs=(whole, whole) + (pl.BlockSpec(memory_space=pl.ANY),) * 2,
        scratch_shapes=scratch,
        compiler_params=pltpu.CompilerParams(
            collective_id=0, has_side_effects=True, vmem_limit_bytes=56 * 1024 * 1024
        ),
    )(logit_scale, img_feat, txt_feat, img_proj, txt_proj)


def solution(mesh):
    ny = mesh.shape["dp"] // (Z * XL)
    return jax.shard_map(
        functools.partial(shards, ny),
        mesh=mesh,
        in_specs=(P("dp", None), P("dp", None), P(None, "tensor"), P(None, "tensor"), P()),
        out_specs=(P("dp", "tensor"), P("dp", "tensor"), P("dp", "tensor"), P("dp", "tensor")),
        check_vma=False,
    )
```

```python
import functools

import jax
import jax.numpy as jnp
from jax import lax
from jax.experimental import pallas as pl
from jax.experimental.pallas import tpu as pltpu
from jax.sharding import PartitionSpec as P

Z = 16
XL = 2
T = 4
ROWS = 128
Q = 128
SUMS = 16
PIECE = ROWS + SUMS
eps = 1e-06
loss_factor = 256.0
f32 = jnp.float32
bf16 = jnp.bfloat16


def nt(left, right):
    return lax.dot_general(left, right, (((1,), (1,)), ((), ())), preferred_element_type=f32)


def tn(left, right):
    return lax.dot_general(left, right, (((0,), (0,)), ((), ())), preferred_element_type=f32)


def row_sums(values):
    return jnp.sum(jnp.transpose(values), axis=0, keepdims=True)


def as_columns(row):
    return jnp.transpose(jnp.broadcast_to(row, (ROWS, ROWS)))


def rows_of(*rows):
    index = lax.broadcasted_iota(jnp.int32, (8, rows[0].shape[1]), 0)
    out = jnp.zeros((8, rows[0].shape[1]), f32)
    for k, row in enumerate(rows):
        out = jnp.where(index == k, row, out)
    return out


def pack(values):
    high = values.astype(bf16)
    return jnp.concatenate([high, (values - high.astype(f32)).astype(bf16)], axis=0)


def unpack(parts):
    parts = parts.astype(f32)
    return parts[0:8] + parts[8:16]


def window_of(per):
    return max(-(-(((k * per) % 8) + per) // 8) * 8 for k in range(8))


def kernel(
    ny, di, dt,
    scale_ref, imgf_hbm, txtf_hbm, imgp_hbm, txtp_hbm,
    gip, gtp, gif, gtf,
    imgf, txtf, imgp, txtp,
    sqb, invr, own, img_all, zbuf, txt_all,
    psi, pst, gt_acc, col_acc, weight,
    cs_send, cs_recv, rs_mid, rs_recv, gx_send, gx_recv, ga_send, ga_recv,
    gr_own, gr_all, yi_send, yi_recv, yt_send, yt_recv,
    term_i, term_t, back_i, back_t, zi_send, zi_recv, zt_send, zt_recv,
    in_ss, sq_ss, sq_rs, pp_ss, pp_rs, ig_ss, fw_ss, ig_rs, za_ss, za_rs,
    tx_ss, tx_rs, cs_ss, cs_rs, ri_ss, ri_rs, gx_ss, gx_rs, ga_ss, ga_rs,
    gr_ss, gr_rs, yi_ss, yi_rs, yt_ss, yt_rs, zi_ss, zi_rs, zt_ss, zt_rs,
):
    n_blocks = ny * XL
    n_plane = n_blocks * T
    n_half = n_plane // 2
    na = Z // T
    batch = ny * Z * XL * ROWS
    dp = lax.axis_index("dp")
    t = lax.axis_index("tensor")
    core = t % 2
    xl = dp % XL
    z = (dp // XL) % Z
    y = dp // (XL * Z)
    b = y * XL + xl
    p = b * T + t
    h = p // 2
    xh = t // 2
    a = z // T
    c = z % T

    def plane_dev(q):
        block = q // T
        return (((block // XL) * Z + z) * XL + block % XL, q % T)

    def zt_dev(other, tensor):
        return ((y * Z + other) * XL + xl, tensor)

    def z_dev(other):
        return zt_dev(other, t)

    def t_dev(other):
        return (dp, other)

    sibling = (dp, t + 1 - 2 * core)

    def remote(src, dst, send, recv, dev):
        return pltpu.make_async_remote_copy(
            src_ref=src, dst_ref=dst, send_sem=send, recv_sem=recv,
            device_id=dev, device_id_type=pl.DeviceIdType.MESH,
        )

    barrier = pltpu.get_barrier_semaphore()

    def greet(dev):
        pl.semaphore_signal(barrier, inc=1, device_id=dev, device_id_type=pl.DeviceIdType.MESH)

    @pl.loop(1, Z)
    def _(i):
        greet(z_dev((z + i) % Z))

    loads = [
        pltpu.make_async_copy(src, dst, in_ss.at[k])
        for k, (src, dst) in enumerate(
            [(imgf_hbm, imgf), (imgp_hbm, imgp), (txtf_hbm, txtf), (txtp_hbm, txtp)]
        )
    ]
    for copy in loads:
        copy.start()

    for e in (1, 2, Z - 1, Z - 2):
        for i in range(1, T):
            greet(zt_dev((z + e) % Z, (t + i) % T))

    @pl.loop(1, n_plane)
    def _(i):
        greet(plane_dev((p + i) % n_plane))

    scale = scale_ref[0]
    coef = scale * (loss_factor / (2.0 * batch))

    loads[0].wait()
    loads[1].wait()
    raw_img = jnp.dot(imgf[...], imgp[...], preferred_element_type=f32)
    loads[2].wait()
    loads[3].wait()
    raw_txt = jnp.dot(txtf[...], txtp[...], preferred_element_type=f32)
    sqb[t] = rows_of(row_sums(raw_img * raw_img), row_sums(raw_txt * raw_txt))
    pl.semaphore_wait(barrier, n_plane - 1 + Z - 1 + 4 * (T - 1))

    def sq_copy(i):
        return remote(sqb.at[t], sqb.at[t], sq_ss.at[i - 1], sq_rs.at[t], t_dev((t + i) % T))

    for i in range(1, T):
        sq_copy(i).start()

    di4, dt4 = di // T, dt // T

    def pp_pair(i, src, first):
        other = (t + i) % T
        quarter = pl.ds(pl.multiple_of(src * Q, Q), Q)
        return (
            remote(
                imgp.at[pl.ds(pl.multiple_of(first * di4, 16), di4), :], psi.at[:, quarter],
                pp_ss.at[2 * i], pp_rs.at[2 * src], t_dev(other),
            ),
            remote(
                txtp.at[pl.ds(pl.multiple_of(first * dt4, 16), dt4), :], pst.at[:, quarter],
                pp_ss.at[2 * i + 1], pp_rs.at[2 * src + 1], t_dev(other),
            ),
        )

    def pp_copies(i):
        return pp_pair(i, t, (t + i) % T)

    for i in range(1, T):
        for copy in pp_copies(i):
            copy.start()
    own_pp = [
        pltpu.make_async_copy(
            ref.at[pl.ds(pl.multiple_of(t * size, 16), size), :],
            dst.at[:, pl.ds(pl.multiple_of(t * Q, Q), Q)], pp_ss.at[k],
        )
        for k, (ref, dst, size) in enumerate([(imgp, psi, di4), (txtp, pst, dt4)])
    ]
    for copy in own_pp:
        copy.start()

    for i in range(1, T):
        src = (t + i) % T
        remote(sqb.at[src], sqb.at[src], sq_ss.at[i - 1], sq_rs.at[src], t_dev(src)).wait_recv()
    square = (sqb[0] + sqb[1]) + (sqb[2] + sqb[3])
    inv = lax.rsqrt(square + eps)
    invr[...] = inv
    emb_txt = (raw_txt * as_columns(inv[1:2])).astype(bf16)
    own[1] = emb_txt
    zbuf[a] = emb_txt

    def img_slot(q):
        return img_all.at[
            pl.ds(pl.multiple_of((q // T) * ROWS, ROWS), ROWS),
            pl.ds(pl.multiple_of((q % T) * Q, Q), Q),
        ]

    def txt_slot(k, quarter):
        return txt_all.at[
            pl.ds(pl.multiple_of(k * ROWS, ROWS), ROWS),
            pl.ds(pl.multiple_of(quarter * Q, Q), Q),
        ]

    def za_copy(o):
        return remote(zbuf.at[a], zbuf.at[a], za_ss.at[o], za_rs.at[a], z_dev((z + T * o) % Z))

    def za_land(o):
        src = (a + o) % na
        return remote(zbuf.at[src], zbuf.at[src], za_ss.at[o], za_rs.at[src], z_dev((z + T * o) % Z))

    two = 2 - 4 * core

    def tx_copy(k, m):
        delta = (0, 1, two, -1)[m]
        return remote(
            zbuf.at[k], txt_slot(k, t), tx_ss.at[k * T + m], tx_rs.at[k * T + t],
            zt_dev((z - delta + Z) % Z, c),
        )

    def tx_local(k):
        return pltpu.make_async_copy(zbuf.at[k], txt_slot(k, t), tx_ss.at[k * T])

    def pass_on(k):
        for m in range(1, T):
            tx_copy(k, m).start()

        @pl.when(c != t)
        def _():
            tx_copy(k, 0).start()

        @pl.when(c == t)
        def _():
            tx_local(k).start()

    far_first = sorted(range(1, na), key=lambda o: -min(o, na - o))
    near_first = far_first[::-1]
    near_groups = [o for o in near_first if min(o, na - o) == 1]
    far_groups = [o for o in near_first if min(o, na - o) > 1]
    for o in far_groups:
        za_copy(o).start()

    emb_img = (raw_img * as_columns(inv[0:1])).astype(bf16)
    own[0] = emb_img
    own_img_copy = pltpu.make_async_copy(own.at[0], img_slot(p), in_ss.at[0])
    own_img_copy.start()

    def peer(n, flip):
        return ((b + n + n_blocks) % n_blocks) * 2 + xh + flip - 2 * xh * flip

    def ig_copy(i):
        dst = peer(-(i // 2), i % 2) * 2 + core
        return remote(own.at[0], img_slot(p), ig_ss.at[i], ig_rs.at[p], plane_dev(dst))

    def ig_land(i):
        q = peer(i // 2, i % 2) * 2 + core
        return remote(own.at[0], img_slot(q), ig_ss.at[i], ig_rs.at[q], plane_dev(q))

    def fw_copy(i):
        q = peer(i // 2, i % 2) * 2 + core
        return remote(img_slot(q), img_slot(q), fw_ss.at[i], ig_rs.at[q], sibling)

    def fw_land(i):
        q = peer(i // 2, i % 2) * 2 + 1 - core
        return remote(img_slot(q), img_slot(q), fw_ss.at[i], ig_rs.at[q], sibling)

    fw_own = remote(own.at[0], img_slot(p), fw_ss.at[0], ig_rs.at[p], sibling)

    @pl.loop(1, n_half)
    def _(i):
        ig_copy(i).start()

    fw_own.start()
    for o in near_groups:
        za_copy(o).start()
    pass_on(a)

    mine = (t - c + T) % T

    def delta_of(quarter):
        return jnp.where(
            mine == 0, 0, jnp.where(mine == 1, 1, jnp.where(mine == 3, -1, 2 - 4 * (quarter % 2)))
        )

    base = jnp.where(mine == 2, a, ((z + delta_of(0) + Z) % Z) // T)
    turn = jnp.where((mine == 2) & (c < T // 2), -1, 1)
    if na == 4:
        order = [base, (base + turn + na) % na, (base - turn + na) % na, (base + 2) % na]
    else:
        order = [(base + n) % na for n in range(na)]

    def keys_ready(k):
        for quarter in range(T):
            @pl.when((mine != 0) | (t != quarter))
            def _(quarter=quarter):
                remote(
                    zbuf.at[0], txt_slot(k, quarter), tx_ss.at[0],
                    tx_rs.at[k * T + quarter], sibling,
                ).wait_recv()

        @pl.when(c == t)
        def _():
            tx_local(k).wait()

    keys = na * ROWS
    col_acc[...] = jnp.zeros_like(col_acc)

    def fold(values):
        return sum(values[:, k * ROWS:(k + 1) * ROWS] for k in range(values.shape[1] // ROWS))

    def score(first, count, k):
        rows = img_all[pl.ds(pl.multiple_of(first, ROWS), count), :]
        cos = nt(rows, txt_all[pl.ds(pl.multiple_of(k * ROWS, ROWS), ROWS), :])
        expo = jnp.exp(scale * (cos - 1.0))
        i = lax.broadcasted_iota(jnp.int32, (count, ROWS), 0)
        j = lax.broadcasted_iota(jnp.int32, (count, ROWS), 1)
        mask = (j - i) == jnp.where((k == a) & (t == c), first - b * ROWS, ROWS)
        part = jnp.where(mask, 0.0, expo).astype(bf16)
        weight[
            pl.ds(pl.multiple_of(first, ROWS), count), pl.ds(pl.multiple_of(k * ROWS, ROWS), ROWS)
        ] = part
        none = jnp.zeros((1, ROWS), f32)
        col_acc[k] += rows_of(
            jnp.sum(part.astype(f32), axis=0, keepdims=True),
            jnp.sum(jnp.where(mask, expo, 0.0), axis=0, keepdims=True),
            none,
            jnp.sum(jnp.where(mask, cos, 0.0), axis=0, keepdims=True),
        )
        gt_acc[...] += tn(part, rows)

    def gx_copy(k, quarter):
        return remote(
            gx_send.at[k * T + quarter], gx_recv.at[k * T + mine], gx_ss.at[k * T + quarter],
            gx_rs.at[k * T + mine], zt_dev((z + delta_of(quarter) + Z) % Z, quarter),
        )

    def texts_out(k):
        total = gt_acc[...]
        rows = txt_all[pl.ds(pl.multiple_of(k * ROWS, ROWS), ROWS), :].astype(f32)
        none = jnp.zeros((1, ROWS), f32)
        sums = pack(col_acc[k] + rows_of(none, none, row_sums(fold(total * rows))))
        for quarter in range(T):
            gx_send[k * T + quarter, 0:ROWS, :] = total[:, quarter * Q:(quarter + 1) * Q].astype(bf16)
            gx_send[k * T + quarter, ROWS:PIECE, :] = sums

            @pl.when((mine != 0) | (t != quarter))
            def _(quarter=quarter):
                gx_copy(k, quarter).start()

    for o in near_groups:
        za_land(o).wait_recv()
        pass_on((a + o) % na)

    middle = n_half * 5 // 8

    @pl.loop(1, middle)
    def _(i):
        ig_land(i).wait_recv()
        fw_copy(i).start()

    for o in far_groups:
        za_land(o).wait_recv()
        pass_on((a + o) % na)

    @pl.loop(middle, n_half)
    def _(i):
        ig_land(i).wait_recv()
        fw_copy(i).start()

    own_img_copy.wait()

    @pl.loop(0, n_half)
    def _(i):
        fw_land(i).wait_recv()

    tall_rows = min(4, n_blocks) * ROWS
    for k in order:
        keys_ready(k)
        gt_acc[...] = jnp.zeros_like(gt_acc)

        @pl.loop(0, n_blocks * ROWS // tall_rows)
        def _(n, k=k):
            score(n * tall_rows, tall_rows, k)

        texts_out(k)

    def cs_copy(block):
        return remote(
            cs_send.at[pl.ds((1 - core) * n_half + block * 2, 2)],
            cs_recv.at[pl.ds(block * 2, 2)], cs_ss.at[block], cs_rs.at[block], sibling,
        )

    def rs_copy(k):
        return remote(
            rs_mid.at[k], rs_recv.at[h], ri_ss.at[k], ri_rs.at[h], plane_dev(k * 2 + core)
        )

    def both_cores(block):
        cs_copy(block).wait_recv()
        for part in range(2):
            k = block * 2 + part
            one = cs_send.at[core * n_half + k]
            other = cs_recv.at[k]
            rs_mid[k, 0:ROWS, :] = (
                one[0:ROWS, :].astype(f32) + other[0:ROWS, :].astype(f32)
            ).astype(bf16)
            rs_mid[k, ROWS:PIECE, :] = pack(unpack(one[ROWS:PIECE, :]) + unpack(other[ROWS:PIECE, :]))

            @pl.when(k != h)
            def _(k=k):
                rs_copy(k).start()

    @pl.loop(0, n_blocks)
    def _(n):
        block = (b + 1 + n) % n_blocks
        first = pl.ds(pl.multiple_of(block * ROWS, ROWS), ROWS)
        part = jnp.dot(weight[first, :], txt_all[...], preferred_element_type=f32)
        diag = jnp.where(block == b, col_acc[a], 0.0)
        sums = pack(
            rows_of(
                row_sums(fold(weight[first, :].astype(f32))), diag[1:2],
                row_sums(fold(part * img_all[first, :].astype(f32))), diag[3:4],
            )
        )
        for quarter in range(T):
            k = (quarter % 2) * n_half + block * 2 + quarter // 2
            cs_send[k, 0:ROWS, :] = part[:, quarter * Q:(quarter + 1) * Q].astype(bf16)
            cs_send[k, ROWS:PIECE, :] = sums
        cs_copy(block).start()

    def ga_copy(o):
        return remote(
            ga_send.at[o], ga_recv.at[a], ga_ss.at[o], ga_rs.at[a], z_dev((z + T * o) % Z)
        )

    def near_sum(o):
        k = (a + o) % na

        @pl.when(c == t)
        def _():
            gx_recv[k * T] = gx_send[k * T + t]

        for m in range(T):
            wait = remote(
                gx_send.at[0], gx_recv.at[k * T + m], gx_ss.at[0], gx_rs.at[k * T + m], sibling
            ).wait_recv
            if m == 0:
                pl.when(c != t)(wait)
            else:
                wait()
        total = sum(gx_recv[k * T + m, 0:ROWS, :].astype(f32) for m in range(T))
        ga_send[o, 0:ROWS, :] = total.astype(bf16)
        ga_send[o, ROWS:PIECE, :] = pack(
            sum(unpack(gx_recv[k * T + m, ROWS:PIECE, :]) for m in range(T))
        )

    @pl.loop(0, n_blocks)
    def _(n):
        both_cores((b + 1 + n) % n_blocks)

    for o in near_groups:
        near_sum(o)
        ga_copy(o).start()

    for o in far_groups:
        near_sum(o)
        ga_copy(o).start()
    near_sum(0)

    def raw_grad(total, sums, emb, target, inv_row):
        off, diag, inner, match = (sums[k:k + 1] for k in range(4))
        factor = coef / (off + diag) * inv_row
        align = inner - off * match
        return (
            as_columns(factor) * (total - as_columns(off) * target - as_columns(align) * emb)
        ).astype(bf16)

    def gr_copy(m, i):
        return remote(
            gr_own.at[m], gr_all.at[m, :, pl.ds(pl.multiple_of(t * Q, Q), Q)],
            gr_ss.at[m * T + i], gr_rs.at[m * T + t], t_dev((t + i) % T),
        )

    own_gr = [
        pltpu.make_async_copy(
            gr_own.at[m], gr_all.at[m, :, pl.ds(pl.multiple_of(t * Q, Q), Q)], gr_ss.at[m * T]
        )
        for m in range(2)
    ]

    diy, dty = di // ny, dt // ny
    per_i, per_t = diy // (Z * XL), dty // (Z * XL)
    win = window_of(per_i)
    pair = 2 if per_t % 16 else 1

    def img_rows(block, other):
        return (block // XL) * diy + ((other * XL + block % XL) * per_i) // 8 * 8

    def txt_rows(block, other):
        return (block // XL) * dty + (other * XL + block % XL) * per_t

    def yi_copy(i):
        dst = (b + i) % n_blocks
        return remote(
            yi_send.at[dst], yi_recv.at[b], yi_ss.at[i], yi_rs.at[b], plane_dev(dst * T + t)
        )

    def yt_copy(i):
        dst = (b + i) % n_blocks
        return remote(
            yt_send.at[dst], yt_recv.at[b], yt_ss.at[i], yt_rs.at[b], plane_dev(dst * T + t)
        )

    def terms(feat, grad, term):
        for k in range(0, feat.shape[1], 128):
            term[k:k + 128, :] = tn(feat[:, k:k + 128], grad)

    def img_begin(grad):
        gr_own[0] = grad
        terms(imgf, grad, term_i)
        for block in range(n_blocks):
            for other in range(Z):
                first = img_rows(block, other)
                yi_send[block, other] = term_i[first:first + win, :].astype(bf16)
        for i in range(1, n_blocks):
            yi_copy(i).start()

    def txt_begin(grad):
        gr_own[1] = grad
        terms(txtf, grad, term_t)
        for block in range(n_blocks):
            for group in range(Z // pair):
                rows = [
                    term_t[txt_rows(block, group * pair + n):txt_rows(block, group * pair + n) + per_t, :]
                    for n in range(pair)
                ]
                yt_send[block, group] = jnp.concatenate(rows, axis=0).astype(bf16)
        for i in range(1, n_blocks):
            yt_copy(i).start()

    def plane_sum(send, recv, ss, rs):
        total = send[b].astype(f32)
        for i in range(1, n_blocks):
            src = (b + i) % n_blocks
            remote(send.at[0], recv.at[src], ss.at[i], rs.at[src], sibling).wait_recv()
            total += recv[src].astype(f32)
        return total

    def rs_sum(i, carry):
        total, sums = carry
        src = (h + i) % n_half
        remote(
            rs_mid.at[0], rs_recv.at[src], ri_ss.at[0], ri_rs.at[src], sibling
        ).wait_recv()
        return (
            total + rs_recv[src, 0:ROWS, :].astype(f32),
            sums + unpack(rs_recv[src, ROWS:PIECE, :]),
        )

    total_img, sums_img = lax.fori_loop(
        1, n_half, rs_sum, (rs_mid[h, 0:ROWS, :].astype(f32), unpack(rs_mid[h, ROWS:PIECE, :]))
    )
    own_img = own[0].astype(f32)
    own_txt = own[1].astype(f32)
    img_begin(raw_grad(total_img, sums_img, own_img, own_txt, invr[0:1, :]))

    total_txt = ga_send[0, 0:ROWS, :].astype(f32)
    sums_txt = unpack(ga_send[0, ROWS:PIECE, :])
    for o in near_first:
        src = (a + o) % na
        remote(ga_send.at[0], ga_recv.at[src], ga_ss.at[o], ga_rs.at[src], sibling).wait_recv()
        total_txt += ga_recv[src, 0:ROWS, :].astype(f32)
        sums_txt += unpack(ga_recv[src, ROWS:PIECE, :])
    txt_begin(raw_grad(total_txt, sums_txt, own_txt, own_img, invr[1:2, :]))

    def zi_copy(i):
        dst = (z + i) % Z
        return remote(zi_send.at[dst], zi_recv.at[z], zi_ss.at[i], zi_rs.at[z], z_dev(dst))

    def zt_copy(i):
        dst = (z + i) % Z
        return remote(zt_send.at[dst], zt_recv.at[z], zt_ss.at[i], zt_rs.at[z], z_dev(dst))

    zi_send[...] = plane_sum(yi_send, yi_recv, yi_ss, yi_rs).astype(bf16)

    @pl.loop(0, Z)
    def _(n):
        i = (Z // 2 + n) % Z

        @pl.when(i > 0)
        def _():
            zi_copy(i).start()

    total = plane_sum(yt_send, yt_recv, yt_ss, yt_rs)
    for other in range(Z):
        first = other % pair * per_t
        rows = total[other // pair, first:first + per_t, :]
        zt_send[other] = jnp.concatenate([rows] * pair, axis=0).astype(bf16)

    @pl.loop(0, Z)
    def _(n):
        i = (Z // 2 + n) % Z

        @pl.when(i > 0)
        def _():
            zt_copy(i).start()

    for m in range(2):
        own_gr[m].start()
        for i in range(1, T):
            gr_copy(m, i).start()
    for m in range(2):
        own_gr[m].wait()
        own_pp[m].wait()
        for i in range(1, T):
            src = (t + i) % T
            remote(
                gr_own.at[m], gr_all.at[m, :, pl.ds(pl.multiple_of(src * Q, Q), Q)],
                gr_ss.at[m * T + i], gr_rs.at[m * T + src], t_dev(src),
            ).wait_recv()
    for i in range(1, T):
        for copy in pp_pair(i, (t + i) % T, 0):
            copy.wait_recv()
    back_i[...] = nt(gr_all[0], psi[...])
    back_t[...] = nt(gr_all[1], pst[...])
    feature_out = [
        pltpu.make_async_copy(src, dst, in_ss.at[k])
        for k, (src, dst) in enumerate([(back_i, gif), (back_t, gtf)])
    ]
    for copy in feature_out:
        copy.start()

    for i in range(1, T):
        sq_copy(i).wait_send()
        for copy in pp_copies(i):
            copy.wait_send()
        for m in range(2):
            gr_copy(m, i).wait_send()
    for o in far_first:
        za_copy(o).wait_send()
        ga_copy(o).wait_send()
    fw_own.wait_send()

    @pl.loop(1, n_half)
    def _(i):
        ig_copy(i).wait_send()
        fw_copy(i).wait_send()
        rs_copy((h + i) % n_half).wait_send()

    @pl.loop(0, n_blocks)
    def _(block):
        cs_copy(block).wait_send()

    @pl.loop(0, na)
    def _(k):
        for m in range(1, T):
            tx_copy(k, m).wait_send()

        @pl.when(c != t)
        def _():
            tx_copy(k, 0).wait_send()

        for quarter in range(T):
            @pl.when((mine != 0) | (t != quarter))
            def _(quarter=quarter):
                gx_copy(k, quarter).wait_send()

    for i in range(1, n_blocks):
        yi_copy(i).wait_send()
        yt_copy(i).wait_send()

    def zi_add(i, total):
        src = (z + i) % Z
        remote(zi_send.at[0], zi_recv.at[src], zi_ss.at[i], zi_rs.at[src], sibling).wait_recv()
        return total + zi_recv[src].astype(f32)

    total = lax.fori_loop(1, Z, zi_add, zi_send[z].astype(f32))
    shift = ((z * XL + xl) * per_i) % 8
    result = total[0:per_i]
    for k in sorted({(k * per_i) % 8 for k in range(8)} - {0}):
        result = jnp.where(shift == k, total[k:k + per_i], result)
    gip[...] = result

    def zt_add(i, total):
        src = (z + i) % Z
        remote(zt_send.at[0], zt_recv.at[src], zt_ss.at[i], zt_rs.at[src], sibling).wait_recv()
        return total + zt_recv[src, 0:per_t, :].astype(f32)

    gtp[...] = lax.fori_loop(1, Z, zt_add, zt_send[z, 0:per_t, :].astype(f32))

    @pl.loop(1, Z)
    def _(i):
        zi_copy(i).wait_send()
        zt_copy(i).wait_send()
    for copy in feature_out:
        copy.wait()


def shards(ny, img_feat, txt_feat, img_proj, txt_proj, logit_scale):
    di, dt = img_feat.shape[1], txt_feat.shape[1]
    n_blocks = ny * XL
    n_plane = n_blocks * T
    n_half = n_plane // 2
    na = Z // T
    keys = na * ROWS
    emb = T * Q
    ndp = ny * Z * XL
    diy, dty = di // ny, dt // ny
    win = window_of(diy // (Z * XL))
    per_t = dty // (Z * XL)
    pair = 2 if per_t % 16 else 1
    tall = per_t * pair
    dma = pltpu.SemaphoreType.DMA
    vmem = pltpu.VMEM
    piece = (PIECE, Q)
    scratch = [
        vmem((ROWS, di), bf16),
        vmem((ROWS, dt), bf16),
        vmem((di, Q), bf16),
        vmem((dt, Q), bf16),
        vmem((T, 8, ROWS), f32),
        vmem((8, ROWS), f32),
        vmem((2, ROWS, Q), bf16),
        vmem((n_blocks * ROWS, emb), bf16),
        vmem((na, ROWS, Q), bf16),
        vmem((keys, emb), bf16),
        vmem((di // T, emb), bf16),
        vmem((dt // T, emb), bf16),
        vmem((ROWS, emb), f32),
        vmem((na, 8, ROWS), f32),
        vmem((n_blocks * ROWS, keys), bf16),
        vmem((n_plane, *piece), bf16),
        vmem((n_half, *piece), bf16),
        vmem((n_half, *piece), bf16),
        vmem((n_half, *piece), bf16),
        vmem((na * T, *piece), bf16),
        vmem((na * T, *piece), bf16),
        vmem((na, *piece), bf16),
        vmem((na, *piece), bf16),
        vmem((2, ROWS, Q), bf16),
        vmem((2, ROWS, emb), bf16),
        vmem((n_blocks, Z, win, Q), bf16),
        vmem((n_blocks, Z, win, Q), bf16),
        vmem((n_blocks, Z // pair, pair * per_t, Q), bf16),
        vmem((n_blocks, Z // pair, pair * per_t, Q), bf16),
        vmem((di, Q), f32),
        vmem((dt, Q), f32),
        vmem((ROWS, di // T), f32),
        vmem((ROWS, dt // T), f32),
        vmem((Z, win, Q), bf16),
        vmem((Z, win, Q), bf16),
        vmem((Z, tall, Q), bf16),
        vmem((Z, tall, Q), bf16),
    ]
    wide = max(n_blocks, 2)
    sems = [
        4, T, T, 2 * T, 2 * T, n_half, n_half, n_plane, na, na,
        na * T, na * T, n_blocks, n_blocks, n_half, n_half, na * T, na * T, na, na,
        2 * T, 2 * T, wide, wide, wide, wide, Z, Z, Z, Z,
    ]
    scratch += [dma((n,)) for n in sems]
    whole = pl.BlockSpec(memory_space=pltpu.VMEM)
    return pl.pallas_call(
        functools.partial(kernel, ny, di, dt),
        out_shape=(
            jax.ShapeDtypeStruct((di // ndp, Q), f32),
            jax.ShapeDtypeStruct((dt // ndp, Q), f32),
            jax.ShapeDtypeStruct((ROWS, di // T), f32),
            jax.ShapeDtypeStruct((ROWS, dt // T), f32),
        ),
        in_specs=[pl.BlockSpec(memory_space=pltpu.SMEM)]
        + [pl.BlockSpec(memory_space=pl.ANY)] * 4,
        out_specs=(whole, whole) + (pl.BlockSpec(memory_space=pl.ANY),) * 2,
        scratch_shapes=scratch,
        compiler_params=pltpu.CompilerParams(
            collective_id=0, has_side_effects=True, vmem_limit_bytes=56 * 1024 * 1024
        ),
    )(logit_scale, img_feat, txt_feat, img_proj, txt_proj)


def solution(mesh):
    ny = mesh.shape["dp"] // (Z * XL)
    return jax.shard_map(
        functools.partial(shards, ny),
        mesh=mesh,
        in_specs=(P("dp", None), P("dp", None), P(None, "tensor"), P(None, "tensor"), P()),
        out_specs=(P("dp", "tensor"), P("dp", "tensor"), P("dp", "tensor"), P("dp", "tensor")),
        check_vma=False,
    )
```

```python
import functools

import jax
import jax.numpy as jnp
from jax import lax
from jax.experimental import pallas as pl
from jax.experimental.pallas import tpu as pltpu
from jax.sharding import PartitionSpec as P

Z = 16
XL = 2
T = 4
ROWS = 128
Q = 128
SUMS = 16
PIECE = ROWS + SUMS
eps = 1e-06
loss_factor = 256.0
f32 = jnp.float32
bf16 = jnp.bfloat16


def nt(left, right):
    return lax.dot_general(left, right, (((1,), (1,)), ((), ())), preferred_element_type=f32)


def tn(left, right):
    return lax.dot_general(left, right, (((0,), (0,)), ((), ())), preferred_element_type=f32)


def row_sums(values):
    return jnp.sum(jnp.transpose(values), axis=0, keepdims=True)


def as_columns(row):
    return jnp.transpose(jnp.broadcast_to(row, (ROWS, ROWS)))


def rows_of(*rows):
    index = lax.broadcasted_iota(jnp.int32, (8, rows[0].shape[1]), 0)
    out = jnp.zeros((8, rows[0].shape[1]), f32)
    for k, row in enumerate(rows):
        out = jnp.where(index == k, row, out)
    return out


def pack(values):
    high = values.astype(bf16)
    return jnp.concatenate([high, (values - high.astype(f32)).astype(bf16)], axis=0)


def unpack(parts):
    parts = parts.astype(f32)
    return parts[0:8] + parts[8:16]


def window_of(per):
    return max(-(-(((k * per) % 8) + per) // 8) * 8 for k in range(8))


def kernel(
    ny, di, dt,
    scale_ref, imgf_hbm, txtf_hbm, imgp_hbm, txtp_hbm,
    gip, gtp, gif, gtf,
    imgf, txtf, imgp, txtp,
    sqb, invr, own, img_all, zbuf, txt_all,
    psi, pst, gt_acc, col_acc, weight,
    cs_send, cs_recv, rs_mid, rs_recv, gx_send, gx_recv, ga_send, ga_recv,
    gr_own, gr_all, yi_send, yi_recv, yt_send, yt_recv,
    term_i, term_t, back_i, back_t, zi_send, zi_recv, zt_send, zt_recv,
    in_ss, sq_ss, sq_rs, pp_ss, pp_rs, ig_ss, fw_ss, ig_rs, za_ss, za_rs,
    tx_ss, tx_rs, cs_ss, cs_rs, ri_ss, ri_rs, gx_ss, gx_rs, ga_ss, ga_rs,
    gr_ss, gr_rs, yi_ss, yi_rs, yt_ss, yt_rs, zi_ss, zi_rs, zt_ss, zt_rs,
):
    n_blocks = ny * XL
    n_plane = n_blocks * T
    n_half = n_plane // 2
    na = Z // T
    batch = ny * Z * XL * ROWS
    dp = lax.axis_index("dp")
    t = lax.axis_index("tensor")
    core = t % 2
    xl = dp % XL
    z = (dp // XL) % Z
    y = dp // (XL * Z)
    b = y * XL + xl
    p = b * T + t
    h = p // 2
    xh = t // 2
    a = z // T
    c = z % T

    def plane_dev(q):
        block = q // T
        return (((block // XL) * Z + z) * XL + block % XL, q % T)

    def zt_dev(other, tensor):
        return ((y * Z + other) * XL + xl, tensor)

    def z_dev(other):
        return zt_dev(other, t)

    def t_dev(other):
        return (dp, other)

    sibling = (dp, t + 1 - 2 * core)

    def remote(src, dst, send, recv, dev):
        return pltpu.make_async_remote_copy(
            src_ref=src, dst_ref=dst, send_sem=send, recv_sem=recv,
            device_id=dev, device_id_type=pl.DeviceIdType.MESH,
        )

    barrier = pltpu.get_barrier_semaphore()

    def greet(dev):
        pl.semaphore_signal(barrier, inc=1, device_id=dev, device_id_type=pl.DeviceIdType.MESH)

    @pl.loop(1, Z)
    def _(i):
        greet(z_dev((z + i) % Z))

    loads = [
        pltpu.make_async_copy(src, dst, in_ss.at[k])
        for k, (src, dst) in enumerate(
            [(imgf_hbm, imgf), (imgp_hbm, imgp), (txtf_hbm, txtf), (txtp_hbm, txtp)]
        )
    ]
    for copy in loads:
        copy.start()

    for e in (1, 2, Z - 1, Z - 2):
        for i in range(1, T):
            greet(zt_dev((z + e) % Z, (t + i) % T))

    @pl.loop(1, n_plane)
    def _(i):
        greet(plane_dev((p + i) % n_plane))

    scale = scale_ref[0]
    coef = scale * (loss_factor / (2.0 * batch))

    loads[0].wait()
    loads[1].wait()
    raw_img = jnp.dot(imgf[...], imgp[...], preferred_element_type=f32)
    loads[2].wait()
    loads[3].wait()
    raw_txt = jnp.dot(txtf[...], txtp[...], preferred_element_type=f32)
    sqb[t] = rows_of(row_sums(raw_img * raw_img), row_sums(raw_txt * raw_txt))
    pl.semaphore_wait(barrier, n_plane - 1 + Z - 1 + 4 * (T - 1))

    def sq_copy(i):
        return remote(sqb.at[t], sqb.at[t], sq_ss.at[i - 1], sq_rs.at[t], t_dev((t + i) % T))

    for i in range(1, T):
        sq_copy(i).start()

    di4, dt4 = di // T, dt // T

    def pp_pair(i, src, first):
        other = (t + i) % T
        quarter = pl.ds(pl.multiple_of(src * Q, Q), Q)
        return (
            remote(
                imgp.at[pl.ds(pl.multiple_of(first * di4, 16), di4), :], psi.at[:, quarter],
                pp_ss.at[2 * i], pp_rs.at[2 * src], t_dev(other),
            ),
            remote(
                txtp.at[pl.ds(pl.multiple_of(first * dt4, 16), dt4), :], pst.at[:, quarter],
                pp_ss.at[2 * i + 1], pp_rs.at[2 * src + 1], t_dev(other),
            ),
        )

    def pp_copies(i):
        return pp_pair(i, t, (t + i) % T)

    for i in range(1, T):
        for copy in pp_copies(i):
            copy.start()
    own_pp = [
        pltpu.make_async_copy(
            ref.at[pl.ds(pl.multiple_of(t * size, 16), size), :],
            dst.at[:, pl.ds(pl.multiple_of(t * Q, Q), Q)], pp_ss.at[k],
        )
        for k, (ref, dst, size) in enumerate([(imgp, psi, di4), (txtp, pst, dt4)])
    ]
    for copy in own_pp:
        copy.start()

    for i in range(1, T):
        src = (t + i) % T
        remote(sqb.at[src], sqb.at[src], sq_ss.at[i - 1], sq_rs.at[src], t_dev(src)).wait_recv()
    square = (sqb[0] + sqb[1]) + (sqb[2] + sqb[3])
    inv = lax.rsqrt(square + eps)
    invr[...] = inv
    emb_txt = (raw_txt * as_columns(inv[1:2])).astype(bf16)
    own[1] = emb_txt
    zbuf[a] = emb_txt

    def img_slot(q):
        return img_all.at[
            pl.ds(pl.multiple_of((q // T) * ROWS, ROWS), ROWS),
            pl.ds(pl.multiple_of((q % T) * Q, Q), Q),
        ]

    def txt_slot(k, quarter):
        return txt_all.at[
            pl.ds(pl.multiple_of(k * ROWS, ROWS), ROWS),
            pl.ds(pl.multiple_of(quarter * Q, Q), Q),
        ]

    def za_copy(o):
        return remote(zbuf.at[a], zbuf.at[a], za_ss.at[o], za_rs.at[a], z_dev((z + T * o) % Z))

    def za_land(o):
        src = (a + o) % na
        return remote(zbuf.at[src], zbuf.at[src], za_ss.at[o], za_rs.at[src], z_dev((z + T * o) % Z))

    two = 2 - 4 * core

    def tx_copy(k, m):
        delta = (0, 1, two, -1)[m]
        return remote(
            zbuf.at[k], txt_slot(k, t), tx_ss.at[k * T + m], tx_rs.at[k * T + t],
            zt_dev((z - delta + Z) % Z, c),
        )

    def tx_local(k):
        return pltpu.make_async_copy(zbuf.at[k], txt_slot(k, t), tx_ss.at[k * T])

    def pass_on(k):
        for m in range(1, T):
            tx_copy(k, m).start()

        @pl.when(c != t)
        def _():
            tx_copy(k, 0).start()

        @pl.when(c == t)
        def _():
            tx_local(k).start()

    far_first = sorted(range(1, na), key=lambda o: -min(o, na - o))
    near_first = far_first[::-1]
    near_groups = [o for o in near_first if min(o, na - o) == 1]
    far_groups = [o for o in near_first if min(o, na - o) > 1]
    for o in far_groups:
        za_copy(o).start()

    emb_img = (raw_img * as_columns(inv[0:1])).astype(bf16)
    own[0] = emb_img
    own_img_copy = pltpu.make_async_copy(own.at[0], img_slot(p), in_ss.at[0])
    own_img_copy.start()

    def peer(n, flip):
        return ((b + n + n_blocks) % n_blocks) * 2 + xh + flip - 2 * xh * flip

    def ig_copy(i):
        dst = peer(-(i // 2), i % 2) * 2 + core
        return remote(own.at[0], img_slot(p), ig_ss.at[i], ig_rs.at[p], plane_dev(dst))

    def ig_land(i):
        q = peer(i // 2, i % 2) * 2 + core
        return remote(own.at[0], img_slot(q), ig_ss.at[i], ig_rs.at[q], plane_dev(q))

    def fw_copy(i):
        q = peer(i // 2, i % 2) * 2 + core
        return remote(img_slot(q), img_slot(q), fw_ss.at[i], ig_rs.at[q], sibling)

    def fw_land(i):
        q = peer(i // 2, i % 2) * 2 + 1 - core
        return remote(img_slot(q), img_slot(q), fw_ss.at[i], ig_rs.at[q], sibling)

    fw_own = remote(own.at[0], img_slot(p), fw_ss.at[0], ig_rs.at[p], sibling)

    @pl.loop(1, n_half)
    def _(i):
        ig_copy(i).start()

    fw_own.start()
    for o in near_groups:
        za_copy(o).start()
    pass_on(a)

    mine = (t - c + T) % T

    def delta_of(quarter):
        return jnp.where(
            mine == 0, 0, jnp.where(mine == 1, 1, jnp.where(mine == 3, -1, 2 - 4 * (quarter % 2)))
        )

    base = jnp.where(mine == 2, a, ((z + delta_of(0) + Z) % Z) // T)
    turn = jnp.where((mine == 2) & (c < T // 2), -1, 1)
    if na == 4:
        order = [base, (base + turn + na) % na, (base - turn + na) % na, (base + 2) % na]
    else:
        order = [(base + n) % na for n in range(na)]

    def keys_ready(k):
        for quarter in range(T):
            @pl.when((mine != 0) | (t != quarter))
            def _(quarter=quarter):
                remote(
                    zbuf.at[0], txt_slot(k, quarter), tx_ss.at[0],
                    tx_rs.at[k * T + quarter], sibling,
                ).wait_recv()

        @pl.when(c == t)
        def _():
            tx_local(k).wait()

    keys = na * ROWS
    col_acc[...] = jnp.zeros_like(col_acc)

    def fold(values):
        return sum(values[:, k * ROWS:(k + 1) * ROWS] for k in range(values.shape[1] // ROWS))

    def score(first, count, k):
        rows = img_all[pl.ds(pl.multiple_of(first, ROWS), count), :]
        cos = nt(rows, txt_all[pl.ds(pl.multiple_of(k * ROWS, ROWS), ROWS), :])
        expo = jnp.exp(scale * (cos - 1.0))
        i = lax.broadcasted_iota(jnp.int32, (count, ROWS), 0)
        j = lax.broadcasted_iota(jnp.int32, (count, ROWS), 1)
        mask = (j - i) == jnp.where((k == a) & (t == c), first - b * ROWS, ROWS)
        part = jnp.where(mask, 0.0, expo).astype(bf16)
        weight[
            pl.ds(pl.multiple_of(first, ROWS), count), pl.ds(pl.multiple_of(k * ROWS, ROWS), ROWS)
        ] = part
        none = jnp.zeros((1, ROWS), f32)
        col_acc[k] += rows_of(
            jnp.sum(part.astype(f32), axis=0, keepdims=True),
            jnp.sum(jnp.where(mask, expo, 0.0), axis=0, keepdims=True),
            none,
            jnp.sum(jnp.where(mask, cos, 0.0), axis=0, keepdims=True),
        )
        gt_acc[...] += tn(part, rows)

    def gx_copy(k, quarter):
        return remote(
            gx_send.at[k * T + quarter], gx_recv.at[k * T + mine], gx_ss.at[k * T + quarter],
            gx_rs.at[k * T + mine], zt_dev((z + delta_of(quarter) + Z) % Z, quarter),
        )

    def texts_out(k):
        total = gt_acc[...]
        rows = txt_all[pl.ds(pl.multiple_of(k * ROWS, ROWS), ROWS), :].astype(f32)
        none = jnp.zeros((1, ROWS), f32)
        sums = pack(col_acc[k] + rows_of(none, none, row_sums(fold(total * rows))))
        for quarter in range(T):
            gx_send[k * T + quarter, 0:ROWS, :] = total[:, quarter * Q:(quarter + 1) * Q].astype(bf16)
            gx_send[k * T + quarter, ROWS:PIECE, :] = sums

            @pl.when((mine != 0) | (t != quarter))
            def _(quarter=quarter):
                gx_copy(k, quarter).start()

    for o in near_groups:
        za_land(o).wait_recv()
        pass_on((a + o) % na)

    middle = n_half * 5 // 8

    @pl.loop(1, middle)
    def _(i):
        ig_land(i).wait_recv()
        fw_copy(i).start()

    for o in far_groups:
        za_land(o).wait_recv()
        pass_on((a + o) % na)

    @pl.loop(middle, n_half)
    def _(i):
        ig_land(i).wait_recv()
        fw_copy(i).start()

    own_img_copy.wait()

    @pl.loop(0, n_half)
    def _(i):
        fw_land(i).wait_recv()

    tall_rows = min(4, n_blocks) * ROWS
    for k in order:
        keys_ready(k)
        gt_acc[...] = jnp.zeros_like(gt_acc)

        @pl.loop(0, n_blocks * ROWS // tall_rows)
        def _(n, k=k):
            score(n * tall_rows, tall_rows, k)

        texts_out(k)

    def cs_copy(block):
        return remote(
            cs_send.at[pl.ds((1 - core) * n_half + block * 2, 2)],
            cs_recv.at[pl.ds(block * 2, 2)], cs_ss.at[block], cs_rs.at[block], sibling,
        )

    def rs_copy(k):
        return remote(
            rs_mid.at[k], rs_recv.at[h], ri_ss.at[k], ri_rs.at[h], plane_dev(k * 2 + core)
        )

    def both_cores(block):
        cs_copy(block).wait_recv()
        for part in range(2):
            k = block * 2 + part
            one = cs_send.at[core * n_half + k]
            other = cs_recv.at[k]
            rs_mid[k, 0:ROWS, :] = (
                one[0:ROWS, :].astype(f32) + other[0:ROWS, :].astype(f32)
            ).astype(bf16)
            rs_mid[k, ROWS:PIECE, :] = pack(unpack(one[ROWS:PIECE, :]) + unpack(other[ROWS:PIECE, :]))

            @pl.when(k != h)
            def _(k=k):
                rs_copy(k).start()

    @pl.loop(0, n_blocks)
    def _(n):
        block = (b + 1 + n) % n_blocks
        first = pl.ds(pl.multiple_of(block * ROWS, ROWS), ROWS)
        part = jnp.dot(weight[first, :], txt_all[...], preferred_element_type=f32)
        diag = jnp.where(block == b, col_acc[a], 0.0)
        sums = pack(
            rows_of(
                row_sums(fold(weight[first, :].astype(f32))), diag[1:2],
                row_sums(fold(part * img_all[first, :].astype(f32))), diag[3:4],
            )
        )
        for quarter in range(T):
            k = (quarter % 2) * n_half + block * 2 + quarter // 2
            cs_send[k, 0:ROWS, :] = part[:, quarter * Q:(quarter + 1) * Q].astype(bf16)
            cs_send[k, ROWS:PIECE, :] = sums
        cs_copy(block).start()

    def ga_copy(o):
        return remote(
            ga_send.at[o], ga_recv.at[a], ga_ss.at[o], ga_rs.at[a], z_dev((z + T * o) % Z)
        )

    def near_sum(o):
        k = (a + o) % na

        @pl.when(c == t)
        def _():
            gx_recv[k * T] = gx_send[k * T + t]

        for m in range(T):
            wait = remote(
                gx_send.at[0], gx_recv.at[k * T + m], gx_ss.at[0], gx_rs.at[k * T + m], sibling
            ).wait_recv
            if m == 0:
                pl.when(c != t)(wait)
            else:
                wait()
        total = sum(gx_recv[k * T + m, 0:ROWS, :].astype(f32) for m in range(T))
        ga_send[o, 0:ROWS, :] = total.astype(bf16)
        ga_send[o, ROWS:PIECE, :] = pack(
            sum(unpack(gx_recv[k * T + m, ROWS:PIECE, :]) for m in range(T))
        )

    @pl.loop(0, n_blocks)
    def _(n):
        both_cores((b + 1 + n) % n_blocks)

    for o in near_groups:
        near_sum(o)
        ga_copy(o).start()

    for o in far_groups:
        near_sum(o)
        ga_copy(o).start()
    near_sum(0)

    def raw_grad(total, sums, emb, target, inv_row):
        off, diag, inner, match = (sums[k:k + 1] for k in range(4))
        factor = coef / (off + diag) * inv_row
        align = inner - off * match
        return (
            as_columns(factor) * (total - as_columns(off) * target - as_columns(align) * emb)
        ).astype(bf16)

    def gr_copy(m, i):
        return remote(
            gr_own.at[m], gr_all.at[m, :, pl.ds(pl.multiple_of(t * Q, Q), Q)],
            gr_ss.at[m * T + i], gr_rs.at[m * T + t], t_dev((t + i) % T),
        )

    own_gr = [
        pltpu.make_async_copy(
            gr_own.at[m], gr_all.at[m, :, pl.ds(pl.multiple_of(t * Q, Q), Q)], gr_ss.at[m * T]
        )
        for m in range(2)
    ]

    diy, dty = di // ny, dt // ny
    per_i, per_t = diy // (Z * XL), dty // (Z * XL)
    win = window_of(per_i)
    pair = 2 if per_t % 16 else 1

    def img_rows(block, other):
        return (block // XL) * diy + ((other * XL + block % XL) * per_i) // 8 * 8

    def txt_rows(block, other):
        return (block // XL) * dty + (other * XL + block % XL) * per_t

    def yi_copy(i):
        dst = (b + i) % n_blocks
        return remote(
            yi_send.at[dst], yi_recv.at[b], yi_ss.at[i], yi_rs.at[b], plane_dev(dst * T + t)
        )

    def yt_copy(i):
        dst = (b + i) % n_blocks
        return remote(
            yt_send.at[dst], yt_recv.at[b], yt_ss.at[i], yt_rs.at[b], plane_dev(dst * T + t)
        )

    def terms(feat, grad, term):
        for k in range(0, feat.shape[1], 128):
            term[k:k + 128, :] = tn(feat[:, k:k + 128], grad)

    def img_begin(grad):
        gr_own[0] = grad
        terms(imgf, grad, term_i)
        for block in range(n_blocks):
            for other in range(Z):
                first = img_rows(block, other)
                yi_send[block, other] = term_i[first:first + win, :].astype(bf16)
        for i in range(1, n_blocks):
            yi_copy(i).start()

    def txt_begin(grad):
        gr_own[1] = grad
        terms(txtf, grad, term_t)
        for block in range(n_blocks):
            for group in range(Z // pair):
                rows = [
                    term_t[txt_rows(block, group * pair + n):txt_rows(block, group * pair + n) + per_t, :]
                    for n in range(pair)
                ]
                yt_send[block, group] = jnp.concatenate(rows, axis=0).astype(bf16)
        for i in range(1, n_blocks):
            yt_copy(i).start()

    def plane_sum(send, recv, ss, rs):
        total = send[b].astype(f32)
        for i in range(1, n_blocks):
            src = (b + i) % n_blocks
            remote(send.at[0], recv.at[src], ss.at[i], rs.at[src], sibling).wait_recv()
            total += recv[src].astype(f32)
        return total

    def rs_sum(i, carry):
        total, sums = carry
        src = (h + i) % n_half
        remote(
            rs_mid.at[0], rs_recv.at[src], ri_ss.at[0], ri_rs.at[src], sibling
        ).wait_recv()
        return (
            total + rs_recv[src, 0:ROWS, :].astype(f32),
            sums + unpack(rs_recv[src, ROWS:PIECE, :]),
        )

    total_img, sums_img = lax.fori_loop(
        1, n_half, rs_sum, (rs_mid[h, 0:ROWS, :].astype(f32), unpack(rs_mid[h, ROWS:PIECE, :]))
    )
    own_img = own[0].astype(f32)
    own_txt = own[1].astype(f32)
    img_begin(raw_grad(total_img, sums_img, own_img, own_txt, invr[0:1, :]))

    total_txt = ga_send[0, 0:ROWS, :].astype(f32)
    sums_txt = unpack(ga_send[0, ROWS:PIECE, :])
    for o in near_first:
        src = (a + o) % na
        remote(ga_send.at[0], ga_recv.at[src], ga_ss.at[o], ga_rs.at[src], sibling).wait_recv()
        total_txt += ga_recv[src, 0:ROWS, :].astype(f32)
        sums_txt += unpack(ga_recv[src, ROWS:PIECE, :])
    txt_begin(raw_grad(total_txt, sums_txt, own_txt, own_img, invr[1:2, :]))

    def zi_copy(i):
        dst = (z + i) % Z
        return remote(zi_send.at[dst], zi_recv.at[z], zi_ss.at[i], zi_rs.at[z], z_dev(dst))

    def zt_copy(i):
        dst = (z + i) % Z
        return remote(zt_send.at[dst], zt_recv.at[z], zt_ss.at[i], zt_rs.at[z], z_dev(dst))

    zi_send[...] = plane_sum(yi_send, yi_recv, yi_ss, yi_rs).astype(bf16)

    @pl.loop(0, Z)
    def _(n):
        i = (Z // 2 + n) % Z

        @pl.when(i > 0)
        def _():
            zi_copy(i).start()

    for m in range(2):
        own_gr[m].start()
        for i in range(1, T):
            gr_copy(m, i).start()

    total = plane_sum(yt_send, yt_recv, yt_ss, yt_rs)
    for other in range(Z):
        first = other % pair * per_t
        rows = total[other // pair, first:first + per_t, :]
        zt_send[other] = jnp.concatenate([rows] * pair, axis=0).astype(bf16)

    @pl.loop(0, Z)
    def _(n):
        i = (Z // 2 + n) % Z

        @pl.when(i > 0)
        def _():
            zt_copy(i).start()

    for m in range(2):
        own_gr[m].wait()
        own_pp[m].wait()
        for i in range(1, T):
            src = (t + i) % T
            remote(
                gr_own.at[m], gr_all.at[m, :, pl.ds(pl.multiple_of(src * Q, Q), Q)],
                gr_ss.at[m * T + i], gr_rs.at[m * T + src], t_dev(src),
            ).wait_recv()
    for i in range(1, T):
        for copy in pp_pair(i, (t + i) % T, 0):
            copy.wait_recv()
    back_i[...] = nt(gr_all[0], psi[...])
    back_t[...] = nt(gr_all[1], pst[...])
    feature_out = [
        pltpu.make_async_copy(src, dst, in_ss.at[k])
        for k, (src, dst) in enumerate([(back_i, gif), (back_t, gtf)])
    ]
    for copy in feature_out:
        copy.start()

    for i in range(1, T):
        sq_copy(i).wait_send()
        for copy in pp_copies(i):
            copy.wait_send()
        for m in range(2):
            gr_copy(m, i).wait_send()
    for o in far_first:
        za_copy(o).wait_send()
        ga_copy(o).wait_send()
    fw_own.wait_send()

    @pl.loop(1, n_half)
    def _(i):
        ig_copy(i).wait_send()
        fw_copy(i).wait_send()
        rs_copy((h + i) % n_half).wait_send()

    @pl.loop(0, n_blocks)
    def _(block):
        cs_copy(block).wait_send()

    @pl.loop(0, na)
    def _(k):
        for m in range(1, T):
            tx_copy(k, m).wait_send()

        @pl.when(c != t)
        def _():
            tx_copy(k, 0).wait_send()

        for quarter in range(T):
            @pl.when((mine != 0) | (t != quarter))
            def _(quarter=quarter):
                gx_copy(k, quarter).wait_send()

    for i in range(1, n_blocks):
        yi_copy(i).wait_send()
        yt_copy(i).wait_send()

    def zi_add(i, total):
        src = (z + i) % Z
        remote(zi_send.at[0], zi_recv.at[src], zi_ss.at[i], zi_rs.at[src], sibling).wait_recv()
        return total + zi_recv[src].astype(f32)

    total = lax.fori_loop(1, Z, zi_add, zi_send[z].astype(f32))
    shift = ((z * XL + xl) * per_i) % 8
    result = total[0:per_i]
    for k in sorted({(k * per_i) % 8 for k in range(8)} - {0}):
        result = jnp.where(shift == k, total[k:k + per_i], result)
    gip[...] = result

    def zt_add(i, total):
        src = (z + i) % Z
        remote(zt_send.at[0], zt_recv.at[src], zt_ss.at[i], zt_rs.at[src], sibling).wait_recv()
        return total + zt_recv[src, 0:per_t, :].astype(f32)

    gtp[...] = lax.fori_loop(1, Z, zt_add, zt_send[z, 0:per_t, :].astype(f32))

    @pl.loop(1, Z)
    def _(i):
        zi_copy(i).wait_send()
        zt_copy(i).wait_send()
    for copy in feature_out:
        copy.wait()


def shards(ny, img_feat, txt_feat, img_proj, txt_proj, logit_scale):
    di, dt = img_feat.shape[1], txt_feat.shape[1]
    n_blocks = ny * XL
    n_plane = n_blocks * T
    n_half = n_plane // 2
    na = Z // T
    keys = na * ROWS
    emb = T * Q
    ndp = ny * Z * XL
    diy, dty = di // ny, dt // ny
    win = window_of(diy // (Z * XL))
    per_t = dty // (Z * XL)
    pair = 2 if per_t % 16 else 1
    tall = per_t * pair
    dma = pltpu.SemaphoreType.DMA
    vmem = pltpu.VMEM
    piece = (PIECE, Q)
    scratch = [
        vmem((ROWS, di), bf16),
        vmem((ROWS, dt), bf16),
        vmem((di, Q), bf16),
        vmem((dt, Q), bf16),
        vmem((T, 8, ROWS), f32),
        vmem((8, ROWS), f32),
        vmem((2, ROWS, Q), bf16),
        vmem((n_blocks * ROWS, emb), bf16),
        vmem((na, ROWS, Q), bf16),
        vmem((keys, emb), bf16),
        vmem((di // T, emb), bf16),
        vmem((dt // T, emb), bf16),
        vmem((ROWS, emb), f32),
        vmem((na, 8, ROWS), f32),
        vmem((n_blocks * ROWS, keys), bf16),
        vmem((n_plane, *piece), bf16),
        vmem((n_half, *piece), bf16),
        vmem((n_half, *piece), bf16),
        vmem((n_half, *piece), bf16),
        vmem((na * T, *piece), bf16),
        vmem((na * T, *piece), bf16),
        vmem((na, *piece), bf16),
        vmem((na, *piece), bf16),
        vmem((2, ROWS, Q), bf16),
        vmem((2, ROWS, emb), bf16),
        vmem((n_blocks, Z, win, Q), bf16),
        vmem((n_blocks, Z, win, Q), bf16),
        vmem((n_blocks, Z // pair, pair * per_t, Q), bf16),
        vmem((n_blocks, Z // pair, pair * per_t, Q), bf16),
        vmem((di, Q), f32),
        vmem((dt, Q), f32),
        vmem((ROWS, di // T), f32),
        vmem((ROWS, dt // T), f32),
        vmem((Z, win, Q), bf16),
        vmem((Z, win, Q), bf16),
        vmem((Z, tall, Q), bf16),
        vmem((Z, tall, Q), bf16),
    ]
    wide = max(n_blocks, 2)
    sems = [
        4, T, T, 2 * T, 2 * T, n_half, n_half, n_plane, na, na,
        na * T, na * T, n_blocks, n_blocks, n_half, n_half, na * T, na * T, na, na,
        2 * T, 2 * T, wide, wide, wide, wide, Z, Z, Z, Z,
    ]
    scratch += [dma((n,)) for n in sems]
    whole = pl.BlockSpec(memory_space=pltpu.VMEM)
    return pl.pallas_call(
        functools.partial(kernel, ny, di, dt),
        out_shape=(
            jax.ShapeDtypeStruct((di // ndp, Q), f32),
            jax.ShapeDtypeStruct((dt // ndp, Q), f32),
            jax.ShapeDtypeStruct((ROWS, di // T), f32),
            jax.ShapeDtypeStruct((ROWS, dt // T), f32),
        ),
        in_specs=[pl.BlockSpec(memory_space=pltpu.SMEM)]
        + [pl.BlockSpec(memory_space=pl.ANY)] * 4,
        out_specs=(whole, whole) + (pl.BlockSpec(memory_space=pl.ANY),) * 2,
        scratch_shapes=scratch,
        compiler_params=pltpu.CompilerParams(
            collective_id=0, has_side_effects=True, vmem_limit_bytes=56 * 1024 * 1024
        ),
    )(logit_scale, img_feat, txt_feat, img_proj, txt_proj)


def solution(mesh):
    ny = mesh.shape["dp"] // (Z * XL)
    return jax.shard_map(
        functools.partial(shards, ny),
        mesh=mesh,
        in_specs=(P("dp", None), P("dp", None), P(None, "tensor"), P(None, "tensor"), P()),
        out_specs=(P("dp", "tensor"), P("dp", "tensor"), P("dp", "tensor"), P("dp", "tensor")),
        check_vma=False,
    )
```
